512 devices in a mesh: grp: 32 (over y, x), slab: 16 (over z, core).
Axes of the slice: x: 4, y: 8, z: 8, core: 2. Of those that a mesh axis runs over, the one named last changes fastest.
Arguments:
- hall_now: float32 [32, 256, 128, 128], P('grp', None, 'slab'), may hold values from -6 to 6
- hall_prev: float32 [32, 256, 128, 128], P('grp', None, 'slab'), may hold values from -6 to 6
- room_now: float32 [32, 16, 32, 32, 128], P('grp', 'slab'), may hold values from -6 to 6
- room_prev: float32 [32, 16, 32, 32, 128], P('grp', 'slab'), may hold values from -6 to 6
- room_length: int32 [32, 16, 32], P('grp', 'slab'), may hold values from 16 to 32
- right_neighbor: int32 [16, 1024], P('slab'), may hold values from 0 to 1023, as said below
Outputs:
- hall_pressure: float32 [32, 256, 128, 128], P('grp', 'slab')
- room_pressure: float32 [32, 16, 32, 32, 128], P('grp', 'slab')
The draws below stay inside these ranges and needn't reach their ends.
Inputs may be any that keep to these rules, and one draw needn't show every extreme that they name: For each index of slab, right_neighbor is a permutation of the 1024 room partitions, numbered grp index times 32 plus slot. Slot p of grp index g has its right neighbour at grp index (g + s) mod 32, where s depends only on the index of slab and on p. At most 2 of one device's partitions have their right neighbour on any one device, and exactly 2 do for some device.
All inputs are finite; a program needn't handle non-finite values.
Results may differ from the reference program's by a relative error of at most 0.0003.
Values sent between devices are 32-bit elements; how exact they have to be, the bound alone decides.
A program may use at most 64 MiB of HBM per device.

```python
import jax
import jax.numpy as jnp
from jax import lax

LX = 256
LY = 128
LZ = 128
SX = 32
SY = 8
SZ = 16
P_SIZE = 32
STEPS = 4
N_GRP = 32
N_SLAB = 16


def neighbor_column(key):
    key_pairs, key_order, key_places, key_landing = jax.random.split(key, 4)
    capacity = 2 * P_SIZE // N_GRP
    pair_count = N_GRP // 2
    first_counts = jax.random.randint(key_pairs, (pair_count,), 0, capacity + 1)
    first_counts = first_counts.at[0].set(capacity)
    counts = jnp.stack([first_counts, capacity - first_counts], axis=1).reshape(N_GRP).astype(jnp.int32)
    peer_order = jax.random.permutation(key_order, N_GRP)
    shift_counts = jnp.zeros((N_GRP,), jnp.int32).at[peer_order].set(counts)
    shift_list = jnp.repeat(jnp.arange(N_GRP, dtype=jnp.int32), shift_counts, total_repeat_length=P_SIZE)
    places = jax.random.permutation(key_places, P_SIZE)
    slot_shift = jnp.zeros((P_SIZE,), jnp.int32).at[places].set(shift_list)
    landing = jax.random.permutation(key_landing, P_SIZE).astype(jnp.int32)
    home_group = jnp.arange(N_GRP, dtype=jnp.int32)[:, None]
    target = (home_group + slot_shift[None, :]) % N_GRP * P_SIZE + landing[None, :]
    return target.reshape(N_GRP * P_SIZE)


def draw_right_neighbor(key, part):
    key = jax.random.fold_in(key, 7)
    column_keys = jax.random.split(key, N_SLAB)
    return jax.vmap(neighbor_column)(column_keys).astype(jnp.int32)


def place_ends(values, key, smallest, largest):
    shape = values.shape
    index_at = [jax.random.randint(jax.random.fold_in(key, axis), (), 0, shape[axis]) for axis in range(len(shape))]
    values = values.at[tuple(index_at)].set(smallest)
    longest = shape.index(max(shape))
    index_at[longest] = (index_at[longest] + 1) % shape[longest]
    return values.at[tuple(index_at)].set(largest)


def shard_levels(key, dims, pieces, least, high):
    gain, own = 1.0, jax.random.fold_in(key, 6)
    for axis_at, blocks in pieces:
        draws = jnp.exp(jax.random.uniform(jax.random.fold_in(own, axis_at), (blocks,), jnp.float32, least / len(pieces), high / len(pieces)))
        gain = gain * jnp.repeat(draws, dims[axis_at] // blocks).reshape([-1 if axis == axis_at else 1 for axis in range(len(dims))])
    return gain


def bell_draw(stream_key, shape, scale, most, cuts=(), kind=jnp.bfloat16):
    level = shard_levels(stream_key, shape, cuts, -0.22, 0.18) if cuts else 1.0
    result = jax.random.normal(stream_key, shape, jnp.float32) * scale * level
    return jnp.minimum(jnp.maximum(result, -most), most).astype(kind)


def setup_inputs(seed: int = 0) -> dict:
    seeds = jax.random.split(jax.random.key(seed), 7)
    return {
        "hall_now": bell_draw(seeds[0], (N_GRP, LX, LY, LZ), 1.0, 6.0, ((0, 32), (2, 16)), jnp.float32),
        "hall_prev": bell_draw(seeds[1], (N_GRP, LX, LY, LZ), 1.0, 6.0, ((0, 32), (2, 16)), jnp.float32),
        "room_now": bell_draw(seeds[2], (N_GRP, N_SLAB, P_SIZE, SX, SY * SZ), 1.0, 6.0, ((0, 32), (1, 16)), jnp.float32),
        "room_prev": bell_draw(seeds[3], (N_GRP, N_SLAB, P_SIZE, SX, SY * SZ), 1.0, 6.0, ((0, 32), (1, 16)), jnp.float32),
        "room_length": place_ends(jax.random.randint(seeds[4], (N_GRP, N_SLAB, P_SIZE), SX // 2, SX + 1), jax.random.fold_in(seeds[4], 1), SX // 2, SX).astype(jnp.int32),
        "right_neighbor": draw_right_neighbor(jax.random.fold_in(seeds[6], 71), 0),
    }


TIME_STEP = 0.4
PRECISE = lax.Precision.HIGHEST
STENCIL_ROWS = ((1.5, -0.15, 1.0 / 90.0), (-0.15, 1.0 / 90.0, 0.0), (1.0 / 90.0, 0.0, 0.0))

def cosine_table(length):
    modes = jnp.arange(length, dtype=jnp.float32)[:, None]
    cells = jnp.arange(length, dtype=jnp.float32)[None, :]
    weight = jnp.where(modes == 0, jnp.sqrt(1.0 / length), jnp.sqrt(2.0 / length))
    return weight * jnp.cos(jnp.pi * modes * (2.0 * cells + 1.0) / (2.0 * length))

def ragged_table(lengths, width):
    extent = lengths.astype(jnp.float32)[:, None, None]
    modes = jnp.arange(width, dtype=jnp.float32)[None, :, None]
    cells = jnp.arange(width, dtype=jnp.float32)[None, None, :]
    weight = jnp.where(modes == 0, jnp.sqrt(1.0 / extent), jnp.sqrt(2.0 / extent))
    values = weight * jnp.cos(jnp.pi * modes * (2.0 * cells + 1.0) / (2.0 * extent))
    return jnp.where((modes < extent) & (cells < extent), values, 0.0)

def step_factors(omega):
    sinc_value = jnp.sinc(omega * (TIME_STEP / (2.0 * jnp.pi)))
    return (jnp.cos(omega * TIME_STEP), TIME_STEP * TIME_STEP * sinc_value * sinc_value)

def stencil():
    return jnp.array(STENCIL_ROWS, dtype=jnp.float32)

def hall_forcing(lower, upper, lower_next, upper_prev, has_prev, has_next):
    weights = stencil()
    below = lower - upper_prev[..., ::-1]
    above = lower_next - upper[..., ::-1]
    force_low = -jnp.einsum('...k,jk->...j', below, weights, precision=PRECISE) * has_prev
    force_high = jnp.einsum('...k,jk->...j', above, weights, precision=PRECISE)[..., ::-1] * has_next
    return jnp.concatenate([force_low, force_high], axis=-1)

def room_space(modes, table, cos_cross):
    along = jnp.einsum('rki,rkc->ric', table, modes, precision=PRECISE)
    return jnp.einsum('rik,kc->ric', along, cos_cross, precision=PRECISE)

def room_modes(force, table, cos_cross):
    along = jnp.einsum('rki,ric->rkc', table, force, precision=PRECISE)
    return jnp.einsum('rkc,mc->rkm', along, cos_cross, precision=PRECISE)

def room_column(current, previous, lengths, neighbor, cos_cross):
    count = lengths.shape[0]
    width = current.shape[1]
    table = ragged_table(lengths, width)
    cells = jnp.arange(width)
    live = (cells[None, :] < lengths[:, None]).astype(jnp.float32)[:, :, None]
    current = current * live
    previous = previous * live
    cross_ids = jnp.arange(SY * SZ)
    wave_x = cells.astype(jnp.float32)[None, :, None] / lengths.astype(jnp.float32)[:, None, None]
    wave_y = ((cross_ids // SZ).astype(jnp.float32) / SY)[None, None, :]
    wave_z = ((cross_ids % SZ).astype(jnp.float32) / SZ)[None, None, :]
    omega = jnp.pi * jnp.sqrt(wave_x * wave_x + wave_y * wave_y + wave_z * wave_z)
    room_cos, room_gain = step_factors(omega)
    left = jnp.zeros_like(neighbor).at[neighbor].set(jnp.arange(count, dtype=jnp.int32))
    layers = jnp.arange(3)
    upper_pick = (cells[None, :, None] == lengths[:, None, None] - 1 - layers[None, None, :]).astype(jnp.float32)
    lower_pick = (cells[:, None] == layers[None, :]).astype(jnp.float32)
    weights = stencil()
    for step_index in range(STEPS):
        space = room_space(current, table, cos_cross)
        upper = jnp.einsum('rxj,rxc->rjc', upper_pick, space, precision=PRECISE)
        lower = space[:, :3]
        force_high = jnp.einsum('jk,rkc->rjc', weights, lower[neighbor] - upper, precision=PRECISE)
        force_low = -jnp.einsum('jk,rkc->rjc', weights, lower - upper[left], precision=PRECISE)
        force = jnp.einsum('xj,rjc->rxc', lower_pick, force_low, precision=PRECISE)
        force = force + jnp.einsum('rxj,rjc->rxc', upper_pick, force_high, precision=PRECISE)
        modal = room_modes(force, table, cos_cross)
        fresh = 2.0 * room_cos * current - previous + room_gain * modal
        previous, current = (current, fresh)
    return room_space(current, table, cos_cross)

def reference(hall_now, hall_prev, room_now, room_prev, room_length, right_neighbor):
    cos_x = cosine_table(LX)
    cos_y = cosine_table(LY)
    cos_z = cosine_table(LZ)
    cos_face = jnp.concatenate([cos_z[:, :3], cos_z[:, LZ - 3:]], axis=1)
    wave_x = jnp.arange(LX, dtype=jnp.float32)[:, None, None] / LX
    wave_y = jnp.arange(LY, dtype=jnp.float32)[None, :, None] / LY
    wave_z = jnp.arange(LZ, dtype=jnp.float32)[None, None, :] / LZ
    omega = jnp.pi * jnp.sqrt(wave_x * wave_x + wave_y * wave_y + wave_z * wave_z)
    hall_cos, hall_gain = step_factors(omega)
    group_ids = jnp.arange(N_GRP)
    has_prev = (group_ids > 0).astype(jnp.float32)[:, None, None, None]
    has_next = (group_ids < N_GRP - 1).astype(jnp.float32)[:, None, None, None]
    modes_now, modes_prev = (hall_now, hall_prev)
    for step_index in range(STEPS):
        spread = jnp.einsum('gabc,cf->gabf', modes_now, cos_face, precision=PRECISE)
        spread = jnp.einsum('by,gabf->gayf', cos_y, spread, precision=PRECISE)
        faces = jnp.einsum('ax,gayf->gxyf', cos_x, spread, precision=PRECISE)
        lower = faces[..., :3]
        upper = faces[..., 3:]
        blank = jnp.zeros_like(lower[:1])
        lower_next = jnp.concatenate([lower[1:], blank], axis=0)
        upper_prev = jnp.concatenate([blank, upper[:-1]], axis=0)
        force = hall_forcing(lower, upper, lower_next, upper_prev, has_prev, has_next)
        spread = jnp.einsum('ax,gxyf->gayf', cos_x, force, precision=PRECISE)
        spread = jnp.einsum('by,gayf->gabf', cos_y, spread, precision=PRECISE)

        def advance(items):
            current, previous, forced = items
            modal = jnp.einsum('abf,cf->abc', forced, cos_face, precision=PRECISE)
            return 2.0 * hall_cos * current - previous + hall_gain * modal
        fresh = lax.map(advance, (modes_now, modes_prev, spread))
        modes_prev, modes_now = (modes_now, fresh)

    def hall_space(modes):
        inner = jnp.einsum('abc,cz->abz', modes, cos_z, precision=PRECISE)
        inner = jnp.einsum('by,abz->ayz', cos_y, inner, precision=PRECISE)
        return jnp.einsum('ax,ayz->xyz', cos_x, inner, precision=PRECISE)
    hall_pressure = lax.map(hall_space, modes_now)
    room_count = N_GRP * P_SIZE
    cross = SY * SZ
    cos_cross = jnp.kron(cosine_table(SY), cosine_table(SZ))
    now_cols = jnp.moveaxis(room_now, 1, 0).reshape(N_SLAB, room_count, SX, cross)
    prev_cols = jnp.moveaxis(room_prev, 1, 0).reshape(N_SLAB, room_count, SX, cross)
    length_cols = jnp.moveaxis(room_length, 1, 0).reshape(N_SLAB, room_count)

    def one_column(items):
        current, previous, lengths, neighbor = items
        return room_column(current, previous, lengths, neighbor, cos_cross)
    room_out = lax.map(one_column, (now_cols, prev_cols, length_cols, right_neighbor))
    room_pressure = jnp.moveaxis(room_out.reshape(N_SLAB, N_GRP, P_SIZE, SX, cross), 0, 1)
    return (hall_pressure, room_pressure)
```

```python
import functools
import math

import jax
import jax.numpy as jnp
import ml_dtypes
import numpy as np
from jax import lax
from jax.experimental import pallas as pl
from jax.experimental.pallas import tpu as pltpu
from jax.sharding import PartitionSpec as P

SY = 8
SZ = 16
STEPS = 4
SHORTEST = 16
TIME_STEP = 0.4
SCALE = (TIME_STEP * math.pi) ** 2
STENCIL = np.array([[270, -27, 2], [-27, 2, 0], [2, 0, 0]], np.float64) / 180.0
F32 = jnp.float32
BF16 = jnp.bfloat16
MESH = pl.DeviceIdType.MESH


def dct(length):
    k = np.arange(length)[:, None]
    i = np.arange(length)[None, :]
    w = np.where(k == 0, np.sqrt(1.0 / length), np.sqrt(2.0 / length))
    return w * np.cos(np.pi * k * (2 * i + 1) / (2 * length))


def halves(x):
    high = x.astype(np.float32).astype(ml_dtypes.bfloat16)
    low = (x - high.astype(np.float64)).astype(ml_dtypes.bfloat16)
    return high, low


def left_table(x):
    high, low = halves(x)
    return np.concatenate([high, high, low], axis=1)


def right_table(x):
    high, low = halves(x)
    return np.concatenate([high, high, low], axis=0)


def face_rows(table):
    length = table.shape[0]
    sign = np.where(np.arange(length) % 2 == 0, 1.0, -1.0)
    low = table[:, :3].T
    forced = STENCIL.T @ low
    zero = np.zeros((2, length))
    return (
        np.concatenate([low, low * sign, zero], axis=0),
        np.concatenate([forced, forced * sign, zero], axis=0),
    )


def hall_tables(nx, ny, nz):
    faces, forced = face_rows(dct(nz))
    high, low = halves(faces)
    spread = np.concatenate(
        [np.concatenate([high, high], axis=1), np.concatenate([low, 0 * low], axis=1)], axis=0
    )
    pairs = np.concatenate([forced[k : k + 1] * faces for k in range(6)], axis=0)
    high, low = halves(pairs)
    respond = np.concatenate(
        [np.concatenate([high, high], axis=1), np.concatenate([low, 0 * low], axis=1)], axis=0
    )
    high, low = halves(forced)
    outer = np.concatenate([high, high, low, low], axis=0)
    return spread, respond, outer, left_table(dct(nx).T), left_table(dct(ny).T), right_table(dct(nz))


def room_tables(width):
    faces, forced, full = [], [], []
    for length in range(SHORTEST, width + 1):
        table = np.zeros((width, width))
        table[:length, :length] = dct(length)
        low, high = face_rows(table[:, :])
        faces.append(np.tile(low, (1, 4)))
        forced.append(np.tile(high, (1, 4)))
        full.append(np.tile(table.T, (1, 4)))
    return [np.stack(t).astype(np.float32) for t in (faces, forced, full)]


def factors(q):
    h = jnp.full_like(q, 2.0 / math.factorial(18))
    for n in range(7, -1, -1):
        h = 2.0 / math.factorial(2 * n + 2) - h * q
    return 2.0 - q * h, (TIME_STEP * TIME_STEP) * h


def mm(a, b):
    return jnp.dot(a, b, preferred_element_type=F32)


def mm_nt(a, b):
    return lax.dot_general(a, b, (((1,), (1,)), ((), ())), preferred_element_type=F32)


def split(x):
    high = x.astype(BF16)
    return high, (x - high.astype(F32)).astype(BF16)


def stacked(x, axis):
    high, low = split(x)
    return jnp.concatenate([high, low, high], axis=axis)


def iota(shape, dim):
    return lax.broadcasted_iota(jnp.int32, shape, dim).astype(F32)


def total(mask, values, axis):
    return jnp.sum(jnp.where(mask, values, 0.0), axis=axis, keepdims=True)


def kernel(
    groups, slabs, count,
    hall_now, hall_prev, room_now, room_prev, lengths, ids, shifts,
    spread_t, respond_t, outer_t, cosx_t, cosy_t, cosz_t, face_t, force_t, room_t, cross_t,
    hall_out, room_out,
    hall_c2, hall_gain, hall_base, hall_faces, hall_resp, hall_diff, hall_other,
    hall_send, hall_recv, a2a_send, a2a_recv,
    room_c2, room_gain, room_a, room_b, room_faces, raw_faces, raw_force, raw_full,
    face_l, force_l, full_l, pack_l, take_l, room_send, room_recv,
    hall_ssem, hall_rsem, a2a_ssem, a2a_rsem, room_ssem, room_rsem,
):
    me = lax.axis_index("grp")
    column = lax.axis_index("slab")
    nx, part_y, nz = hall_now.shape
    ny = part_y * slabs
    part_x = nx // slabs
    lanes = nx * part_y
    width = room_now.shape[0] // count
    batches = count // 4

    barrier = pltpu.get_barrier_semaphore()

    def greet_grp(step, carry):
        pl.semaphore_signal(
            barrier, inc=1, device_id=(lax.rem(me + step, groups), column), device_id_type=MESH
        )
        return carry

    def greet_slab(step, carry):
        pl.semaphore_signal(
            barrier, inc=1, device_id=(me, lax.rem(column + step, slabs)), device_id_type=MESH
        )
        return carry

    lax.fori_loop(1, groups, greet_grp, 0)
    lax.fori_loop(1, slabs, greet_slab, 0)

    chunk = 256
    deep = chunk // part_y

    def spread_of(x):
        high, low = split(x)
        both = mm_nt(spread_t[...], jnp.concatenate([high, low], axis=1))
        return both[:8] + both[8:]

    def first_faces(i, carry):
        x = hall_now[pl.ds(i * deep, deep)].reshape(chunk, nz)
        hall_faces[0, :, pl.ds(pl.multiple_of(i * chunk, chunk), chunk)] = spread_of(x)
        return carry

    lax.fori_loop(0, lanes // chunk, first_faces, 0)

    def hall_copy(t, side):
        peer = lax.rem(me + (1 if side == 0 else groups - 1), groups)
        return pltpu.make_async_remote_copy(
            src_ref=hall_send.at[t, side],
            dst_ref=hall_recv.at[t, side],
            send_sem=hall_ssem.at[t, side],
            recv_sem=hall_rsem.at[t, side],
            device_id=(peer, column),
            device_id_type=MESH,
        )

    def hall_put(t):
        own = hall_faces[t]
        for k in range(3):
            for j in range(lanes // 128):
                cut = slice(128 * j, 128 * j + 128)
                hall_send[t, 0, k, j : j + 1, :] = own[3 + k : 4 + k, cut]
                hall_send[t, 1, k, j : j + 1, :] = own[k : k + 1, cut]
        hall_copy(t, 0).start()
        hall_copy(t, 1).start()

    def hall_get(t):
        hall_copy(t, 0).wait_recv()
        hall_copy(t, 1).wait_recv()
        for k in range(3):
            for j in range(lanes // 128):
                cut = slice(128 * j, 128 * j + 128)
                hall_other[k : k + 1, cut] = hall_recv[t, 0, k, j : j + 1, :]
                hall_other[3 + k : 4 + k, cut] = hall_recv[t, 1, k, j : j + 1, :]
        row = lax.broadcasted_iota(jnp.int32, (8, lanes), 0)
        first = jnp.where(me > 0, 0, 3)
        last = jnp.where(me < groups - 1, 6, 3)
        diff = jnp.where((row >= first) & (row < last), hall_other[...] - hall_faces[t], 0.0)
        hall_diff[t] = diff
        return diff

    def hall_respond(t, lag, diff):
        acc = hall_faces[t + lag]
        for k in range(6):
            acc = acc + hall_resp[lag - 1, 8 * k : 8 * k + 8, :] * diff[k : k + 1, :]
        hall_faces[t + lag] = acc

    def hall_accumulate(t):
        def body(i, carry):
            at = pl.ds(i * deep, deep)
            e = hall_diff[t, :, pl.ds(pl.multiple_of(i * chunk, chunk), chunk)]
            high = e.astype(BF16).astype(F32)
            low = e - high
            e = jnp.concatenate([high, low, high, low], axis=0).T.astype(BF16)
            forced = mm(e, outer_t[...]).reshape(deep, part_y, nz)
            c2 = hall_c2[at]
            weight = hall_gain[at]
            if t == 2:
                weight = weight * c2
            elif t == 1:
                weight = weight * (c2 * c2 - 1.0)
            elif t == 0:
                weight = weight * (c2 * (c2 * c2 - 2.0))
            hall_base[at] = hall_base[at] + weight * forced
            return carry

        lax.fori_loop(0, lanes // chunk, body, 0)

    hall_other[...] = jnp.zeros_like(hall_other)
    pl.semaphore_wait(barrier, groups + slabs - 2)
    hall_put(0)

    lane = lax.broadcasted_iota(jnp.int32, (width, 128), 1)
    kx = lax.broadcasted_iota(jnp.int32, (width, 128), 0)
    q_cross = (lane // SZ).astype(F32) / SY
    q_cross = SCALE * (q_cross * q_cross)
    z_part = (lane % SZ).astype(F32) / SZ
    q_cross = q_cross + SCALE * (z_part * z_part)
    kx_f = kx.astype(F32)
    kx_sq = SCALE * (kx_f * kx_f)

    def room_setup(b, carry):
        for i in range(4):
            r = 4 * b + i
            length = lengths[r]
            which = jnp.maximum(length - SHORTEST, 0)
            at = pl.ds(pl.multiple_of(r * width, width), width)
            at8 = pl.ds(pl.multiple_of(r * 8, 8), 8)
            mine = lane // width == i
            raw_faces[at8, :] = jnp.where(mine[:8], face_t[which], 0.0)
            raw_force[at8, :] = jnp.where(mine[:8], force_t[which], 0.0)
            raw_full[at, :] = jnp.where(mine, room_t[which], 0.0)
            extent = jnp.full((width, 128), length, jnp.int32)
            live = kx < extent
            extent = extent.astype(F32)
            c2, gain = factors(kx_sq / (extent * extent) + q_cross)
            room_c2[at, :] = c2
            room_gain[at, :] = gain
            room_a[at, :] = jnp.where(live, room_now[at, :], 0.0)
            room_b[at, :] = jnp.where(live, room_prev[at, :], 0.0)
        return carry

    lax.fori_loop(0, batches, room_setup, 0)

    for b in range(batches):
        cut = slice(32 * b, 32 * b + 32)
        high, low = split(raw_faces[cut, :])
        face_l[cut, :] = jnp.concatenate([high, high, low], axis=1)
        x = raw_force[cut, :]
        high = x.astype(BF16).astype(F32)
        low = x - high
        big = slice(128 * b, 128 * b + 128)
        force_l[big, :] = jnp.concatenate([high, high, low, low], axis=0).T.astype(BF16)
        high, low = split(raw_full[big, :])
        full_l[big, :] = jnp.concatenate([high, high, low], axis=1)
        room_faces[cut, :] = mm(face_l[cut, :], stacked(room_a[big, :], 0))

    bits = int(math.log2(count))
    wide = 8 * count
    s_col = (ids[:, 0:1] >> bits).astype(F32)
    s_row = shifts[...].astype(F32)
    p_col = iota((count, wide), 0)
    lane_i = lax.broadcasted_iota(jnp.int32, (count, wide), 1)
    p_row = (lane_i >> 3).astype(F32)
    f_row = (lane_i & 7).astype(F32)
    same = s_col == s_row
    rank_row = total(same & (p_col < p_row), 1.0, 0)
    rank_col = total(same & (p_row < p_col) & (f_row == 0.0), 1.0, 1)
    home = me.astype(F32) - s_col
    home = jnp.where(home < 0.0, home + groups, home)
    landing = total(iota((count, groups), 1) == home, (ids[...] & (count - 1)).astype(F32), 1)
    match = landing == p_row
    ls_row = total(match, jnp.broadcast_to(s_col, (count, wide)), 0)
    lr_row = total(match, jnp.broadcast_to(rank_col, (count, wide)), 0)

    def back(s):
        return jnp.where(s == 0.0, 0.0, groups - s)

    f = f_row[0:1]
    layer = jnp.where(f < 3.0, f, f - 3.0)
    pack_row = jnp.where(
        f < 3.0, 16.0 * back(ls_row) + 6.0 + 3.0 * lr_row + layer, 16.0 * s_row + 3.0 * rank_row + layer
    )
    take_row = jnp.where(
        f < 3.0, 16.0 * ls_row + 3.0 * lr_row + layer, 16.0 * back(s_row) + 6.0 + 3.0 * rank_row + layer
    )
    pack_row = jnp.where(f < 6.0, pack_row, -1.0)
    take_row = jnp.where(f < 6.0, take_row, -1.0)
    slots = 16 * groups
    hot = jnp.where(iota((slots, wide), 0) == pack_row, 1.0, 0.0).astype(BF16)
    pack_l[...] = jnp.concatenate([hot, hot], axis=1)
    take_col = jnp.broadcast_to(take_row, (8, wide)).T[:, 0:1]
    hot = jnp.where(iota((wide, slots), 1) == take_col, 1.0, 0.0).astype(BF16)
    take_l[...] = jnp.concatenate([hot, hot], axis=1)

    def room_copy(t, step):
        return pltpu.make_async_remote_copy(
            src_ref=room_send.at[t, step],
            dst_ref=room_recv.at[t, step - 1],
            send_sem=room_ssem.at[t, step - 1],
            recv_sem=room_rsem.at[t, step - 1],
            device_id=(lax.rem(me + step, groups), column),
            device_id_type=MESH,
        )

    def room_put(t):
        high, low = split(room_faces[...])
        packed = mm(pack_l[...], jnp.concatenate([high, low], axis=0))
        room_send[t] = packed.reshape(groups, 16, 128)[:, :12, :]

        def body(step, carry):
            room_copy(t, step).start()
            return carry

        lax.fori_loop(1, groups, body, 0)

    def room_get(t):
        def body(step, carry):
            room_copy(t, step).wait_recv()
            return carry

        lax.fori_loop(1, groups, body, 0)
        got = jnp.concatenate([room_send[t, 0:1], room_recv[t]], axis=0)
        got = jnp.concatenate([got, jnp.zeros((groups, 4, 128), F32)], axis=1).reshape(slots, 128)
        high, low = split(got)
        other = mm(take_l[...], jnp.concatenate([high, low], axis=0))
        return other - room_faces[...]

    def room_step(t):
        diff = room_get(t)
        now, prev = (room_a, room_b) if t % 2 == 0 else (room_b, room_a)
        for b in range(batches):
            cut = slice(32 * b, 32 * b + 32)
            big = slice(128 * b, 128 * b + 128)
            high, low = split(diff[cut])
            forced = mm(force_l[big, :], jnp.concatenate([high, low, high, low], axis=0))
            fresh = room_c2[big, :] * now[big, :] - prev[big, :] + room_gain[big, :] * forced
            if t < STEPS - 1:
                prev[big, :] = fresh
                room_faces[cut, :] = mm(face_l[cut, :], stacked(fresh, 0))
            else:
                x = mm(full_l[big, :], stacked(fresh, 0))
                room_out[big, :] = mm(stacked(x, 1), cross_t[...])
        if t < STEPS - 1:
            room_put(t + 1)

    room_put(0)

    yz = lax.broadcasted_iota(jnp.int32, (part_y, nz), 0) + column * part_y
    ky_f = yz.astype(F32)
    kz_f = iota((part_y, nz), 1)
    q_yz = (SCALE / ny**2) * (ky_f * ky_f) + (SCALE / nz**2) * (kz_f * kz_f)

    def prepare(i, carry):
        at = pl.ds(i * deep, deep)
        cols = pl.ds(pl.multiple_of(i * chunk, chunk), chunk)
        a = (lax.broadcasted_iota(jnp.int32, (deep, part_y, nz), 0) + i * deep).astype(F32)
        c2, gain = factors((SCALE / nx**2) * (a * a) + q_yz[None])
        hall_c2[at] = c2
        hall_gain[at] = gain
        now = hall_now[at]
        prev = hall_prev[at]
        s_now = gain
        s_prev = jnp.zeros_like(gain)
        for t in range(1, STEPS):
            now, prev = c2 * now - prev, now
            hall_faces[t, :, cols] = spread_of(now.reshape(chunk, nz))
            high, low = split(s_now.reshape(chunk, nz))
            both = mm_nt(respond_t[...], jnp.concatenate([high, low], axis=1))
            hall_resp[t - 1, :, cols] = both[:48] + both[48:]
            s_now, s_prev = c2 * s_now - s_prev, s_now
        hall_base[at] = c2 * now - prev
        return carry

    lax.fori_loop(0, lanes // chunk, prepare, 0)

    def hall_step(t):
        diff = hall_get(t)
        if t < STEPS - 1:
            hall_respond(t, 1, diff)
            hall_put(t + 1)
            for lag in range(2, STEPS - t):
                hall_respond(t, lag, diff)
        hall_accumulate(t)

    hall_step(0)
    hall_step(1)
    room_step(0)
    hall_step(2)
    hall_step(3)

    for b in range(part_y):
        a2a_send[b] = mm(cosx_t[...], stacked(hall_base[:, b, :], 0))

    def a2a_copy(step):
        peer = lax.rem(column + step, slabs)
        return pltpu.make_async_remote_copy(
            src_ref=a2a_send.at[:, pl.ds(pl.multiple_of(peer * part_x, part_x), part_x), :],
            dst_ref=a2a_recv.at[pl.ds(column * part_y, part_y)],
            send_sem=a2a_ssem.at[step],
            recv_sem=a2a_rsem.at[step],
            device_id=(me, peer),
            device_id_type=MESH,
        )

    def a2a_start(step, carry):
        a2a_copy(step).start()
        return carry

    lax.fori_loop(1, slabs, a2a_start, 0)

    def z_part_of(x):
        x = stacked(x.reshape(part_y * part_x, nz), 1)
        return mm(x, cosz_t[...]).reshape(part_y, part_x, nz)

    own = pl.ds(pl.multiple_of(column * part_x, part_x), part_x)
    a2a_recv[pl.ds(column * part_y, part_y)] = z_part_of(a2a_send[:, own, :])

    for t in range(1, STEPS):
        room_step(t)

    def a2a_take(step, carry):
        a2a_copy(step).wait_recv()
        source = lax.rem(column + slabs - step, slabs)
        at = pl.ds(source * part_y, part_y)
        a2a_recv[at] = z_part_of(a2a_recv[at])
        return carry

    lax.fori_loop(1, slabs, a2a_take, 0)
    for x in range(0, part_x, 2):
        pair = jnp.concatenate([stacked(a2a_recv[:, x, :], 0), stacked(a2a_recv[:, x + 1, :], 0)], axis=1)
        y = mm(cosy_t[...], pair)
        hall_out[x] = y[:, :nz]
        hall_out[x + 1] = y[:, nz:]

    for t in range(STEPS):
        hall_copy(t, 0).wait_send()
        hall_copy(t, 1).wait_send()

        def sent(step, carry):
            room_copy(t, step).wait_send()
            return carry

        lax.fori_loop(1, groups, sent, 0)

    def a2a_sent(step, carry):
        a2a_copy(step).wait_send()
        return carry

    lax.fori_loop(1, slabs, a2a_sent, 0)


def local(hall_now, hall_prev, room_now, room_prev, room_length, right_neighbor):
    groups = lax.axis_size("grp")
    slabs = lax.axis_size("slab")
    _, nx, part_y, nz = hall_now.shape
    _, _, count, width, cross = room_now.shape
    ny = part_y * slabs
    part_x = nx // slabs
    lanes = nx * part_y
    slots = 16 * groups
    ids = right_neighbor[0].reshape(groups, count)
    shifts = jnp.repeat(ids[0] // count, 8)[None, :]
    tables = [jnp.asarray(t) for t in hall_tables(nx, ny, nz)]
    tables += [jnp.asarray(t) for t in room_tables(width)]
    tables += [jnp.asarray(right_table(np.kron(dct(SY), dct(SZ))))]
    vmem = pl.BlockSpec(memory_space=pltpu.VMEM)
    smem = pl.BlockSpec(memory_space=pltpu.SMEM)
    rows = count * width
    dma = pltpu.SemaphoreType.DMA
    hall_pressure, room_pressure = pl.pallas_call(
        functools.partial(kernel, groups, slabs, count),
        out_shape=(
            jax.ShapeDtypeStruct((part_x, ny, nz), F32),
            jax.ShapeDtypeStruct((rows, cross), F32),
        ),
        in_specs=[vmem] * 4 + [smem] + [vmem] * (2 + len(tables)),
        out_specs=(vmem, vmem),
        scratch_shapes=[
            pltpu.VMEM((nx, part_y, nz), F32),
            pltpu.VMEM((nx, part_y, nz), F32),
            pltpu.VMEM((nx, part_y, nz), F32),
            pltpu.VMEM((STEPS, 8, lanes), F32),
            pltpu.VMEM((STEPS - 1, 48, lanes), F32),
            pltpu.VMEM((STEPS, 8, lanes), F32),
            pltpu.VMEM((8, lanes), F32),
            pltpu.VMEM((STEPS, 2, 3, lanes // 128, 128), F32),
            pltpu.VMEM((STEPS, 2, 3, lanes // 128, 128), F32),
            pltpu.VMEM((part_y, nx, nz), F32),
            pltpu.VMEM((ny, part_x, nz), F32),
            pltpu.VMEM((rows, cross), F32),
            pltpu.VMEM((rows, cross), F32),
            pltpu.VMEM((rows, cross), F32),
            pltpu.VMEM((rows, cross), F32),
            pltpu.VMEM((8 * count, cross), F32),
            pltpu.VMEM((8 * count, 4 * width), F32),
            pltpu.VMEM((8 * count, 4 * width), F32),
            pltpu.VMEM((rows, 4 * width), F32),
            pltpu.VMEM((8 * count, 12 * width), BF16),
            pltpu.VMEM((rows, 128), BF16),
            pltpu.VMEM((rows, 12 * width), BF16),
            pltpu.VMEM((slots, 16 * count), BF16),
            pltpu.VMEM((8 * count, 2 * slots), BF16),
            pltpu.VMEM((STEPS, groups, 12, 128), F32),
            pltpu.VMEM((STEPS, groups - 1, 12, 128), F32),
            dma((STEPS, 2)),
            dma((STEPS, 2)),
            dma((slabs,)),
            dma((slabs,)),
            dma((STEPS, groups - 1)),
            dma((STEPS, groups - 1)),
        ],
        compiler_params=pltpu.CompilerParams(
            collective_id=0, has_side_effects=True, vmem_limit_bytes=48 * 1024 * 1024
        ),
    )(
        hall_now[0],
        hall_prev[0],
        room_now.reshape(rows, cross),
        room_prev.reshape(rows, cross),
        room_length.reshape(count),
        ids.T,
        shifts,
        *tables,
    )
    return (hall_pressure[None], room_pressure.reshape(1, 1, count, width, cross))


def solution(mesh):
    in_specs = (
        P("grp", None, "slab", None),
        P("grp", None, "slab", None),
        P("grp", "slab", None, None, None),
        P("grp", "slab", None, None, None),
        P("grp", "slab", None),
        P("slab", None),
    )
    out_specs = (P("grp", "slab", None, None), P("grp", "slab", None, None, None))
    return jax.shard_map(local, mesh=mesh, in_specs=in_specs, out_specs=out_specs, check_vma=False)
```

```python
import functools
import math

import jax
import jax.numpy as jnp
import ml_dtypes
import numpy as np
from jax import lax
from jax.experimental import pallas as pl
from jax.experimental.pallas import tpu as pltpu
from jax.sharding import PartitionSpec as P

SY = 8
SZ = 16
STEPS = 4
SHORTEST = 16
TIME_STEP = 0.4
SCALE = (TIME_STEP * math.pi) ** 2
STENCIL = np.array([[270, -27, 2], [-27, 2, 0], [2, 0, 0]], np.float64) / 180.0
F32 = jnp.float32
BF16 = jnp.bfloat16
MESH = pl.DeviceIdType.MESH


def dct(length):
    k = np.arange(length)[:, None]
    i = np.arange(length)[None, :]
    w = np.where(k == 0, np.sqrt(1.0 / length), np.sqrt(2.0 / length))
    return w * np.cos(np.pi * k * (2 * i + 1) / (2 * length))


def halves(x):
    high = x.astype(np.float32).astype(ml_dtypes.bfloat16)
    low = (x - high.astype(np.float64)).astype(ml_dtypes.bfloat16)
    return high, low


def left_table(x):
    high, low = halves(x)
    return np.concatenate([high, high, low], axis=1)


def right_table(x):
    high, low = halves(x)
    return np.concatenate([high, high, low], axis=0)


def face_rows(table):
    length = table.shape[0]
    sign = np.where(np.arange(length) % 2 == 0, 1.0, -1.0)
    low = table[:, :3].T
    forced = STENCIL.T @ low
    zero = np.zeros((2, length))
    return (
        np.concatenate([low, low * sign, zero], axis=0),
        np.concatenate([forced, forced * sign, zero], axis=0),
    )


def hall_tables(nx, ny, nz):
    faces, forced = face_rows(dct(nz))
    high, low = halves(faces)
    spread = np.concatenate(
        [np.concatenate([high, high], axis=1), np.concatenate([low, 0 * low], axis=1)], axis=0
    )
    pairs = np.concatenate([forced[k : k + 1] * faces for k in range(6)], axis=0)
    both = np.concatenate(halves(pairs), axis=0)
    respond = np.concatenate(
        [np.concatenate([both, 0 * both], axis=1), np.concatenate([0 * both, both], axis=1)], axis=0
    )
    high, low = halves(forced)
    outer = np.concatenate([high, high, low, low], axis=0)
    blank = np.zeros((32, 384), ml_dtypes.bfloat16)
    outer = np.concatenate([np.concatenate([blank[:, : 128 * t], outer, blank[:, 128 * t :]], axis=1) for t in range(4)], axis=0)
    return spread, respond, outer, left_table(dct(nx).T), left_table(dct(ny).T), right_table(dct(nz))


def room_tables(width):
    faces, forced, full = [], [], []
    for length in range(SHORTEST, width + 1):
        table = np.zeros((width, width))
        table[:length, :length] = dct(length)
        low, high = face_rows(table[:, :])
        faces.append(np.tile(low, (1, 4)))
        forced.append(np.tile(high, (1, 4)))
        full.append(np.tile(table.T, (1, 4)))
    return [np.stack(t).astype(np.float32) for t in (faces, forced, full)]


def factors(q):
    h = jnp.full_like(q, 2.0 / math.factorial(16))
    for n in range(6, -1, -1):
        h = 2.0 / math.factorial(2 * n + 2) - h * q
    return 2.0 - q * h, (TIME_STEP * TIME_STEP) * h


def mm(a, b):
    return jnp.dot(a, b, preferred_element_type=F32)


def mm_nt(a, b):
    return lax.dot_general(a, b, (((1,), (1,)), ((), ())), preferred_element_type=F32)


def split(x):
    high = x.astype(BF16)
    return high, (x - high.astype(F32)).astype(BF16)


def stacked(x, axis):
    high, low = split(x)
    return jnp.concatenate([high, low, high], axis=axis)


def lane_tiles(table):
    if table.shape[1] == 128:
        return table
    tile = math.gcd(table.shape[1], 128)
    return table.reshape(table.shape[0], -1, tile).transpose(1, 0, 2)


def broad(ref, tiles=None, rows=None):
    tiles = ref.shape[0] if tiles is None else tiles
    return jnp.concatenate([ref[j, :rows] for j in range(tiles)], axis=1)


def iota(shape, dim):
    return lax.broadcasted_iota(jnp.int32, shape, dim).astype(F32)


def total(mask, values, axis):
    return jnp.sum(jnp.where(mask, values, 0.0), axis=axis, keepdims=True)


def kernel(
    groups, slabs, count, loads, *refs,
):
    lengths, sources, refs = refs[0], refs[1 : 1 + loads], refs[1 + loads :]
    hall_out, room_out = refs[:2]
    landed, refs = refs[2 : 2 + loads], refs[2 + loads :]
    (
        hall_now, hall_prev, room_now, room_prev, ids,
        spread_t, respond_t, outer_t, cosx_t, cosy_t, cosz_t, face_t, force_t, room_t, cross_t,
    ) = landed
    (
        hall_c2, hall_gain, hall_base, hall_faces, hall_resp, hall_diff, hall_other,
        hall_send, hall_recv, a2a_send, a2a_recv,
        room_c2, room_gain, room_a, room_b, room_faces, raw_faces, raw_force, raw_full,
        face_l, force_l, full_l, pack_l, take_l, room_send, room_recv,
        load_sem, hall_ssem, hall_rsem, a2a_ssem, a2a_rsem, room_ssem, room_rsem,
    ) = refs
    me = lax.axis_index("grp")
    column = lax.axis_index("slab")
    nx, part_y, nz = hall_now.shape
    ny = part_y * slabs
    part_x = nx // slabs
    lanes = nx * part_y
    width = room_now.shape[0] // count
    batches = count // 4

    copies = [pltpu.make_async_copy(sources[i], landed[i], load_sem.at[i]) for i in range(loads)]
    order = [0, 5, 2, 4, 11, 1, 6, 3, 12, 7, 13, 8, 10, 9, 14]
    for i in order:
        copies[i].start()

    barrier = pltpu.get_barrier_semaphore()

    def greet_grp(step, carry):
        pl.semaphore_signal(
            barrier, inc=1, device_id=(lax.rem(me + step, groups), column), device_id_type=MESH
        )
        return carry

    def greet_slab(step, carry):
        pl.semaphore_signal(
            barrier, inc=1, device_id=(me, lax.rem(column + step, slabs)), device_id_type=MESH
        )
        return carry

    lax.fori_loop(1, groups, greet_grp, 0)
    lax.fori_loop(1, slabs, greet_slab, 0)
    hall_other[...] = jnp.zeros_like(hall_other)

    chunk = 256
    deep = chunk // part_y

    def spread_of(x):
        high, low = split(x)
        both = mm_nt(broad(spread_t), jnp.concatenate([high, low], axis=1))
        return both[:8] + both[8:]

    def first_faces(i, carry):
        x = hall_now[pl.ds(i * deep, deep)].reshape(chunk, nz)
        hall_faces[0, :, pl.ds(pl.multiple_of(i * chunk, chunk), chunk)] = spread_of(x)
        return carry

    copies[0].wait()
    copies[5].wait()
    lax.fori_loop(0, lanes // chunk, first_faces, 0)

    def hall_copy(t, side):
        peer = lax.rem(me + (1 if side == 0 else groups - 1), groups)
        return pltpu.make_async_remote_copy(
            src_ref=hall_send.at[t, side],
            dst_ref=hall_recv.at[t, side],
            send_sem=hall_ssem.at[t, side],
            recv_sem=hall_rsem.at[t, side],
            device_id=(peer, column),
            device_id_type=MESH,
        )

    def hall_put(t):
        own = hall_faces[t]
        for k in range(3):
            for j in range(lanes // 128):
                cut = slice(128 * j, 128 * j + 128)
                hall_send[t, 0, k, j : j + 1, :] = own[3 + k : 4 + k, cut]
                hall_send[t, 1, k, j : j + 1, :] = own[k : k + 1, cut]
        hall_copy(t, 0).start()
        hall_copy(t, 1).start()

    def hall_get(t):
        hall_copy(t, 0).wait_recv()
        hall_copy(t, 1).wait_recv()
        for k in range(3):
            for j in range(lanes // 128):
                cut = slice(128 * j, 128 * j + 128)
                hall_other[k : k + 1, cut] = hall_recv[t, 0, k, j : j + 1, :]
                hall_other[3 + k : 4 + k, cut] = hall_recv[t, 1, k, j : j + 1, :]
        row = lax.broadcasted_iota(jnp.int32, (8, lanes), 0)
        first = jnp.where(me > 0, 0, 3)
        last = jnp.where(me < groups - 1, 6, 3)
        diff = jnp.where((row >= first) & (row < last), hall_other[...] - hall_faces[t], 0.0)
        hall_diff[t] = diff
        return diff

    def hall_respond(t, lag, diff):
        acc = hall_faces[t + lag]
        for k in range(6):
            acc = acc + hall_resp[lag - 1, 8 * k : 8 * k + 8, :] * diff[k : k + 1, :]
        hall_faces[t + lag] = acc

    def terms(e):
        high = e.astype(BF16).astype(F32)
        low = e - high
        return jnp.concatenate([high, low, high, low], axis=0)

    def accumulate_early(i, carry):
        at = pl.ds(i * deep, deep)
        cols = pl.ds(pl.multiple_of(i * chunk, chunk), chunk)
        e = jnp.concatenate([terms(hall_diff[t, :, cols]) for t in range(3)], axis=0).T.astype(BF16)
        forced = mm(e, broad(outer_t, 3, 96))
        c2 = hall_c2[at]
        f0, f1, f2 = [forced[:, 128 * t : 128 * t + 128].reshape(deep, part_y, nz) for t in range(3)]
        square = c2 * c2
        weighted = c2 * ((square - 2.0) * f0 + f2) + (square - 1.0) * f1
        hall_base[at] = hall_base[at] + hall_gain[at] * weighted
        return carry

    def accumulate_last(i, carry):
        at = pl.ds(i * deep, deep)
        cols = pl.ds(pl.multiple_of(i * chunk, chunk), chunk)
        e = terms(hall_diff[3, :, cols]).T.astype(BF16)
        forced = mm(e, outer_t[0, :32]).reshape(deep, part_y, nz)
        hall_base[at] = hall_base[at] + hall_gain[at] * forced
        return carry

    pl.semaphore_wait(barrier, groups + slabs - 2)
    hall_put(0)

    lane = lax.broadcasted_iota(jnp.int32, (width, 128), 1)
    kx = lax.broadcasted_iota(jnp.int32, (width, 128), 0)

    def room_first(b, carry):
        for i in range(4):
            r = 4 * b + i
            length = lengths[0, 0, r]
            which = jnp.maximum(length - SHORTEST, 0)
            at = pl.ds(pl.multiple_of(r * width, width), width)
            at8 = pl.ds(pl.multiple_of(r * 8, 8), 8)
            mine = lane // width == i
            raw_faces[at8, :] = jnp.where(mine[:8], face_t[which], 0.0)
            room_a[at, :] = jnp.where(kx < jnp.full((width, 128), length, jnp.int32), room_now[at, :], 0.0)
        return carry

    copies[2].wait()
    copies[4].wait()
    copies[11].wait()
    lax.fori_loop(0, batches, room_first, 0)
    for b in range(batches):
        cut = slice(32 * b, 32 * b + 32)
        big = slice(128 * b, 128 * b + 128)
        high, low = split(raw_faces[cut, :])
        face_l[cut, :] = jnp.concatenate([high, high, low], axis=1)
        room_faces[cut, :] = mm(face_l[cut, :], stacked(room_a[big, :], 0))

    bits = int(math.log2(count))
    wide = 8 * count
    span = ids.shape[1]
    row_lanes = min(128, span)
    flat = jnp.concatenate(
        [ids[0:1, row_lanes * j : row_lanes * (j + 1)] for j in range(span // row_lanes)], axis=0
    )
    device = (flat >> bits).astype(F32)
    slot = (flat & (count - 1)).astype(F32)
    lane_i = lax.broadcasted_iota(jnp.int32, (count, wide), 1)
    p_col = iota((count, wide), 0)
    p_row = (lane_i >> 3).astype(F32)
    f_row = (lane_i & 7).astype(F32)
    expand = lax.broadcasted_iota(jnp.int32, (row_lanes, wide), 1) >> 3
    expand = jnp.where(expand == lax.broadcasted_iota(jnp.int32, (row_lanes, wide), 0), 1.0, 0.0)
    s_row = mm(device.astype(BF16), expand.astype(BF16))[0:1]
    s_col = device.T[:count, 0:1]
    same = s_col == s_row
    rank_row = total(same & (p_col < p_row), 1.0, 0)
    rank_col = total(same & (p_row < p_col) & (f_row == 0.0), 1.0, 1)
    home = me.astype(F32) - s_col
    home = jnp.where(home < 0.0, home + groups, home)
    per_row = row_lanes // count
    home = jnp.concatenate([home] * per_row, axis=0)
    shape = (row_lanes, span // row_lanes)
    group = per_row * lax.broadcasted_iota(jnp.int32, shape, 1)
    group = group + (lax.broadcasted_iota(jnp.int32, shape, 0) >> bits)
    landing = total(group.astype(F32) == home, slot.T, 1)
    landing = sum(landing[count * i : count * (i + 1)] for i in range(per_row))
    match = landing == p_row
    ls_row = total(match, jnp.broadcast_to(s_col, (count, wide)), 0)
    lr_row = total(match, jnp.broadcast_to(rank_col, (count, wide)), 0)

    def back(s):
        return jnp.where(s == 0.0, 0.0, groups - s)

    f = f_row[0:1]
    layer = jnp.where(f < 3.0, f, f - 3.0)
    pack_row = jnp.where(
        f < 3.0, 16.0 * back(ls_row) + 6.0 + 3.0 * lr_row + layer, 16.0 * s_row + 3.0 * rank_row + layer
    )
    take_row = jnp.where(
        f < 3.0, 16.0 * ls_row + 3.0 * lr_row + layer, 16.0 * back(s_row) + 6.0 + 3.0 * rank_row + layer
    )
    pack_row = jnp.where(f < 6.0, pack_row, -1.0)
    take_row = jnp.where(f < 6.0, take_row, -1.0)
    slots = 16 * groups
    pack_l[...] = jnp.where(iota((slots, wide), 0) == pack_row, 1.0, 0.0).astype(BF16)

    def room_copy(t, step):
        return pltpu.make_async_remote_copy(
            src_ref=room_send.at[t, step],
            dst_ref=room_recv.at[t, step - 1],
            send_sem=room_ssem.at[t, step - 1],
            recv_sem=room_rsem.at[t, step - 1],
            device_id=(lax.rem(me + step, groups), column),
            device_id_type=MESH,
        )

    def far_first(i, count):
        half = i // 2
        return count // 2 + jnp.where(lax.rem(i, 2) == 0, half, -half)

    def two_parts(x):
        return jnp.concatenate(split(x), axis=1)

    def room_put(t):
        packed = mm(pack_l[...], two_parts(room_faces[...]))
        packed = packed[:, :128] + packed[:, 128:]
        room_send[t] = packed.reshape(groups, 16, 128)[:, :12, :]

        def body(i, carry):
            room_copy(t, far_first(i, groups)).start()
            return carry

        lax.fori_loop(1, groups, body, 0)

    def room_get(t):
        def body(i, carry):
            room_copy(t, far_first(i, groups)).wait_recv()
            return carry

        lax.fori_loop(1, groups, body, 0)
        got = jnp.concatenate([room_send[t, 0:1], room_recv[t]], axis=0)
        got = jnp.concatenate([got, jnp.zeros((groups, 4, 128), F32)], axis=1).reshape(slots, 128)
        other = mm(take_l[...], two_parts(got))
        return other[:, :128] + other[:, 128:] - room_faces[...]

    def room_sent(t):
        def body(step, carry):
            room_copy(t, step).wait_send()
            return carry

        lax.fori_loop(1, groups, body, 0)

    def room_step(t):
        diff = room_get(t)
        now, prev = (room_a, room_b) if t % 2 == 0 else (room_b, room_a)
        for b in range(batches):
            cut = slice(32 * b, 32 * b + 32)
            big = slice(128 * b, 128 * b + 128)
            high, low = split(diff[cut])
            forced = mm(force_l[big, :], jnp.concatenate([high, low, high, low], axis=0))
            fresh = room_c2[big, :] * now[big, :] - prev[big, :] + room_gain[big, :] * forced
            if t < STEPS - 1:
                prev[big, :] = fresh
                room_faces[cut, :] = mm(face_l[cut, :], stacked(fresh, 0))
            else:
                x = mm(full_l[big, :], stacked(fresh, 0))
                room_out[big, :] = mm(stacked(x, 1), cross_t[...])
        if t < STEPS - 1:
            room_put(t + 1)
            room_sent(t)

    room_put(0)

    yz = lax.broadcasted_iota(jnp.int32, (part_y, nz), 0) + column * part_y
    ky_f = yz.astype(F32)
    kz_f = iota((part_y, nz), 1)
    q_yz = (SCALE / ny**2) * (ky_f * ky_f) + (SCALE / nz**2) * (kz_f * kz_f)

    def prepare_first(i, carry):
        at = pl.ds(i * deep, deep)
        cols = pl.ds(pl.multiple_of(i * chunk, chunk), chunk)
        a = (lax.broadcasted_iota(jnp.int32, (deep, part_y, nz), 0) + i * deep).astype(F32)
        c2, gain = factors((SCALE / nx**2) * (a * a) + q_yz[None])
        hall_c2[at] = c2
        hall_gain[at] = gain
        fresh = c2 * hall_now[at] - hall_prev[at]
        hall_base[at] = fresh
        hall_faces[1, :, cols] = spread_of(fresh.reshape(chunk, nz))
        both = mm_nt(respond_t[0, :96], gain.reshape(chunk, nz).astype(BF16))
        hall_resp[0, :, cols] = both[:48] + both[48:]
        return carry

    def prepare_last(i, carry):
        at = pl.ds(i * deep, deep)
        cols = pl.ds(pl.multiple_of(i * chunk, chunk), chunk)
        c2 = hall_c2[at]
        gain = hall_gain[at]
        m1 = hall_base[at]
        m2 = c2 * m1 - hall_now[at]
        m3 = c2 * m2 - m1
        hall_base[at] = c2 * m3 - m2
        hall_faces[2, :, cols] = spread_of(m2.reshape(chunk, nz))
        hall_faces[3, :, cols] = spread_of(m3.reshape(chunk, nz))
        s2 = gain * c2
        s3 = s2 * c2 - gain
        both = [s.reshape(chunk, nz).astype(BF16) for s in (s2, s3)]
        both = mm_nt(broad(respond_t), jnp.concatenate(both, axis=1))
        hall_resp[1, :, cols] = both[:48] + both[48:96]
        hall_resp[2, :, cols] = both[96:144] + both[144:]
        return carry

    copies[1].wait()
    copies[6].wait()
    lax.fori_loop(0, lanes // chunk, prepare_first, 0)
    diff = hall_get(0)
    hall_respond(0, 1, diff)
    hall_put(1)
    lax.fori_loop(0, lanes // chunk, prepare_last, 0)
    hall_respond(0, 2, diff)
    hall_respond(0, 3, diff)
    diff = hall_get(1)
    hall_respond(1, 1, diff)
    hall_put(2)
    hall_respond(1, 2, diff)

    q_cross = (lane // SZ).astype(F32) / SY
    q_cross = SCALE * (q_cross * q_cross)
    z_part = (lane % SZ).astype(F32) / SZ
    q_cross = q_cross + SCALE * (z_part * z_part)
    kx_f = kx.astype(F32)
    kx_sq = SCALE * (kx_f * kx_f)

    def room_second(b, carry):
        for i in range(4):
            r = 4 * b + i
            length = lengths[0, 0, r]
            which = jnp.maximum(length - SHORTEST, 0)
            at = pl.ds(pl.multiple_of(r * width, width), width)
            at8 = pl.ds(pl.multiple_of(r * 8, 8), 8)
            mine = lane // width == i
            raw_force[at8, :] = jnp.where(mine[:8], force_t[which], 0.0)
            extent = jnp.full((width, 128), length, jnp.int32)
            live = kx < extent
            extent = extent.astype(F32)
            c2, gain = factors(kx_sq / (extent * extent) + q_cross)
            room_c2[at, :] = c2
            room_gain[at, :] = gain
            room_b[at, :] = jnp.where(live, room_prev[at, :], 0.0)
        return carry

    copies[3].wait()
    copies[12].wait()
    copies[7].wait()
    lax.fori_loop(0, batches, room_second, 0)
    for b in range(batches):
        x = raw_force[32 * b : 32 * b + 32, :]
        high = x.astype(BF16).astype(F32)
        low = x - high
        force_l[128 * b : 128 * b + 128, :] = jnp.concatenate([high, high, low, low], axis=0).T.astype(BF16)
    take_col = jnp.broadcast_to(take_row, (8, wide)).T[:, 0:1]
    take_l[...] = jnp.where(iota((wide, slots), 1) == take_col, 1.0, 0.0).astype(BF16)

    diff = hall_get(2)
    hall_respond(2, 1, diff)
    hall_put(3)
    room_step(0)
    lax.fori_loop(0, lanes // chunk, accumulate_early, 0)
    hall_get(3)
    lax.fori_loop(0, lanes // chunk, accumulate_last, 0)

    parts = 2
    part_b = part_y // parts

    def a2a_copy(h, step):
        peer = lax.rem(column + step, slabs)
        return pltpu.make_async_remote_copy(
            src_ref=a2a_send.at[pl.ds(part_b * h, part_b), pl.ds(pl.multiple_of(peer * part_x, part_x), part_x), :],
            dst_ref=a2a_recv.at[pl.ds(column * part_y + part_b * h, part_b)],
            send_sem=a2a_ssem.at[h, step],
            recv_sem=a2a_rsem.at[h, step],
            device_id=(me, peer),
            device_id_type=MESH,
        )

    copies[8].wait()
    for h in range(parts):
        for b in range(part_b * h, part_b * h + part_b, 2):
            pair = [stacked(hall_base[:, b + i, :], 0) for i in range(2)]
            y = mm(broad(cosx_t), jnp.concatenate(pair, axis=1))
            a2a_send[b] = y[:, :nz]
            a2a_send[b + 1] = y[:, nz:]

        def a2a_start(i, carry):
            a2a_copy(h, far_first(i, slabs)).start()
            return carry

        lax.fori_loop(1, slabs, a2a_start, 0)

    def z_part_of(x):
        x = stacked(x.reshape(part_y * part_x, nz), 1)
        return mm(x, cosz_t[...]).reshape(part_y, part_x, nz)

    copies[10].wait()
    own = pl.ds(pl.multiple_of(column * part_x, part_x), part_x)
    a2a_recv[pl.ds(column * part_y, part_y)] = z_part_of(a2a_send[:, own, :])

    def a2a_take(i, carry):
        step = far_first(i, slabs)
        a2a_copy(0, step).wait_recv()
        a2a_copy(1, step).wait_recv()
        source = lax.rem(column + slabs - step, slabs)
        at = pl.ds(source * part_y, part_y)
        a2a_recv[at] = z_part_of(a2a_recv[at])
        return carry

    def room_tables_full(b, carry):
        for i in range(4):
            r = 4 * b + i
            which = jnp.maximum(lengths[0, 0, r] - SHORTEST, 0)
            at = pl.ds(pl.multiple_of(r * width, width), width)
            raw_full[at, :] = jnp.where(lane // width == i, room_t[which], 0.0)
        return carry

    copies[13].wait()
    copies[14].wait()
    lax.fori_loop(0, batches, room_tables_full, 0)
    for b in range(batches):
        big = slice(128 * b, 128 * b + 128)
        high, low = split(raw_full[big, :])
        full_l[big, :] = jnp.concatenate([high, high, low], axis=1)

    room_step(1)
    for t in range(STEPS - 1):
        hall_copy(t, 0).wait_send()
        hall_copy(t, 1).wait_send()
    room_step(2)
    hall_copy(3, 0).wait_send()
    hall_copy(3, 1).wait_send()
    room_step(3)
    room_sent(3)
    lax.fori_loop(1, slabs, a2a_take, 0)
    copies[9].wait()
    for x in range(0, part_x, 2):
        pair = jnp.concatenate([stacked(a2a_recv[:, x, :], 0), stacked(a2a_recv[:, x + 1, :], 0)], axis=1)
        y = mm(broad(cosy_t), pair)
        hall_out[x] = y[:, :nz]
        hall_out[x + 1] = y[:, nz:]

    def a2a_sent(step, carry):
        a2a_copy(0, step).wait_send()
        a2a_copy(1, step).wait_send()
        return carry

    lax.fori_loop(1, slabs, a2a_sent, 0)


def local(hall_now, hall_prev, room_now, room_prev, room_length, right_neighbor):
    groups = lax.axis_size("grp")
    slabs = lax.axis_size("slab")
    _, nx, part_y, nz = hall_now.shape
    _, _, count, width, cross = room_now.shape
    ny = part_y * slabs
    part_x = nx // slabs
    lanes = nx * part_y
    slots = 16 * groups
    rows = count * width
    inputs = [
        hall_now[0], hall_prev[0], room_now.reshape(rows, cross), room_prev.reshape(rows, cross), right_neighbor,
    ]
    inputs += [jnp.asarray(lane_tiles(t)) for t in hall_tables(nx, ny, nz)]
    inputs += [jnp.asarray(t) for t in room_tables(width)]
    inputs += [jnp.asarray(right_table(np.kron(dct(SY), dct(SZ))))]
    vmem = pl.BlockSpec(memory_space=pltpu.VMEM)
    smem = pl.BlockSpec(memory_space=pltpu.SMEM)
    away = pl.BlockSpec(memory_space=pl.ANY)
    dma = pltpu.SemaphoreType.DMA
    hall_pressure, room_pressure = pl.pallas_call(
        functools.partial(kernel, groups, slabs, count, len(inputs)),
        out_shape=(
            jax.ShapeDtypeStruct((part_x, ny, nz), F32),
            jax.ShapeDtypeStruct((rows, cross), F32),
        ),
        in_specs=[smem] + [away] * len(inputs),
        out_specs=(vmem, vmem),
        scratch_shapes=[pltpu.VMEM(x.shape, x.dtype) for x in inputs]
        + [
            pltpu.VMEM((nx, part_y, nz), F32),
            pltpu.VMEM((nx, part_y, nz), F32),
            pltpu.VMEM((nx, part_y, nz), F32),
            pltpu.VMEM((STEPS, 8, lanes), F32),
            pltpu.VMEM((STEPS - 1, 48, lanes), F32),
            pltpu.VMEM((STEPS, 8, lanes), F32),
            pltpu.VMEM((8, lanes), F32),
            pltpu.VMEM((STEPS, 2, 3, lanes // 128, 128), F32),
            pltpu.VMEM((STEPS, 2, 3, lanes // 128, 128), F32),
            pltpu.VMEM((part_y, nx, nz), F32),
            pltpu.VMEM((ny, part_x, nz), F32),
            pltpu.VMEM((rows, cross), F32),
            pltpu.VMEM((rows, cross), F32),
            pltpu.VMEM((rows, cross), F32),
            pltpu.VMEM((rows, cross), F32),
            pltpu.VMEM((8 * count, cross), F32),
            pltpu.VMEM((8 * count, 4 * width), F32),
            pltpu.VMEM((8 * count, 4 * width), F32),
            pltpu.VMEM((rows, 4 * width), F32),
            pltpu.VMEM((8 * count, 12 * width), BF16),
            pltpu.VMEM((rows, 128), BF16),
            pltpu.VMEM((rows, 12 * width), BF16),
            pltpu.VMEM((slots, 8 * count), BF16),
            pltpu.VMEM((8 * count, slots), BF16),
            pltpu.VMEM((STEPS, groups, 12, 128), F32),
            pltpu.VMEM((STEPS, groups - 1, 12, 128), F32),
            dma((len(inputs),)),
            dma((STEPS, 2)),
            dma((STEPS, 2)),
            dma((2, slabs)),
            dma((2, slabs)),
            dma((STEPS, groups - 1)),
            dma((STEPS, groups - 1)),
        ],
        compiler_params=pltpu.CompilerParams(
            collective_id=0, has_side_effects=True, vmem_limit_bytes=60 * 1024 * 1024
        ),
    )(room_length, *inputs)
    return (hall_pressure[None], room_pressure.reshape(1, 1, count, width, cross))


def solution(mesh):
    in_specs = (
        P("grp", None, "slab", None),
        P("grp", None, "slab", None),
        P("grp", "slab", None, None, None),
        P("grp", "slab", None, None, None),
        P("grp", "slab", None),
        P("slab", None),
    )
    out_specs = (P("grp", "slab", None, None), P("grp", "slab", None, None, None))
    return jax.shard_map(local, mesh=mesh, in_specs=in_specs, out_specs=out_specs, check_vma=False)
```

```python
import functools
import math

import jax
import jax.numpy as jnp
import ml_dtypes
import numpy as np
from jax import lax
from jax.experimental import pallas as pl
from jax.experimental.pallas import tpu as pltpu
from jax.sharding import PartitionSpec as P

SY = 8
SZ = 16
STEPS = 4
SHORTEST = 16
TIME_STEP = 0.4
SCALE = (TIME_STEP * math.pi) ** 2
STENCIL = np.array([[270, -27, 2], [-27, 2, 0], [2, 0, 0]], np.float64) / 180.0
F32 = jnp.float32
BF16 = jnp.bfloat16
MESH = pl.DeviceIdType.MESH


def dct(length):
    k = np.arange(length)[:, None]
    i = np.arange(length)[None, :]
    w = np.where(k == 0, np.sqrt(1.0 / length), np.sqrt(2.0 / length))
    return w * np.cos(np.pi * k * (2 * i + 1) / (2 * length))


def halves(x):
    high = x.astype(np.float32).astype(ml_dtypes.bfloat16)
    low = (x - high.astype(np.float64)).astype(ml_dtypes.bfloat16)
    return high, low


def left_table(x):
    high, low = halves(x)
    return np.concatenate([high, high, low], axis=1)


def right_table(x):
    high, low = halves(x)
    return np.concatenate([high, high, low], axis=0)


def face_rows(table):
    length = table.shape[0]
    sign = np.where(np.arange(length) % 2 == 0, 1.0, -1.0)
    low = table[:, :3].T
    forced = STENCIL.T @ low
    zero = np.zeros((2, length))
    return (
        np.concatenate([low, low * sign, zero], axis=0),
        np.concatenate([forced, forced * sign, zero], axis=0),
    )


def hall_tables(nx, ny, nz):
    faces, forced = face_rows(dct(nz))
    high, low = halves(faces)
    spread = np.concatenate(
        [np.concatenate([high, high], axis=1), np.concatenate([low, 0 * low], axis=1)], axis=0
    )
    pairs = np.concatenate([forced[k : k + 1] * faces for k in range(6)], axis=0)
    both = np.concatenate(halves(pairs), axis=0)
    respond = np.concatenate(
        [np.concatenate([both, 0 * both], axis=1), np.concatenate([0 * both, both], axis=1)], axis=0
    )
    high, low = halves(forced)
    outer = np.concatenate([high, high, low, low], axis=0)
    blank = np.zeros((32, 384), ml_dtypes.bfloat16)
    outer = np.concatenate([np.concatenate([blank[:, : 128 * t], outer, blank[:, 128 * t :]], axis=1) for t in range(4)], axis=0)
    return spread, respond, outer, left_table(dct(nx).T), left_table(dct(ny).T), right_table(dct(nz))


def room_tables(width):
    faces, forced, full = [], [], []
    for length in range(SHORTEST, width + 1):
        table = np.zeros((width, width))
        table[:length, :length] = dct(length)
        low, high = face_rows(table[:, :])
        faces.append(np.tile(low, (1, 4)))
        forced.append(np.tile(high, (1, 4)))
        full.append(np.tile(table.T, (1, 4)))
    return [np.stack(t).astype(np.float32) for t in (faces, forced, full)]


def factors(q):
    h = jnp.full_like(q, 2.0 / math.factorial(16))
    for n in range(6, -1, -1):
        h = 2.0 / math.factorial(2 * n + 2) - h * q
    return 2.0 - q * h, (TIME_STEP * TIME_STEP) * h


def mm(a, b):
    return jnp.dot(a, b, preferred_element_type=F32)


def mm_nt(a, b):
    return lax.dot_general(a, b, (((1,), (1,)), ((), ())), preferred_element_type=F32)


def split(x):
    high = x.astype(BF16)
    return high, (x - high.astype(F32)).astype(BF16)


def stacked(x, axis):
    high, low = split(x)
    return jnp.concatenate([high, low, high], axis=axis)


def lane_tiles(table):
    if table.shape[1] == 128:
        return table
    tile = math.gcd(table.shape[1], 128)
    return table.reshape(table.shape[0], -1, tile).transpose(1, 0, 2)


def broad(ref, tiles=None, rows=None):
    tiles = ref.shape[0] if tiles is None else tiles
    return jnp.concatenate([ref[j, :rows] for j in range(tiles)], axis=1)


def iota(shape, dim):
    return lax.broadcasted_iota(jnp.int32, shape, dim).astype(F32)


def total(mask, values, axis):
    return jnp.sum(jnp.where(mask, values, 0.0), axis=axis, keepdims=True)


def kernel(
    groups, slabs, count, loads, *refs,
):
    lengths, sources, refs = refs[0], refs[1 : 1 + loads], refs[1 + loads :]
    hall_far, room_far = refs[:2]
    landed, refs = refs[2 : 2 + loads], refs[2 + loads :]
    (
        hall_now, hall_prev, room_now, room_prev, ids,
        spread_t, respond_t, outer_t, cosx_t, cosy_t, cosz_t, face_t, force_t, room_t, cross_t,
    ) = landed
    (
        hall_c2, hall_gain, hall_base, hall_faces, hall_resp, hall_diff, hall_other,
        hall_send, hall_recv, a2a_send, a2a_recv,
        room_c2, room_gain, room_a, room_b, room_faces, raw_faces, raw_force, raw_full,
        face_l, force_l, full_l, pack_l, take_l, room_send, room_recv, hall_out, room_out,
        load_sem, store_sem, hall_ssem, hall_rsem, a2a_ssem, a2a_rsem, room_ssem, room_rsem,
    ) = refs
    me = lax.axis_index("grp")
    column = lax.axis_index("slab")
    nx, part_y, nz = hall_now.shape
    ny = part_y * slabs
    part_x = nx // slabs
    lanes = nx * part_y
    width = room_now.shape[0] // count
    batches = count // 4

    copies = [pltpu.make_async_copy(sources[i], landed[i], load_sem.at[i]) for i in range(loads)]
    order = [0, 5, 2, 4, 11, 1, 6, 3, 12, 7, 13, 8, 10, 9, 14]
    for i in order:
        copies[i].start()

    barrier = pltpu.get_barrier_semaphore()

    def greet_grp(step, carry):
        pl.semaphore_signal(
            barrier, inc=1, device_id=(lax.rem(me + step, groups), column), device_id_type=MESH
        )
        return carry

    def greet_slab(step, carry):
        pl.semaphore_signal(
            barrier, inc=1, device_id=(me, lax.rem(column + step, slabs)), device_id_type=MESH
        )
        return carry

    lax.fori_loop(1, groups, greet_grp, 0)
    lax.fori_loop(1, slabs, greet_slab, 0)
    hall_other[...] = jnp.zeros_like(hall_other)

    chunk = 256
    deep = chunk // part_y

    def spread_of(x):
        high, low = split(x)
        both = mm_nt(broad(spread_t), jnp.concatenate([high, low], axis=1))
        return both[:8] + both[8:]

    def first_faces(i, carry):
        x = hall_now[pl.ds(i * deep, deep)].reshape(chunk, nz)
        hall_faces[0, :, pl.ds(pl.multiple_of(i * chunk, chunk), chunk)] = spread_of(x)
        return carry

    copies[0].wait()
    copies[5].wait()
    lax.fori_loop(0, lanes // chunk, first_faces, 0)

    def hall_copy(t, side):
        peer = lax.rem(me + (1 if side == 0 else groups - 1), groups)
        return pltpu.make_async_remote_copy(
            src_ref=hall_send.at[t, side],
            dst_ref=hall_recv.at[t, side],
            send_sem=hall_ssem.at[t, side],
            recv_sem=hall_rsem.at[t, side],
            device_id=(peer, column),
            device_id_type=MESH,
        )

    def hall_put(t):
        own = hall_faces[t]
        for k in range(3):
            for j in range(lanes // 128):
                cut = slice(128 * j, 128 * j + 128)
                hall_send[t, 0, k, j : j + 1, :] = own[3 + k : 4 + k, cut]
                hall_send[t, 1, k, j : j + 1, :] = own[k : k + 1, cut]
        hall_copy(t, 0).start()
        hall_copy(t, 1).start()

    def hall_get(t):
        hall_copy(t, 0).wait_recv()
        hall_copy(t, 1).wait_recv()
        for k in range(3):
            for j in range(lanes // 128):
                cut = slice(128 * j, 128 * j + 128)
                hall_other[k : k + 1, cut] = hall_recv[t, 0, k, j : j + 1, :]
                hall_other[3 + k : 4 + k, cut] = hall_recv[t, 1, k, j : j + 1, :]
        row = lax.broadcasted_iota(jnp.int32, (8, lanes), 0)
        first = jnp.where(me > 0, 0, 3)
        last = jnp.where(me < groups - 1, 6, 3)
        diff = jnp.where((row >= first) & (row < last), hall_other[...] - hall_faces[t], 0.0)
        hall_diff[t] = diff
        return diff

    def hall_respond(t, lag, diff):
        acc = hall_faces[t + lag]
        for k in range(6):
            acc = acc + hall_resp[lag - 1, 8 * k : 8 * k + 8, :] * diff[k : k + 1, :]
        hall_faces[t + lag] = acc

    def terms(e):
        high = e.astype(BF16).astype(F32)
        low = e - high
        return jnp.concatenate([high, low, high, low], axis=0)

    def accumulate_early(i, carry):
        at = pl.ds(i * deep, deep)
        cols = pl.ds(pl.multiple_of(i * chunk, chunk), chunk)
        e = jnp.concatenate([terms(hall_diff[t, :, cols]) for t in range(3)], axis=0).T.astype(BF16)
        forced = mm(e, broad(outer_t, 3, 96))
        c2 = hall_c2[at]
        f0, f1, f2 = [forced[:, 128 * t : 128 * t + 128].reshape(deep, part_y, nz) for t in range(3)]
        square = c2 * c2
        weighted = c2 * ((square - 2.0) * f0 + f2) + (square - 1.0) * f1
        hall_base[at] = hall_base[at] + hall_gain[at] * weighted
        return carry

    def accumulate_last(i, carry):
        at = pl.ds(i * deep, deep)
        cols = pl.ds(pl.multiple_of(i * chunk, chunk), chunk)
        e = terms(hall_diff[3, :, cols]).T.astype(BF16)
        forced = mm(e, outer_t[0, :32]).reshape(deep, part_y, nz)
        hall_base[at] = hall_base[at] + hall_gain[at] * forced
        return carry

    pl.semaphore_wait(barrier, groups + slabs - 2)
    hall_put(0)

    lane = lax.broadcasted_iota(jnp.int32, (width, 128), 1)
    kx = lax.broadcasted_iota(jnp.int32, (width, 128), 0)

    def room_first(b, carry):
        for i in range(4):
            r = 4 * b + i
            length = lengths[0, 0, r]
            which = jnp.maximum(length - SHORTEST, 0)
            at = pl.ds(pl.multiple_of(r * width, width), width)
            at8 = pl.ds(pl.multiple_of(r * 8, 8), 8)
            mine = lane // width == i
            raw_faces[at8, :] = jnp.where(mine[:8], face_t[which], 0.0)
            room_a[at, :] = jnp.where(kx < jnp.full((width, 128), length, jnp.int32), room_now[at, :], 0.0)
        return carry

    copies[2].wait()
    copies[4].wait()
    copies[11].wait()
    lax.fori_loop(0, batches, room_first, 0)
    for b in range(batches):
        cut = slice(32 * b, 32 * b + 32)
        big = slice(128 * b, 128 * b + 128)
        high, low = split(raw_faces[cut, :])
        face_l[cut, :] = jnp.concatenate([high, high, low], axis=1)
        room_faces[cut, :] = mm(face_l[cut, :], stacked(room_a[big, :], 0))

    bits = int(math.log2(count))
    wide = 8 * count
    span = ids.shape[1]
    row_lanes = min(128, span)
    flat = jnp.concatenate(
        [ids[0:1, row_lanes * j : row_lanes * (j + 1)] for j in range(span // row_lanes)], axis=0
    )
    device = (flat >> bits).astype(F32)
    slot = (flat & (count - 1)).astype(F32)
    lane_i = lax.broadcasted_iota(jnp.int32, (count, wide), 1)
    p_col = iota((count, wide), 0)
    p_row = (lane_i >> 3).astype(F32)
    f_row = (lane_i & 7).astype(F32)
    expand = lax.broadcasted_iota(jnp.int32, (row_lanes, wide), 1) >> 3
    expand = jnp.where(expand == lax.broadcasted_iota(jnp.int32, (row_lanes, wide), 0), 1.0, 0.0)
    s_row = mm(device.astype(BF16), expand.astype(BF16))[0:1]
    s_col = device.T[:count, 0:1]
    same = s_col == s_row
    rank_row = total(same & (p_col < p_row), 1.0, 0)
    rank_col = total(same & (p_row < p_col) & (f_row == 0.0), 1.0, 1)
    home = me.astype(F32) - s_col
    home = jnp.where(home < 0.0, home + groups, home)
    per_row = row_lanes // count
    home = jnp.concatenate([home] * per_row, axis=0)
    shape = (row_lanes, span // row_lanes)
    group = per_row * lax.broadcasted_iota(jnp.int32, shape, 1)
    group = group + (lax.broadcasted_iota(jnp.int32, shape, 0) >> bits)
    landing = total(group.astype(F32) == home, slot.T, 1)
    landing = sum(landing[count * i : count * (i + 1)] for i in range(per_row))
    match = landing == p_row
    ls_row = total(match, jnp.broadcast_to(s_col, (count, wide)), 0)
    lr_row = total(match, jnp.broadcast_to(rank_col, (count, wide)), 0)

    def back(s):
        return jnp.where(s == 0.0, 0.0, groups - s)

    f = f_row[0:1]
    layer = jnp.where(f < 3.0, f, f - 3.0)
    pack_row = jnp.where(
        f < 3.0, 16.0 * back(ls_row) + 6.0 + 3.0 * lr_row + layer, 16.0 * s_row + 3.0 * rank_row + layer
    )
    take_row = jnp.where(
        f < 3.0, 16.0 * ls_row + 3.0 * lr_row + layer, 16.0 * back(s_row) + 6.0 + 3.0 * rank_row + layer
    )
    pack_row = jnp.where(f < 6.0, pack_row, -1.0)
    take_row = jnp.where(f < 6.0, take_row, -1.0)
    slots = 16 * groups
    pack_l[...] = jnp.where(iota((slots, wide), 0) == pack_row, 1.0, 0.0).astype(BF16)

    def room_copy(t, step):
        return pltpu.make_async_remote_copy(
            src_ref=room_send.at[t, step],
            dst_ref=room_recv.at[t, step - 1],
            send_sem=room_ssem.at[t, step - 1],
            recv_sem=room_rsem.at[t, step - 1],
            device_id=(lax.rem(me + step, groups), column),
            device_id_type=MESH,
        )

    def far_first(i, count):
        half = i // 2
        return count // 2 + jnp.where(lax.rem(i, 2) == 0, half, -half)

    def two_parts(x):
        return jnp.concatenate(split(x), axis=1)

    def room_put(t):
        packed = mm(pack_l[...], two_parts(room_faces[...]))
        packed = packed[:, :128] + packed[:, 128:]
        room_send[t] = packed.reshape(groups, 16, 128)[:, :12, :]

        def body(i, carry):
            room_copy(t, far_first(i, groups)).start()
            return carry

        lax.fori_loop(1, groups, body, 0)

    def store(which, i):
        near, far = ((hall_out, hall_far), (room_out, room_far))[which]
        size = near.shape[0] // (8 if which == 0 else batches)
        at = pl.ds(i * size, size)
        return pltpu.make_async_copy(near.at[at], far.at[at], store_sem.at[which, i])

    def room_get(t):
        def body(i, carry):
            room_copy(t, far_first(i, groups)).wait_recv()
            return carry

        lax.fori_loop(1, groups, body, 0)
        got = jnp.concatenate([room_send[t, 0:1], room_recv[t]], axis=0)
        got = jnp.concatenate([got, jnp.zeros((groups, 4, 128), F32)], axis=1).reshape(slots, 128)
        other = mm(take_l[...], two_parts(got))
        return other[:, :128] + other[:, 128:] - room_faces[...]

    def room_sent(t):
        def body(step, carry):
            room_copy(t, step).wait_send()
            return carry

        lax.fori_loop(1, groups, body, 0)

    def room_step(t):
        diff = room_get(t)
        now, prev = (room_a, room_b) if t % 2 == 0 else (room_b, room_a)
        for b in range(batches):
            cut = slice(32 * b, 32 * b + 32)
            big = slice(128 * b, 128 * b + 128)
            high, low = split(diff[cut])
            forced = mm(force_l[big, :], jnp.concatenate([high, low, high, low], axis=0))
            fresh = room_c2[big, :] * now[big, :] - prev[big, :] + room_gain[big, :] * forced
            if t < STEPS - 1:
                prev[big, :] = fresh
                room_faces[cut, :] = mm(face_l[cut, :], stacked(fresh, 0))
            else:
                x = mm(full_l[big, :], stacked(fresh, 0))
                room_out[big, :] = mm(stacked(x, 1), cross_t[...])
                store(1, b).start()
        if t < STEPS - 1:
            room_put(t + 1)
            room_sent(t)

    room_put(0)

    yz = lax.broadcasted_iota(jnp.int32, (part_y, nz), 0) + column * part_y
    ky_f = yz.astype(F32)
    kz_f = iota((part_y, nz), 1)
    q_yz = (SCALE / ny**2) * (ky_f * ky_f) + (SCALE / nz**2) * (kz_f * kz_f)

    def prepare_first(i, carry):
        at = pl.ds(i * deep, deep)
        cols = pl.ds(pl.multiple_of(i * chunk, chunk), chunk)
        a = (lax.broadcasted_iota(jnp.int32, (deep, part_y, nz), 0) + i * deep).astype(F32)
        c2, gain = factors((SCALE / nx**2) * (a * a) + q_yz[None])
        hall_c2[at] = c2
        hall_gain[at] = gain
        fresh = c2 * hall_now[at] - hall_prev[at]
        hall_base[at] = fresh
        hall_faces[1, :, cols] = spread_of(fresh.reshape(chunk, nz))
        both = mm_nt(respond_t[0, :96], gain.reshape(chunk, nz).astype(BF16))
        hall_resp[0, :, cols] = both[:48] + both[48:]
        return carry

    def prepare_last(i, carry):
        at = pl.ds(i * deep, deep)
        cols = pl.ds(pl.multiple_of(i * chunk, chunk), chunk)
        c2 = hall_c2[at]
        gain = hall_gain[at]
        m1 = hall_base[at]
        m2 = c2 * m1 - hall_now[at]
        m3 = c2 * m2 - m1
        hall_base[at] = c2 * m3 - m2
        hall_faces[2, :, cols] = spread_of(m2.reshape(chunk, nz))
        hall_faces[3, :, cols] = spread_of(m3.reshape(chunk, nz))
        s2 = gain * c2
        s3 = s2 * c2 - gain
        both = [s.reshape(chunk, nz).astype(BF16) for s in (s2, s3)]
        both = mm_nt(broad(respond_t), jnp.concatenate(both, axis=1))
        hall_resp[1, :, cols] = both[:48] + both[48:96]
        hall_resp[2, :, cols] = both[96:144] + both[144:]
        return carry

    copies[1].wait()
    copies[6].wait()
    lax.fori_loop(0, lanes // chunk, prepare_first, 0)
    diff = hall_get(0)
    hall_respond(0, 1, diff)
    hall_put(1)
    lax.fori_loop(0, lanes // chunk, prepare_last, 0)
    hall_respond(0, 2, diff)
    hall_respond(0, 3, diff)
    diff = hall_get(1)
    hall_respond(1, 1, diff)
    hall_put(2)
    hall_respond(1, 2, diff)

    q_cross = (lane // SZ).astype(F32) / SY
    q_cross = SCALE * (q_cross * q_cross)
    z_part = (lane % SZ).astype(F32) / SZ
    q_cross = q_cross + SCALE * (z_part * z_part)
    kx_f = kx.astype(F32)
    kx_sq = SCALE * (kx_f * kx_f)

    def room_second(b, carry):
        for i in range(4):
            r = 4 * b + i
            length = lengths[0, 0, r]
            which = jnp.maximum(length - SHORTEST, 0)
            at = pl.ds(pl.multiple_of(r * width, width), width)
            at8 = pl.ds(pl.multiple_of(r * 8, 8), 8)
            mine = lane // width == i
            raw_force[at8, :] = jnp.where(mine[:8], force_t[which], 0.0)
            extent = jnp.full((width, 128), length, jnp.int32)
            live = kx < extent
            extent = extent.astype(F32)
            c2, gain = factors(kx_sq / (extent * extent) + q_cross)
            room_c2[at, :] = c2
            room_gain[at, :] = gain
            room_b[at, :] = jnp.where(live, room_prev[at, :], 0.0)
        return carry

    copies[3].wait()
    copies[12].wait()
    copies[7].wait()
    lax.fori_loop(0, batches, room_second, 0)
    for b in range(batches):
        x = raw_force[32 * b : 32 * b + 32, :]
        high = x.astype(BF16).astype(F32)
        low = x - high
        force_l[128 * b : 128 * b + 128, :] = jnp.concatenate([high, high, low, low], axis=0).T.astype(BF16)
    take_col = jnp.broadcast_to(take_row, (8, wide)).T[:, 0:1]
    take_l[...] = jnp.where(iota((wide, slots), 1) == take_col, 1.0, 0.0).astype(BF16)

    diff = hall_get(2)
    hall_respond(2, 1, diff)
    hall_put(3)
    room_step(0)
    lax.fori_loop(0, lanes // chunk, accumulate_early, 0)
    hall_get(3)
    lax.fori_loop(0, lanes // chunk, accumulate_last, 0)

    parts = 2
    part_b = part_y // parts

    def a2a_copy(h, step):
        peer = lax.rem(column + step, slabs)
        return pltpu.make_async_remote_copy(
            src_ref=a2a_send.at[pl.ds(part_b * h, part_b), pl.ds(pl.multiple_of(peer * part_x, part_x), part_x), :],
            dst_ref=a2a_recv.at[pl.ds(column * part_y + part_b * h, part_b)],
            send_sem=a2a_ssem.at[h, step],
            recv_sem=a2a_rsem.at[h, step],
            device_id=(me, peer),
            device_id_type=MESH,
        )

    copies[8].wait()
    for h in range(parts):
        for b in range(part_b * h, part_b * h + part_b, 2):
            pair = [stacked(hall_base[:, b + i, :], 0) for i in range(2)]
            y = mm(broad(cosx_t), jnp.concatenate(pair, axis=1))
            a2a_send[b] = y[:, :nz]
            a2a_send[b + 1] = y[:, nz:]

        def a2a_start(i, carry):
            a2a_copy(h, far_first(i, slabs)).start()
            return carry

        lax.fori_loop(1, slabs, a2a_start, 0)

    def z_part_of(x):
        x = stacked(x.reshape(part_y * part_x, nz), 1)
        return mm(x, cosz_t[...]).reshape(part_y, part_x, nz)

    copies[10].wait()
    own = pl.ds(pl.multiple_of(column * part_x, part_x), part_x)
    a2a_recv[pl.ds(column * part_y, part_y)] = z_part_of(a2a_send[:, own, :])

    def a2a_take(i, carry):
        step = far_first(i, slabs)
        a2a_copy(0, step).wait_recv()
        a2a_copy(1, step).wait_recv()
        source = lax.rem(column + slabs - step, slabs)
        at = pl.ds(source * part_y, part_y)
        a2a_recv[at] = z_part_of(a2a_recv[at])
        return carry

    def room_tables_full(b, carry):
        for i in range(4):
            r = 4 * b + i
            which = jnp.maximum(lengths[0, 0, r] - SHORTEST, 0)
            at = pl.ds(pl.multiple_of(r * width, width), width)
            raw_full[at, :] = jnp.where(lane // width == i, room_t[which], 0.0)
        return carry

    copies[13].wait()
    copies[14].wait()
    lax.fori_loop(0, batches, room_tables_full, 0)
    for b in range(batches):
        big = slice(128 * b, 128 * b + 128)
        high, low = split(raw_full[big, :])
        full_l[big, :] = jnp.concatenate([high, high, low], axis=1)

    room_step(1)
    for t in range(STEPS - 1):
        hall_copy(t, 0).wait_send()
        hall_copy(t, 1).wait_send()
    room_step(2)
    hall_copy(3, 0).wait_send()
    hall_copy(3, 1).wait_send()
    lax.fori_loop(1, slabs, a2a_take, 0)
    copies[9].wait()
    for x in range(0, part_x, 2):
        pair = jnp.concatenate([stacked(a2a_recv[:, x, :], 0), stacked(a2a_recv[:, x + 1, :], 0)], axis=1)
        y = mm(broad(cosy_t), pair)
        hall_out[x] = y[:, :nz]
        hall_out[x + 1] = y[:, nz:]
    for i in range(8):
        store(0, i).start()

    room_step(3)
    room_sent(3)

    def a2a_sent(step, carry):
        a2a_copy(0, step).wait_send()
        a2a_copy(1, step).wait_send()
        return carry

    lax.fori_loop(1, slabs, a2a_sent, 0)
    for i in range(8):
        store(0, i).wait()
    for i in range(batches):
        store(1, i).wait()


def hand_on(hall_in, room_in, hall_out, room_out, sem):
    copies = []
    for j, (near, far) in enumerate(((hall_in, hall_out), (room_in, room_out))):
        size = near.shape[0] // 8
        for i in range(8):
            at = pl.ds(i * size, size)
            copies.append(pltpu.make_async_copy(near.at[at], far.at[at], sem.at[j, i]))
    for copy in copies:
        copy.start()
    for copy in copies:
        copy.wait()


def local(hall_now, hall_prev, room_now, room_prev, room_length, right_neighbor):
    groups = lax.axis_size("grp")
    slabs = lax.axis_size("slab")
    _, nx, part_y, nz = hall_now.shape
    _, _, count, width, cross = room_now.shape
    ny = part_y * slabs
    part_x = nx // slabs
    lanes = nx * part_y
    slots = 16 * groups
    rows = count * width
    inputs = [
        hall_now[0], hall_prev[0], room_now.reshape(rows, cross), room_prev.reshape(rows, cross), right_neighbor,
    ]
    inputs += [jnp.asarray(lane_tiles(t)) for t in hall_tables(nx, ny, nz)]
    inputs += [jnp.asarray(t) for t in room_tables(width)]
    inputs += [jnp.asarray(right_table(np.kron(dct(SY), dct(SZ))))]
    smem = pl.BlockSpec(memory_space=pltpu.SMEM)
    away = pl.BlockSpec(memory_space=pl.ANY)
    dma = pltpu.SemaphoreType.DMA
    results = pl.pallas_call(
        functools.partial(kernel, groups, slabs, count, len(inputs)),
        out_shape=(
            jax.ShapeDtypeStruct((part_x, ny, nz), F32),
            jax.ShapeDtypeStruct((rows, cross), F32),
        ),
        in_specs=[smem] + [away] * len(inputs),
        out_specs=(away, away),
        scratch_shapes=[pltpu.VMEM(x.shape, x.dtype) for x in inputs]
        + [
            pltpu.VMEM((nx, part_y, nz), F32),
            pltpu.VMEM((nx, part_y, nz), F32),
            pltpu.VMEM((nx, part_y, nz), F32),
            pltpu.VMEM((STEPS, 8, lanes), F32),
            pltpu.VMEM((STEPS - 1, 48, lanes), F32),
            pltpu.VMEM((STEPS, 8, lanes), F32),
            pltpu.VMEM((8, lanes), F32),
            pltpu.VMEM((STEPS, 2, 3, lanes // 128, 128), F32),
            pltpu.VMEM((STEPS, 2, 3, lanes // 128, 128), F32),
            pltpu.VMEM((part_y, nx, nz), F32),
            pltpu.VMEM((ny, part_x, nz), F32),
            pltpu.VMEM((rows, cross), F32),
            pltpu.VMEM((rows, cross), F32),
            pltpu.VMEM((rows, cross), F32),
            pltpu.VMEM((rows, cross), F32),
            pltpu.VMEM((8 * count, cross), F32),
            pltpu.VMEM((8 * count, 4 * width), F32),
            pltpu.VMEM((8 * count, 4 * width), F32),
            pltpu.VMEM((rows, 4 * width), F32),
            pltpu.VMEM((8 * count, 12 * width), BF16),
            pltpu.VMEM((rows, 128), BF16),
            pltpu.VMEM((rows, 12 * width), BF16),
            pltpu.VMEM((slots, 8 * count), BF16),
            pltpu.VMEM((8 * count, slots), BF16),
            pltpu.VMEM((STEPS, groups, 12, 128), F32),
            pltpu.VMEM((STEPS, groups - 1, 12, 128), F32),
            pltpu.VMEM((part_x, ny, nz), F32),
            pltpu.VMEM((rows, cross), F32),
            dma((len(inputs),)),
            dma((2, 8)),
            dma((STEPS, 2)),
            dma((STEPS, 2)),
            dma((2, slabs)),
            dma((2, slabs)),
            dma((STEPS, groups - 1)),
            dma((STEPS, groups - 1)),
        ],
        compiler_params=pltpu.CompilerParams(
            collective_id=0, has_side_effects=True, vmem_limit_bytes=60 * 1024 * 1024
        ),
    )(room_length, *inputs)
    hall_pressure, room_pressure = pl.pallas_call(
        hand_on,
        out_shape=tuple(jax.ShapeDtypeStruct(x.shape, x.dtype) for x in results),
        in_specs=[away] * 2,
        out_specs=(away, away),
        scratch_shapes=[dma((2, 8))],
        compiler_params=pltpu.CompilerParams(vmem_limit_bytes=60 * 1024 * 1024),
    )(*results)
    return (hall_pressure[None], room_pressure.reshape(1, 1, count, width, cross))


def solution(mesh):
    in_specs = (
        P("grp", None, "slab", None),
        P("grp", None, "slab", None),
        P("grp", "slab", None, None, None),
        P("grp", "slab", None, None, None),
        P("grp", "slab", None),
        P("slab", None),
    )
    out_specs = (P("grp", "slab", None, None), P("grp", "slab", None, None, None))
    return jax.shard_map(local, mesh=mesh, in_specs=in_specs, out_specs=out_specs, check_vma=False)
```

```python
import functools
import math

import jax
import jax.numpy as jnp
import ml_dtypes
import numpy as np
from jax import lax
from jax.experimental import pallas as pl
from jax.experimental.pallas import tpu as pltpu
from jax.sharding import PartitionSpec as P

SY = 8
SZ = 16
STEPS = 4
SHORTEST = 16
TIME_STEP = 0.4
SCALE = (TIME_STEP * math.pi) ** 2
STENCIL = np.array([[270, -27, 2], [-27, 2, 0], [2, 0, 0]], np.float64) / 180.0
F32 = jnp.float32
BF16 = jnp.bfloat16
MESH = pl.DeviceIdType.MESH


def dct(length):
    k = np.arange(length)[:, None]
    i = np.arange(length)[None, :]
    w = np.where(k == 0, np.sqrt(1.0 / length), np.sqrt(2.0 / length))
    return w * np.cos(np.pi * k * (2 * i + 1) / (2 * length))


def halves(x):
    high = x.astype(np.float32).astype(ml_dtypes.bfloat16)
    low = (x - high.astype(np.float64)).astype(ml_dtypes.bfloat16)
    return high, low


def left_table(x):
    high, low = halves(x)
    return np.concatenate([high, high, low], axis=1)


def right_table(x):
    high, low = halves(x)
    return np.concatenate([high, high, low], axis=0)


def face_rows(table):
    length = table.shape[0]
    sign = np.where(np.arange(length) % 2 == 0, 1.0, -1.0)
    low = table[:, :3].T
    forced = STENCIL.T @ low
    zero = np.zeros((2, length))
    return (
        np.concatenate([low, low * sign, zero], axis=0),
        np.concatenate([forced, forced * sign, zero], axis=0),
    )


def hall_tables(nx, ny, nz):
    faces, forced = face_rows(dct(nz))
    high, low = halves(faces)
    spread = np.concatenate(
        [np.concatenate([high, high], axis=1), np.concatenate([low, 0 * low], axis=1)], axis=0
    )
    pairs = np.concatenate([forced[k : k + 1] * faces for k in range(6)], axis=0)
    both = np.concatenate(halves(pairs), axis=0)
    respond = np.concatenate(
        [np.concatenate([both, 0 * both], axis=1), np.concatenate([0 * both, both], axis=1)], axis=0
    )
    high, low = halves(forced)
    outer = np.concatenate([high, high, low, low], axis=0)
    blank = np.zeros((32, 384), ml_dtypes.bfloat16)
    outer = np.concatenate([np.concatenate([blank[:, : 128 * t], outer, blank[:, 128 * t :]], axis=1) for t in range(4)], axis=0)
    return spread, respond, outer, left_table(dct(nx).T), left_table(dct(ny).T), right_table(dct(nz))


def room_tables(width):
    faces, forced, full = [], [], []
    for length in range(SHORTEST, width + 1):
        table = np.zeros((width, width))
        table[:length, :length] = dct(length)
        low, high = face_rows(table[:, :])
        faces.append(np.tile(low, (1, 4)))
        forced.append(np.tile(high, (1, 4)))
        full.append(np.tile(table.T, (1, 4)))
    return [np.stack(t).astype(np.float32) for t in (faces, forced, full)]


def factors(q):
    h = jnp.full_like(q, 2.0 / math.factorial(16))
    for n in range(6, -1, -1):
        h = 2.0 / math.factorial(2 * n + 2) - h * q
    return 2.0 - q * h, (TIME_STEP * TIME_STEP) * h


def mm(a, b):
    return jnp.dot(a, b, preferred_element_type=F32)


def mm_nt(a, b):
    return lax.dot_general(a, b, (((1,), (1,)), ((), ())), preferred_element_type=F32)


def split(x):
    high = x.astype(BF16)
    return high, (x - high.astype(F32)).astype(BF16)


def stacked(x, axis):
    high, low = split(x)
    return jnp.concatenate([high, low, high], axis=axis)


def lane_tiles(table):
    if table.shape[1] == 128:
        return table
    tile = math.gcd(table.shape[1], 128)
    return table.reshape(table.shape[0], -1, tile).transpose(1, 0, 2)


def broad(ref, tiles=None, rows=None):
    tiles = ref.shape[0] if tiles is None else tiles
    return jnp.concatenate([ref[j, :rows] for j in range(tiles)], axis=1)


def iota(shape, dim):
    return lax.broadcasted_iota(jnp.int32, shape, dim).astype(F32)


def total(mask, values, axis):
    return jnp.sum(jnp.where(mask, values, 0.0), axis=axis, keepdims=True)


def kernel(
    groups, slabs, count, loads, *refs,
):
    lengths, sources, refs = refs[0], refs[1 : 1 + loads], refs[1 + loads :]
    hall_far, room_far = refs[:2]
    landed, refs = refs[2 : 2 + loads], refs[2 + loads :]
    (
        hall_now, hall_prev, room_now, room_prev, ids,
        spread_t, respond_t, outer_t, cosx_t, cosy_t, cosz_t, face_t, force_t, room_t, cross_t,
    ) = landed
    (
        hall_c2, hall_gain, hall_base, hall_faces, hall_resp, hall_diff, hall_other,
        hall_send, hall_recv, a2a_send, a2a_recv,
        room_c2, room_gain, room_a, room_b, room_faces, raw_faces, raw_force, raw_full,
        face_l, force_l, full_l, pack_l, take_l, room_send, room_recv, hall_out, room_out,
        load_sem, store_sem, hall_ssem, hall_rsem, a2a_ssem, a2a_rsem, room_ssem, room_rsem,
    ) = refs
    me = lax.axis_index("grp")
    column = lax.axis_index("slab")
    nx, part_y, nz = hall_now.shape
    ny = part_y * slabs
    part_x = nx // slabs
    lanes = nx * part_y
    width = room_now.shape[0] // count
    batches = count // 4

    copies = [pltpu.make_async_copy(sources[i], landed[i], load_sem.at[i]) for i in range(loads)]
    order = [0, 5, 2, 4, 11, 1, 6, 3, 12, 7, 13, 8, 10, 9, 14]
    for i in order:
        copies[i].start()

    barrier = pltpu.get_barrier_semaphore()

    def greet_grp(step, carry):
        pl.semaphore_signal(
            barrier, inc=1, device_id=(lax.rem(me + step, groups), column), device_id_type=MESH
        )
        return carry

    def greet_slab(step, carry):
        pl.semaphore_signal(
            barrier, inc=1, device_id=(me, lax.rem(column + step, slabs)), device_id_type=MESH
        )
        return carry

    lax.fori_loop(1, groups, greet_grp, 0)
    lax.fori_loop(1, slabs, greet_slab, 0)
    hall_other[...] = jnp.zeros_like(hall_other)

    chunk = 256
    deep = chunk // part_y

    def chunks(body, many):
        def several(i, carry):
            for j in range(many):
                body(i * many + j)
            return carry

        lax.fori_loop(0, lanes // chunk // many, several, 0)

    def spread_of(x):
        high, low = split(x)
        both = mm_nt(broad(spread_t), jnp.concatenate([high, low], axis=1))
        return both[:8] + both[8:]

    def first_faces(i):
        x = hall_now[pl.ds(i * deep, deep)].reshape(chunk, nz)
        hall_faces[0, :, pl.ds(pl.multiple_of(i * chunk, chunk), chunk)] = spread_of(x)

    copies[0].wait()
    copies[5].wait()
    chunks(first_faces, 4)

    def hall_copy(t, side):
        peer = lax.rem(me + (1 if side == 0 else groups - 1), groups)
        return pltpu.make_async_remote_copy(
            src_ref=hall_send.at[t, side],
            dst_ref=hall_recv.at[t, side],
            send_sem=hall_ssem.at[t, side],
            recv_sem=hall_rsem.at[t, side],
            device_id=(peer, column),
            device_id_type=MESH,
        )

    def hall_put(t):
        own = hall_faces[t]
        for k in range(3):
            for j in range(lanes // 128):
                cut = slice(128 * j, 128 * j + 128)
                hall_send[t, 0, k, j : j + 1, :] = own[3 + k : 4 + k, cut]
                hall_send[t, 1, k, j : j + 1, :] = own[k : k + 1, cut]
        hall_copy(t, 0).start()
        hall_copy(t, 1).start()

    def hall_get(t):
        hall_copy(t, 0).wait_recv()
        hall_copy(t, 1).wait_recv()
        for k in range(3):
            for j in range(lanes // 128):
                cut = slice(128 * j, 128 * j + 128)
                hall_other[k : k + 1, cut] = hall_recv[t, 0, k, j : j + 1, :]
                hall_other[3 + k : 4 + k, cut] = hall_recv[t, 1, k, j : j + 1, :]
        row = lax.broadcasted_iota(jnp.int32, (8, lanes), 0)
        first = jnp.where(me > 0, 0, 3)
        last = jnp.where(me < groups - 1, 6, 3)
        diff = jnp.where((row >= first) & (row < last), hall_other[...] - hall_faces[t], 0.0)
        hall_diff[t] = diff
        return diff

    def hall_respond(t, lag, diff):
        acc = hall_faces[t + lag]
        for k in range(6):
            acc = acc + hall_resp[lag - 1, 8 * k : 8 * k + 8, :] * diff[k : k + 1, :]
        hall_faces[t + lag] = acc

    def terms(e):
        high = e.astype(BF16).astype(F32)
        low = e - high
        return jnp.concatenate([high, low, high, low], axis=0)

    def accumulate_early(i):
        at = pl.ds(i * deep, deep)
        cols = pl.ds(pl.multiple_of(i * chunk, chunk), chunk)
        e = jnp.concatenate([terms(hall_diff[t, :, cols]) for t in range(3)], axis=0).T.astype(BF16)
        forced = mm(e, broad(outer_t, 3, 96))
        c2 = hall_c2[at]
        f0, f1, f2 = [forced[:, 128 * t : 128 * t + 128].reshape(deep, part_y, nz) for t in range(3)]
        square = c2 * c2
        weighted = c2 * ((square - 2.0) * f0 + f2) + (square - 1.0) * f1
        hall_base[at] = hall_base[at] + hall_gain[at] * weighted

    def accumulate_last(i):
        at = pl.ds(i * deep, deep)
        cols = pl.ds(pl.multiple_of(i * chunk, chunk), chunk)
        e = terms(hall_diff[3, :, cols]).T.astype(BF16)
        forced = mm(e, outer_t[0, :32]).reshape(deep, part_y, nz)
        hall_base[at] = hall_base[at] + hall_gain[at] * forced

    pl.semaphore_wait(barrier, groups + slabs - 2)
    hall_put(0)


    yz = lax.broadcasted_iota(jnp.int32, (part_y, nz), 0) + column * part_y
    ky_f = yz.astype(F32)
    kz_f = iota((part_y, nz), 1)
    q_yz = (SCALE / ny**2) * (ky_f * ky_f) + (SCALE / nz**2) * (kz_f * kz_f)

    def prepare_first(i):
        at = pl.ds(i * deep, deep)
        cols = pl.ds(pl.multiple_of(i * chunk, chunk), chunk)
        a = (lax.broadcasted_iota(jnp.int32, (deep, part_y, nz), 0) + i * deep).astype(F32)
        c2, gain = factors((SCALE / nx**2) * (a * a) + q_yz[None])
        hall_c2[at] = c2
        hall_gain[at] = gain
        fresh = c2 * hall_now[at] - hall_prev[at]
        hall_base[at] = fresh
        hall_faces[1, :, cols] = spread_of(fresh.reshape(chunk, nz))
        both = mm_nt(respond_t[0, :96], gain.reshape(chunk, nz).astype(BF16))
        hall_resp[0, :, cols] = both[:48] + both[48:]

    def prepare_second(i):
        at = pl.ds(i * deep, deep)
        cols = pl.ds(pl.multiple_of(i * chunk, chunk), chunk)
        c2 = hall_c2[at]
        gain = hall_gain[at]
        m2 = c2 * hall_base[at] - hall_now[at]
        hall_faces[2, :, cols] = spread_of(m2.reshape(chunk, nz))
        s2 = gain * c2
        s3 = s2 * c2 - gain
        both = [s.reshape(chunk, nz).astype(BF16) for s in (s2, s3)]
        both = mm_nt(broad(respond_t), jnp.concatenate(both, axis=1))
        hall_resp[1, :, cols] = both[:48] + both[48:96]
        hall_resp[2, :, cols] = both[96:144] + both[144:]

    def prepare_third(i):
        at = pl.ds(i * deep, deep)
        cols = pl.ds(pl.multiple_of(i * chunk, chunk), chunk)
        c2 = hall_c2[at]
        m1 = hall_base[at]
        m2 = c2 * m1 - hall_now[at]
        m3 = c2 * m2 - m1
        hall_base[at] = c2 * m3 - m2
        hall_faces[3, :, cols] = spread_of(m3.reshape(chunk, nz))

    copies[1].wait()
    copies[6].wait()
    chunks(prepare_first, 2)
    diff = hall_get(0)
    hall_respond(0, 1, diff)
    hall_put(1)
    chunks(prepare_second, 2)
    hall_respond(0, 2, diff)
    diff = hall_get(1)
    hall_respond(1, 1, diff)
    hall_put(2)
    chunks(prepare_third, 2)
    hall_respond(0, 3, hall_diff[0])
    hall_respond(1, 2, diff)

    lane = lax.broadcasted_iota(jnp.int32, (width, 128), 1)
    kx = lax.broadcasted_iota(jnp.int32, (width, 128), 0)

    def room_first(b, carry):
        for i in range(4):
            r = 4 * b + i
            length = lengths[0, 0, r]
            which = jnp.maximum(length - SHORTEST, 0)
            at = pl.ds(pl.multiple_of(r * width, width), width)
            at8 = pl.ds(pl.multiple_of(r * 8, 8), 8)
            mine = lane // width == i
            raw_faces[at8, :] = jnp.where(mine[:8], face_t[which], 0.0)
            room_a[at, :] = jnp.where(kx < jnp.full((width, 128), length, jnp.int32), room_now[at, :], 0.0)
        return carry

    copies[2].wait()
    copies[4].wait()
    copies[11].wait()
    lax.fori_loop(0, batches, room_first, 0)
    for b in range(batches):
        cut = slice(32 * b, 32 * b + 32)
        big = slice(128 * b, 128 * b + 128)
        high, low = split(raw_faces[cut, :])
        face_l[cut, :] = jnp.concatenate([high, high, low], axis=1)
        room_faces[cut, :] = mm(face_l[cut, :], stacked(room_a[big, :], 0))

    bits = int(math.log2(count))
    wide = 8 * count
    span = ids.shape[1]
    row_lanes = min(128, span)
    flat = jnp.concatenate(
        [ids[0:1, row_lanes * j : row_lanes * (j + 1)] for j in range(span // row_lanes)], axis=0
    )
    device = (flat >> bits).astype(F32)
    slot = (flat & (count - 1)).astype(F32)
    lane_i = lax.broadcasted_iota(jnp.int32, (count, wide), 1)
    p_col = iota((count, wide), 0)
    p_row = (lane_i >> 3).astype(F32)
    f_row = (lane_i & 7).astype(F32)
    expand = lax.broadcasted_iota(jnp.int32, (row_lanes, wide), 1) >> 3
    expand = jnp.where(expand == lax.broadcasted_iota(jnp.int32, (row_lanes, wide), 0), 1.0, 0.0)
    s_row = mm(device.astype(BF16), expand.astype(BF16))[0:1]
    s_col = device.T[:count, 0:1]
    same = s_col == s_row
    rank_row = total(same & (p_col < p_row), 1.0, 0)
    rank_col = total(same & (p_row < p_col) & (f_row == 0.0), 1.0, 1)
    home = me.astype(F32) - s_col
    home = jnp.where(home < 0.0, home + groups, home)
    per_row = row_lanes // count
    home = jnp.concatenate([home] * per_row, axis=0)
    shape = (row_lanes, span // row_lanes)
    group = per_row * lax.broadcasted_iota(jnp.int32, shape, 1)
    group = group + (lax.broadcasted_iota(jnp.int32, shape, 0) >> bits)
    landing = total(group.astype(F32) == home, slot.T, 1)
    landing = sum(landing[count * i : count * (i + 1)] for i in range(per_row))
    match = landing == p_row
    ls_row = total(match, jnp.broadcast_to(s_col, (count, wide)), 0)
    lr_row = total(match, jnp.broadcast_to(rank_col, (count, wide)), 0)

    def back(s):
        return jnp.where(s == 0.0, 0.0, groups - s)

    f = f_row[0:1]
    layer = jnp.where(f < 3.0, f, f - 3.0)
    pack_row = jnp.where(
        f < 3.0, 16.0 * back(ls_row) + 6.0 + 3.0 * lr_row + layer, 16.0 * s_row + 3.0 * rank_row + layer
    )
    take_row = jnp.where(
        f < 3.0, 16.0 * ls_row + 3.0 * lr_row + layer, 16.0 * back(s_row) + 6.0 + 3.0 * rank_row + layer
    )
    pack_row = jnp.where(f < 6.0, pack_row, -1.0)
    take_row = jnp.where(f < 6.0, take_row, -1.0)
    slots = 16 * groups
    pack_l[...] = jnp.where(iota((slots, wide), 0) == pack_row, 1.0, 0.0).astype(BF16)

    def room_copy(t, step):
        return pltpu.make_async_remote_copy(
            src_ref=room_send.at[t, step],
            dst_ref=room_recv.at[t, step - 1],
            send_sem=room_ssem.at[t, step - 1],
            recv_sem=room_rsem.at[t, step - 1],
            device_id=(lax.rem(me + step, groups), column),
            device_id_type=MESH,
        )

    def far_first(i, count):
        half = i // 2
        return count // 2 + jnp.where(lax.rem(i, 2) == 0, half, -half)

    def two_parts(x):
        return jnp.concatenate(split(x), axis=1)

    def room_put(t):
        packed = mm(pack_l[...], two_parts(room_faces[...]))
        packed = packed[:, :128] + packed[:, 128:]
        room_send[t] = packed.reshape(groups, 16, 128)[:, :12, :]

        def body(i, carry):
            room_copy(t, far_first(i, groups)).start()
            return carry

        lax.fori_loop(1, groups, body, 0)

    def store(which, i):
        near, far = ((hall_out, hall_far), (room_out, room_far))[which]
        size = near.shape[0] // (8 if which == 0 else batches)
        at = pl.ds(i * size, size)
        return pltpu.make_async_copy(near.at[at], far.at[at], store_sem.at[which, i])

    def room_get(t):
        def body(i, carry):
            room_copy(t, far_first(i, groups)).wait_recv()
            return carry

        lax.fori_loop(1, groups, body, 0)
        got = jnp.concatenate([room_send[t, 0:1], room_recv[t]], axis=0)
        got = jnp.concatenate([got, jnp.zeros((groups, 4, 128), F32)], axis=1).reshape(slots, 128)
        other = mm(take_l[...], two_parts(got))
        return other[:, :128] + other[:, 128:] - room_faces[...]

    def room_sent(t):
        def body(step, carry):
            room_copy(t, step).wait_send()
            return carry

        lax.fori_loop(1, groups, body, 0)

    def room_step(t):
        diff = room_get(t)
        now, prev = (room_a, room_b) if t % 2 == 0 else (room_b, room_a)
        for b in range(batches):
            cut = slice(32 * b, 32 * b + 32)
            big = slice(128 * b, 128 * b + 128)
            high, low = split(diff[cut])
            forced = mm(force_l[big, :], jnp.concatenate([high, low, high, low], axis=0))
            fresh = room_c2[big, :] * now[big, :] - prev[big, :] + room_gain[big, :] * forced
            if t < STEPS - 1:
                prev[big, :] = fresh
                room_faces[cut, :] = mm(face_l[cut, :], stacked(fresh, 0))
            else:
                x = mm(full_l[big, :], stacked(fresh, 0))
                room_out[big, :] = mm(stacked(x, 1), cross_t[...])
                store(1, b).start()
        if t < STEPS - 1:
            room_put(t + 1)
            room_sent(t)

    diff = hall_get(2)
    hall_respond(2, 1, diff)
    hall_put(3)
    room_put(0)
    copies[7].wait()
    chunks(accumulate_early, 2)
    hall_get(3)
    chunks(accumulate_last, 2)

    parts = 2
    part_b = part_y // parts

    def a2a_copy(h, step):
        peer = lax.rem(column + step, slabs)
        return pltpu.make_async_remote_copy(
            src_ref=a2a_send.at[pl.ds(part_b * h, part_b), pl.ds(pl.multiple_of(peer * part_x, part_x), part_x), :],
            dst_ref=a2a_recv.at[pl.ds(column * part_y + part_b * h, part_b)],
            send_sem=a2a_ssem.at[h, step],
            recv_sem=a2a_rsem.at[h, step],
            device_id=(me, peer),
            device_id_type=MESH,
        )

    copies[8].wait()
    for h in range(parts):
        for b in range(part_b * h, part_b * h + part_b, 2):
            pair = [stacked(hall_base[:, b + i, :], 0) for i in range(2)]
            y = mm(broad(cosx_t), jnp.concatenate(pair, axis=1))
            a2a_send[b] = y[:, :nz]
            a2a_send[b + 1] = y[:, nz:]

        def a2a_start(i, carry):
            a2a_copy(h, far_first(i, slabs)).start()
            return carry

        lax.fori_loop(1, slabs, a2a_start, 0)

    def z_part_of(x):
        x = stacked(x.reshape(part_y * part_x, nz), 1)
        return mm(x, cosz_t[...]).reshape(part_y, part_x, nz)

    copies[10].wait()
    own = pl.ds(pl.multiple_of(column * part_x, part_x), part_x)
    a2a_recv[pl.ds(column * part_y, part_y)] = z_part_of(a2a_send[:, own, :])

    def a2a_take(i, carry):
        step = far_first(i, slabs)
        a2a_copy(0, step).wait_recv()
        a2a_copy(1, step).wait_recv()
        source = lax.rem(column + slabs - step, slabs)
        at = pl.ds(source * part_y, part_y)
        a2a_recv[at] = z_part_of(a2a_recv[at])
        return carry

    def room_tables_full(b, carry):
        for i in range(4):
            r = 4 * b + i
            which = jnp.maximum(lengths[0, 0, r] - SHORTEST, 0)
            at = pl.ds(pl.multiple_of(r * width, width), width)
            raw_full[at, :] = jnp.where(lane // width == i, room_t[which], 0.0)
        return carry

    copies[13].wait()
    copies[14].wait()
    lax.fori_loop(0, batches, room_tables_full, 0)
    for b in range(batches):
        big = slice(128 * b, 128 * b + 128)
        high, low = split(raw_full[big, :])
        full_l[big, :] = jnp.concatenate([high, high, low], axis=1)

    q_cross = (lane // SZ).astype(F32) / SY
    q_cross = SCALE * (q_cross * q_cross)
    z_part = (lane % SZ).astype(F32) / SZ
    q_cross = q_cross + SCALE * (z_part * z_part)
    kx_f = kx.astype(F32)
    kx_sq = SCALE * (kx_f * kx_f)

    def room_second(b, carry):
        for i in range(4):
            r = 4 * b + i
            length = lengths[0, 0, r]
            which = jnp.maximum(length - SHORTEST, 0)
            at = pl.ds(pl.multiple_of(r * width, width), width)
            at8 = pl.ds(pl.multiple_of(r * 8, 8), 8)
            mine = lane // width == i
            raw_force[at8, :] = jnp.where(mine[:8], force_t[which], 0.0)
            extent = jnp.full((width, 128), length, jnp.int32)
            live = kx < extent
            extent = extent.astype(F32)
            c2, gain = factors(kx_sq / (extent * extent) + q_cross)
            room_c2[at, :] = c2
            room_gain[at, :] = gain
            room_b[at, :] = jnp.where(live, room_prev[at, :], 0.0)
        return carry

    copies[3].wait()
    copies[12].wait()
    lax.fori_loop(0, batches, room_second, 0)
    for b in range(batches):
        x = raw_force[32 * b : 32 * b + 32, :]
        high = x.astype(BF16).astype(F32)
        low = x - high
        force_l[128 * b : 128 * b + 128, :] = jnp.concatenate([high, high, low, low], axis=0).T.astype(BF16)
    take_col = jnp.broadcast_to(take_row, (8, wide)).T[:, 0:1]
    take_l[...] = jnp.where(iota((wide, slots), 1) == take_col, 1.0, 0.0).astype(BF16)

    room_step(0)
    room_step(1)
    for t in range(STEPS - 1):
        hall_copy(t, 0).wait_send()
        hall_copy(t, 1).wait_send()
    room_step(2)
    hall_copy(3, 0).wait_send()
    hall_copy(3, 1).wait_send()
    lax.fori_loop(1, slabs, a2a_take, 0)
    copies[9].wait()
    for x in range(0, part_x, 2):
        pair = jnp.concatenate([stacked(a2a_recv[:, x, :], 0), stacked(a2a_recv[:, x + 1, :], 0)], axis=1)
        y = mm(broad(cosy_t), pair)
        hall_out[x] = y[:, :nz]
        hall_out[x + 1] = y[:, nz:]
    for i in range(8):
        store(0, i).start()

    room_step(3)
    room_sent(3)

    def a2a_sent(step, carry):
        a2a_copy(0, step).wait_send()
        a2a_copy(1, step).wait_send()
        return carry

    lax.fori_loop(1, slabs, a2a_sent, 0)
    for i in range(8):
        store(0, i).wait()
    for i in range(batches):
        store(1, i).wait()


def hand_on(hall_in, room_in, hall_out, room_out, hall_mid, room_mid, load_sem, store_sem):
    loads, stores = [], []
    for j, (near, mid, far) in enumerate(((hall_in, hall_mid, hall_out), (room_in, room_mid, room_out))):
        size = near.shape[0] // 4
        for i in range(4):
            at = pl.ds(i * size, size)
            loads.append(pltpu.make_async_copy(near.at[at], mid.at[at], load_sem.at[j, i]))
            stores.append(pltpu.make_async_copy(mid.at[at], far.at[at], store_sem.at[j, i]))
    for load in loads:
        load.start()
    for load, store in zip(loads, stores):
        load.wait()
        store.start()
    for store in stores:
        store.wait()


def local(hall_now, hall_prev, room_now, room_prev, room_length, right_neighbor):
    groups = lax.axis_size("grp")
    slabs = lax.axis_size("slab")
    _, nx, part_y, nz = hall_now.shape
    _, _, count, width, cross = room_now.shape
    ny = part_y * slabs
    part_x = nx // slabs
    lanes = nx * part_y
    slots = 16 * groups
    rows = count * width
    inputs = [
        hall_now[0], hall_prev[0], room_now.reshape(rows, cross), room_prev.reshape(rows, cross), right_neighbor,
    ]
    inputs += [jnp.asarray(lane_tiles(t)) for t in hall_tables(nx, ny, nz)]
    inputs += [jnp.asarray(t) for t in room_tables(width)]
    inputs += [jnp.asarray(right_table(np.kron(dct(SY), dct(SZ))))]
    smem = pl.BlockSpec(memory_space=pltpu.SMEM)
    away = pl.BlockSpec(memory_space=pl.ANY)
    dma = pltpu.SemaphoreType.DMA
    results = pl.pallas_call(
        functools.partial(kernel, groups, slabs, count, len(inputs)),
        out_shape=(
            jax.ShapeDtypeStruct((part_x, ny, nz), F32),
            jax.ShapeDtypeStruct((rows, cross), F32),
        ),
        in_specs=[smem] + [away] * len(inputs),
        out_specs=(away, away),
        scratch_shapes=[pltpu.VMEM(x.shape, x.dtype) for x in inputs]
        + [
            pltpu.VMEM((nx, part_y, nz), F32),
            pltpu.VMEM((nx, part_y, nz), F32),
            pltpu.VMEM((nx, part_y, nz), F32),
            pltpu.VMEM((STEPS, 8, lanes), F32),
            pltpu.VMEM((STEPS - 1, 48, lanes), F32),
            pltpu.VMEM((STEPS, 8, lanes), F32),
            pltpu.VMEM((8, lanes), F32),
            pltpu.VMEM((STEPS, 2, 3, lanes // 128, 128), F32),
            pltpu.VMEM((STEPS, 2, 3, lanes // 128, 128), F32),
            pltpu.VMEM((part_y, nx, nz), F32),
            pltpu.VMEM((ny, part_x, nz), F32),
            pltpu.VMEM((rows, cross), F32),
            pltpu.VMEM((rows, cross), F32),
            pltpu.VMEM((rows, cross), F32),
            pltpu.VMEM((rows, cross), F32),
            pltpu.VMEM((8 * count, cross), F32),
            pltpu.VMEM((8 * count, 4 * width), F32),
            pltpu.VMEM((8 * count, 4 * width), F32),
            pltpu.VMEM((rows, 4 * width), F32),
            pltpu.VMEM((8 * count, 12 * width), BF16),
            pltpu.VMEM((rows, 128), BF16),
            pltpu.VMEM((rows, 12 * width), BF16),
            pltpu.VMEM((slots, 8 * count), BF16),
            pltpu.VMEM((8 * count, slots), BF16),
            pltpu.VMEM((STEPS, groups, 12, 128), F32),
            pltpu.VMEM((STEPS, groups - 1, 12, 128), F32),
            pltpu.VMEM((part_x, ny, nz), F32),
            pltpu.VMEM((rows, cross), F32),
            dma((len(inputs),)),
            dma((2, 8)),
            dma((STEPS, 2)),
            dma((STEPS, 2)),
            dma((2, slabs)),
            dma((2, slabs)),
            dma((STEPS, groups - 1)),
            dma((STEPS, groups - 1)),
        ],
        compiler_params=pltpu.CompilerParams(
            collective_id=0, has_side_effects=True, vmem_limit_bytes=60 * 1024 * 1024
        ),
    )(room_length, *inputs)
    hall_pressure, room_pressure = pl.pallas_call(
        hand_on,
        out_shape=tuple(jax.ShapeDtypeStruct(x.shape, x.dtype) for x in results),
        in_specs=[away] * 2,
        out_specs=(away, away),
        scratch_shapes=[pltpu.VMEM(x.shape, x.dtype) for x in results] + [dma((2, 4)), dma((2, 4))],
        compiler_params=pltpu.CompilerParams(vmem_limit_bytes=60 * 1024 * 1024),
    )(*results)
    return (hall_pressure[None], room_pressure.reshape(1, 1, count, width, cross))


def solution(mesh):
    in_specs = (
        P("grp", None, "slab", None),
        P("grp", None, "slab", None),
        P("grp", "slab", None, None, None),
        P("grp", "slab", None, None, None),
        P("grp", "slab", None),
        P("slab", None),
    )
    out_specs = (P("grp", "slab", None, None), P("grp", "slab", None, None, None))
    return jax.shard_map(local, mesh=mesh, in_specs=in_specs, out_specs=out_specs, check_vma=False)
```

```python
import functools
import math

import jax
import jax.numpy as jnp
import ml_dtypes
import numpy as np
from jax import lax
from jax.experimental import pallas as pl
from jax.experimental.pallas import tpu as pltpu
from jax.sharding import PartitionSpec as P

SY = 8
SZ = 16
STEPS = 4
SHORTEST = 16
TIME_STEP = 0.4
SCALE = (TIME_STEP * math.pi) ** 2
STENCIL = np.array([[270, -27, 2], [-27, 2, 0], [2, 0, 0]], np.float64) / 180.0
F32 = jnp.float32
BF16 = jnp.bfloat16
MESH = pl.DeviceIdType.MESH


def dct(length):
    k = np.arange(length)[:, None]
    i = np.arange(length)[None, :]
    w = np.where(k == 0, np.sqrt(1.0 / length), np.sqrt(2.0 / length))
    return w * np.cos(np.pi * k * (2 * i + 1) / (2 * length))


def halves(x):
    high = x.astype(np.float32).astype(ml_dtypes.bfloat16)
    low = (x - high.astype(np.float64)).astype(ml_dtypes.bfloat16)
    return high, low


def left_table(x):
    high, low = halves(x)
    return np.concatenate([high, high, low], axis=1)


def right_table(x):
    high, low = halves(x)
    return np.concatenate([high, high, low], axis=0)


def face_rows(table):
    length = table.shape[0]
    sign = np.where(np.arange(length) % 2 == 0, 1.0, -1.0)
    low = table[:, :3].T
    forced = STENCIL.T @ low
    zero = np.zeros((2, length))
    return (
        np.concatenate([low, low * sign, zero], axis=0),
        np.concatenate([forced, forced * sign, zero], axis=0),
    )


def hall_tables(nx, ny, nz):
    faces, forced = face_rows(dct(nz))
    high, low = halves(faces)
    spread = np.concatenate(
        [np.concatenate([high, high], axis=1), np.concatenate([low, 0 * low], axis=1)], axis=0
    )
    pairs = np.concatenate([forced[k : k + 1] * faces for k in range(6)], axis=0)
    both = np.concatenate(halves(pairs), axis=0)
    respond = np.concatenate(
        [np.concatenate([both, 0 * both], axis=1), np.concatenate([0 * both, both], axis=1)], axis=0
    )
    high, low = halves(forced)
    outer = np.concatenate([high, high, low, low], axis=0)
    blank = np.zeros((32, 384), ml_dtypes.bfloat16)
    outer = np.concatenate([np.concatenate([blank[:, : 128 * t], outer, blank[:, 128 * t :]], axis=1) for t in range(4)], axis=0)
    return spread, respond, outer, left_table(dct(nx).T), left_table(dct(ny).T), right_table(dct(nz))


def room_tables(width):
    faces, forced, full = [], [], []
    for length in range(SHORTEST, width + 1):
        table = np.zeros((width, width))
        table[:length, :length] = dct(length)
        low, high = face_rows(table[:, :])
        faces.append(np.tile(low, (1, 4)))
        forced.append(np.tile(high, (1, 4)))
        full.append(np.tile(table.T, (1, 4)))
    return [np.stack(t).astype(np.float32) for t in (faces, forced, full)]


def factors(q):
    h = jnp.full_like(q, 2.0 / math.factorial(16))
    for n in range(6, -1, -1):
        h = 2.0 / math.factorial(2 * n + 2) - h * q
    return 2.0 - q * h, (TIME_STEP * TIME_STEP) * h


def mm(a, b):
    return jnp.dot(a, b, preferred_element_type=F32)


def mm_nt(a, b):
    return lax.dot_general(a, b, (((1,), (1,)), ((), ())), preferred_element_type=F32)


def split(x):
    high = x.astype(BF16)
    return high, (x - high.astype(F32)).astype(BF16)


def stacked(x, axis):
    high, low = split(x)
    return jnp.concatenate([high, low, high], axis=axis)


def lane_tiles(table):
    if table.shape[1] == 128:
        return table
    tile = math.gcd(table.shape[1], 128)
    return table.reshape(table.shape[0], -1, tile).transpose(1, 0, 2)


def broad(ref, tiles=None, rows=None):
    tiles = ref.shape[0] if tiles is None else tiles
    return jnp.concatenate([ref[j, :rows] for j in range(tiles)], axis=1)


def iota(shape, dim):
    return lax.broadcasted_iota(jnp.int32, shape, dim).astype(F32)


def total(mask, values, axis):
    return jnp.sum(jnp.where(mask, values, 0.0), axis=axis, keepdims=True)


def kernel(
    groups, slabs, count, loads, *refs,
):
    lengths, sources, refs = refs[0], refs[1 : 1 + loads], refs[1 + loads :]
    hall_far, room_far = refs[:2]
    landed, refs = refs[2 : 2 + loads], refs[2 + loads :]
    (
        hall_now, hall_prev, room_now, room_prev, ids,
        spread_t, respond_t, outer_t, cosx_t, cosy_t, cosz_t, face_t, force_t, room_t, cross_t,
    ) = landed
    (
        hall_c2, hall_gain, hall_base, hall_faces, hall_resp, hall_diff, hall_other,
        hall_send, hall_recv, a2a_send, a2a_recv,
        room_c2, room_gain, room_a, room_b, room_faces, raw_faces, raw_force, raw_full,
        face_l, force_l, full_l, pack_l, take_l, room_send, room_recv, hall_out, room_out, relay,
        load_sem, store_sem, hall_ssem, hall_rsem, a2a_ssem, a2a_rsem, relay_sem, room_ssem, room_rsem,
    ) = refs
    me = lax.axis_index("grp")
    column = lax.axis_index("slab")
    nx, part_y, nz = hall_now.shape
    ny = part_y * slabs
    part_x = nx // slabs
    lanes = nx * part_y
    width = room_now.shape[0] // count
    batches = count // 4

    copies = [pltpu.make_async_copy(sources[i], landed[i], load_sem.at[i]) for i in range(loads)]
    order = [0, 5, 2, 4, 11, 1, 6, 3, 12, 7, 13, 8, 10, 9, 14]
    for i in order:
        copies[i].start()

    barrier = pltpu.get_barrier_semaphore()

    def greet_grp(step, carry):
        pl.semaphore_signal(
            barrier, inc=1, device_id=(lax.rem(me + step, groups), column), device_id_type=MESH
        )
        return carry

    def greet_slab(step, carry):
        pl.semaphore_signal(
            barrier, inc=1, device_id=(me, lax.rem(column + step, slabs)), device_id_type=MESH
        )
        return carry

    lax.fori_loop(1, groups, greet_grp, 0)
    lax.fori_loop(1, slabs, greet_slab, 0)
    hall_other[...] = jnp.zeros_like(hall_other)

    chunk = 256
    deep = chunk // part_y

    def chunks(body, many):
        def several(i, carry):
            for j in range(many):
                body(i * many + j)
            return carry

        lax.fori_loop(0, lanes // chunk // many, several, 0)

    def spread_of(x):
        high, low = split(x)
        both = mm_nt(broad(spread_t), jnp.concatenate([high, low], axis=1))
        return both[:8] + both[8:]

    def first_faces(i):
        x = hall_now[pl.ds(i * deep, deep)].reshape(chunk, nz)
        hall_faces[0, :, pl.ds(pl.multiple_of(i * chunk, chunk), chunk)] = spread_of(x)

    copies[0].wait()
    copies[5].wait()
    chunks(first_faces, 4)

    def hall_copy(t, side):
        peer = lax.rem(me + (1 if side == 0 else groups - 1), groups)
        return pltpu.make_async_remote_copy(
            src_ref=hall_send.at[t, side],
            dst_ref=hall_recv.at[t, side],
            send_sem=hall_ssem.at[t, side],
            recv_sem=hall_rsem.at[t, side],
            device_id=(peer, column),
            device_id_type=MESH,
        )

    def hall_put(t):
        own = hall_faces[t]
        for k in range(3):
            for j in range(lanes // 128):
                cut = slice(128 * j, 128 * j + 128)
                hall_send[t, 0, k, j : j + 1, :] = own[3 + k : 4 + k, cut]
                hall_send[t, 1, k, j : j + 1, :] = own[k : k + 1, cut]
        hall_copy(t, 0).start()
        hall_copy(t, 1).start()

    def hall_get(t):
        hall_copy(t, 0).wait_recv()
        hall_copy(t, 1).wait_recv()
        for k in range(3):
            for j in range(lanes // 128):
                cut = slice(128 * j, 128 * j + 128)
                hall_other[k : k + 1, cut] = hall_recv[t, 0, k, j : j + 1, :]
                hall_other[3 + k : 4 + k, cut] = hall_recv[t, 1, k, j : j + 1, :]
        row = lax.broadcasted_iota(jnp.int32, (8, lanes), 0)
        first = jnp.where(me > 0, 0, 3)
        last = jnp.where(me < groups - 1, 6, 3)
        diff = jnp.where((row >= first) & (row < last), hall_other[...] - hall_faces[t], 0.0)
        hall_diff[t] = diff
        return diff

    def hall_respond(t, lag, diff):
        acc = hall_faces[t + lag]
        for k in range(6):
            acc = acc + hall_resp[lag - 1, 8 * k : 8 * k + 8, :] * diff[k : k + 1, :]
        hall_faces[t + lag] = acc

    def terms(e):
        high = e.astype(BF16).astype(F32)
        low = e - high
        return jnp.concatenate([high, low, high, low], axis=0)

    def accumulate_early(i):
        at = pl.ds(i * deep, deep)
        cols = pl.ds(pl.multiple_of(i * chunk, chunk), chunk)
        e = jnp.concatenate([terms(hall_diff[t, :, cols]) for t in range(3)], axis=0).T.astype(BF16)
        forced = mm(e, broad(outer_t, 3, 96))
        c2 = hall_c2[at]
        f0, f1, f2 = [forced[:, 128 * t : 128 * t + 128].reshape(deep, part_y, nz) for t in range(3)]
        square = c2 * c2
        weighted = c2 * ((square - 2.0) * f0 + f2) + (square - 1.0) * f1
        hall_base[at] = hall_base[at] + hall_gain[at] * weighted

    def accumulate_last(i):
        at = pl.ds(i * deep, deep)
        cols = pl.ds(pl.multiple_of(i * chunk, chunk), chunk)
        e = terms(hall_diff[3, :, cols]).T.astype(BF16)
        forced = mm(e, outer_t[0, :32]).reshape(deep, part_y, nz)
        hall_base[at] = hall_base[at] + hall_gain[at] * forced

    pl.semaphore_wait(barrier, groups + slabs - 2)
    hall_put(0)


    lane = lax.broadcasted_iota(jnp.int32, (width, 128), 1)
    kx = lax.broadcasted_iota(jnp.int32, (width, 128), 0)

    def room_first(b, carry):
        for i in range(4):
            r = 4 * b + i
            length = lengths[0, 0, r]
            which = jnp.maximum(length - SHORTEST, 0)
            at = pl.ds(pl.multiple_of(r * width, width), width)
            at8 = pl.ds(pl.multiple_of(r * 8, 8), 8)
            mine = lane // width == i
            raw_faces[at8, :] = jnp.where(mine[:8], face_t[which], 0.0)
            room_a[at, :] = jnp.where(kx < jnp.full((width, 128), length, jnp.int32), room_now[at, :], 0.0)
        return carry

    copies[2].wait()
    copies[4].wait()
    copies[11].wait()
    lax.fori_loop(0, batches, room_first, 0)
    for b in range(batches):
        cut = slice(32 * b, 32 * b + 32)
        big = slice(128 * b, 128 * b + 128)
        high, low = split(raw_faces[cut, :])
        face_l[cut, :] = jnp.concatenate([high, high, low], axis=1)
        room_faces[cut, :] = mm(face_l[cut, :], stacked(room_a[big, :], 0))

    bits = int(math.log2(count))
    wide = 8 * count
    span = ids.shape[1]
    row_lanes = min(128, span)
    flat = jnp.concatenate(
        [ids[0:1, row_lanes * j : row_lanes * (j + 1)] for j in range(span // row_lanes)], axis=0
    )
    device = (flat >> bits).astype(F32)
    slot = (flat & (count - 1)).astype(F32)
    lane_i = lax.broadcasted_iota(jnp.int32, (count, wide), 1)
    p_col = iota((count, wide), 0)
    p_row = (lane_i >> 3).astype(F32)
    f_row = (lane_i & 7).astype(F32)
    expand = lax.broadcasted_iota(jnp.int32, (row_lanes, wide), 1) >> 3
    expand = jnp.where(expand == lax.broadcasted_iota(jnp.int32, (row_lanes, wide), 0), 1.0, 0.0)
    s_row = mm(device.astype(BF16), expand.astype(BF16))[0:1]
    s_col = device.T[:count, 0:1]
    same = s_col == s_row
    rank_row = total(same & (p_col < p_row), 1.0, 0)
    rank_col = total(same & (p_row < p_col) & (f_row == 0.0), 1.0, 1)
    home = me.astype(F32) - s_col
    home = jnp.where(home < 0.0, home + groups, home)
    per_row = row_lanes // count
    home = jnp.concatenate([home] * per_row, axis=0)
    shape = (row_lanes, span // row_lanes)
    group = per_row * lax.broadcasted_iota(jnp.int32, shape, 1)
    group = group + (lax.broadcasted_iota(jnp.int32, shape, 0) >> bits)
    landing = total(group.astype(F32) == home, slot.T, 1)
    landing = sum(landing[count * i : count * (i + 1)] for i in range(per_row))
    match = landing == p_row
    ls_row = total(match, jnp.broadcast_to(s_col, (count, wide)), 0)
    lr_row = total(match, jnp.broadcast_to(rank_col, (count, wide)), 0)

    def back(s):
        return jnp.where(s == 0.0, 0.0, groups - s)

    f = f_row[0:1]
    layer = jnp.where(f < 3.0, f, f - 3.0)
    pack_row = jnp.where(
        f < 3.0, 16.0 * back(ls_row) + 6.0 + 3.0 * lr_row + layer, 16.0 * s_row + 3.0 * rank_row + layer
    )
    take_row = jnp.where(
        f < 3.0, 16.0 * ls_row + 3.0 * lr_row + layer, 16.0 * back(s_row) + 6.0 + 3.0 * rank_row + layer
    )
    pack_row = jnp.where(f < 6.0, pack_row, -1.0)
    take_row = jnp.where(f < 6.0, take_row, -1.0)
    slots = 16 * groups
    pack_l[...] = jnp.where(iota((slots, wide), 0) == pack_row, 1.0, 0.0).astype(BF16)

    def room_copy(t, step):
        return pltpu.make_async_remote_copy(
            src_ref=room_send.at[t, step],
            dst_ref=room_recv.at[t, step - 1],
            send_sem=room_ssem.at[t],
            recv_sem=room_rsem.at[t],
            device_id=(lax.rem(me + step, groups), column),
            device_id_type=MESH,
        )

    def room_all(t):
        return pltpu.make_async_remote_copy(
            src_ref=room_send.at[t, pl.ds(1, groups - 1)],
            dst_ref=room_recv.at[t],
            send_sem=room_ssem.at[t],
            recv_sem=room_rsem.at[t],
            device_id=(lax.rem(me + 1, groups), column),
            device_id_type=MESH,
        )

    def far_first(i, count):
        half = i // 2
        return count // 2 + jnp.where(lax.rem(i, 2) == 0, half, -half)

    def two_parts(x):
        return jnp.concatenate(split(x), axis=1)

    def room_put(t):
        packed = mm(pack_l[...], two_parts(room_faces[...]))
        packed = packed[:, :128] + packed[:, 128:]
        room_send[t] = packed.reshape(groups, 16, 128)[:, :12, :]

        def body(i, carry):
            room_copy(t, far_first(i, groups)).start()
            return carry

        lax.fori_loop(1, groups, body, 0)

    def store(which, i):
        near, far = ((hall_out, hall_far), (room_out, room_far))[which]
        size = near.shape[0] // (8 if which == 0 else batches)
        at = pl.ds(i * size, size)
        return pltpu.make_async_copy(near.at[at], far.at[at], store_sem.at[which, i])

    def room_get(t):
        room_all(t).wait_recv()
        got = jnp.concatenate([room_send[t, 0:1], room_recv[t]], axis=0)
        got = jnp.concatenate([got, jnp.zeros((groups, 4, 128), F32)], axis=1).reshape(slots, 128)
        other = mm(take_l[...], two_parts(got))
        return other[:, :128] + other[:, 128:] - room_faces[...]

    def room_sent(t):
        room_all(t).wait_send()

    def room_step(t):
        diff = room_get(t)
        now, prev = (room_a, room_b) if t % 2 == 0 else (room_b, room_a)
        for b in range(batches):
            cut = slice(32 * b, 32 * b + 32)
            big = slice(128 * b, 128 * b + 128)
            high, low = split(diff[cut])
            forced = mm(force_l[big, :], jnp.concatenate([high, low, high, low], axis=0))
            fresh = room_c2[big, :] * now[big, :] - prev[big, :] + room_gain[big, :] * forced
            if t < STEPS - 1:
                prev[big, :] = fresh
                room_faces[cut, :] = mm(face_l[cut, :], stacked(fresh, 0))
            else:
                x = mm(full_l[big, :], stacked(fresh, 0))
                room_out[big, :] = mm(stacked(x, 1), cross_t[...])
                store(1, b).start()
        if t < STEPS - 1:
            room_put(t + 1)
            room_sent(t)

    room_put(0)

    yz = lax.broadcasted_iota(jnp.int32, (part_y, nz), 0) + column * part_y
    ky_f = yz.astype(F32)
    kz_f = iota((part_y, nz), 1)
    q_yz = (SCALE / ny**2) * (ky_f * ky_f) + (SCALE / nz**2) * (kz_f * kz_f)

    def prepare_first(i):
        at = pl.ds(i * deep, deep)
        cols = pl.ds(pl.multiple_of(i * chunk, chunk), chunk)
        a = (lax.broadcasted_iota(jnp.int32, (deep, part_y, nz), 0) + i * deep).astype(F32)
        c2, gain = factors((SCALE / nx**2) * (a * a) + q_yz[None])
        hall_c2[at] = c2
        hall_gain[at] = gain
        fresh = c2 * hall_now[at] - hall_prev[at]
        hall_base[at] = fresh
        hall_faces[1, :, cols] = spread_of(fresh.reshape(chunk, nz))
        both = mm_nt(respond_t[0, :96], gain.reshape(chunk, nz).astype(BF16))
        hall_resp[0, :, cols] = both[:48] + both[48:]

    def prepare_second(i):
        at = pl.ds(i * deep, deep)
        cols = pl.ds(pl.multiple_of(i * chunk, chunk), chunk)
        c2 = hall_c2[at]
        gain = hall_gain[at]
        m2 = c2 * hall_base[at] - hall_now[at]
        hall_faces[2, :, cols] = spread_of(m2.reshape(chunk, nz))
        s2 = gain * c2
        s3 = s2 * c2 - gain
        both = [s.reshape(chunk, nz).astype(BF16) for s in (s2, s3)]
        both = mm_nt(broad(respond_t), jnp.concatenate(both, axis=1))
        hall_resp[1, :, cols] = both[:48] + both[48:96]
        hall_resp[2, :, cols] = both[96:144] + both[144:]

    def prepare_third(i):
        at = pl.ds(i * deep, deep)
        cols = pl.ds(pl.multiple_of(i * chunk, chunk), chunk)
        c2 = hall_c2[at]
        m1 = hall_base[at]
        m2 = c2 * m1 - hall_now[at]
        m3 = c2 * m2 - m1
        hall_base[at] = c2 * m3 - m2
        hall_faces[3, :, cols] = spread_of(m3.reshape(chunk, nz))

    copies[1].wait()
    copies[6].wait()
    chunks(prepare_first, 2)
    diff = hall_get(0)
    hall_respond(0, 1, diff)
    hall_put(1)
    chunks(prepare_second, 2)
    hall_respond(0, 2, diff)
    diff = hall_get(1)
    hall_respond(1, 1, diff)
    hall_put(2)
    chunks(prepare_third, 2)
    hall_respond(0, 3, hall_diff[0])
    hall_respond(1, 2, diff)

    diff = hall_get(2)
    hall_respond(2, 1, diff)
    hall_put(3)
    copies[7].wait()
    chunks(accumulate_early, 2)
    hall_get(3)
    chunks(accumulate_last, 2)

    parts = 2
    part_b = part_y // parts

    ring = slabs // 2
    chip = column // 2
    core = lax.rem(column, 2)
    relayed = ring == 8

    def column_of(hops, k):
        return 2 * lax.rem(chip + hops + ring, ring) + k

    def a2a_copy(h, hops, k, source_core):
        peer = column_of(hops, k)
        return pltpu.make_async_remote_copy(
            src_ref=a2a_send.at[pl.ds(part_b * h, part_b), pl.ds(pl.multiple_of(peer * part_x, part_x), part_x), :],
            dst_ref=a2a_recv.at[pl.ds(column * part_y + part_b * h, part_b)],
            send_sem=a2a_ssem.at[h, 2 * hops + k],
            recv_sem=a2a_rsem.at[h, 2 * hops + source_core],
            device_id=(me, peer),
            device_id_type=MESH,
        )

    def relay_copy(h):
        far = pl.multiple_of(column_of(ring // 2, 0) * part_x, 2 * part_x)
        return pltpu.make_async_remote_copy(
            src_ref=a2a_send.at[pl.ds(part_b * h, part_b), pl.ds(far, 2 * part_x), :],
            dst_ref=relay.at[h],
            send_sem=relay_sem.at[h, 0],
            recv_sem=relay_sem.at[h, 1],
            device_id=(me, column_of(1 - 2 * h, core)),
            device_id_type=MESH,
        )

    def forward_copy(h, k):
        way = 1 - 2 * h
        source = column_of(-way, core)
        return pltpu.make_async_remote_copy(
            src_ref=relay.at[h, :, pl.ds(k * part_x, part_x), :],
            dst_ref=a2a_recv.at[pl.ds(source * part_y + part_b * h, part_b)],
            send_sem=relay_sem.at[h, 2 + k],
            recv_sem=a2a_rsem.at[h, ring + core],
            device_id=(me, column_of(3 * way, k)),
            device_id_type=MESH,
        )

    first_hop = 2 if relayed else 1

    copies[8].wait()
    for h in range(parts):
        for b in range(part_b * h, part_b * h + part_b, 2):
            pair = [stacked(hall_base[:, b + i, :], 0) for i in range(2)]
            y = mm(broad(cosx_t), jnp.concatenate(pair, axis=1))
            a2a_send[b] = y[:, :nz]
            a2a_send[b + 1] = y[:, nz:]

        if relayed:
            relay_copy(h).start()

        def a2a_start(i, carry):
            a2a_copy(h, far_first(i // 2, ring), lax.rem(i, 2), core).start()
            return carry

        lax.fori_loop(2 * first_hop, 2 * ring, a2a_start, 0)
        a2a_copy(h, 0, 1 - core, core).start()

    def z_part_of(x):
        x = stacked(x.reshape(part_y * part_x, nz), 1)
        return mm(x, cosz_t[...]).reshape(part_y, part_x, nz)

    copies[10].wait()
    own = pl.ds(pl.multiple_of(column * part_x, part_x), part_x)
    a2a_recv[pl.ds(column * part_y, part_y)] = z_part_of(a2a_send[:, own, :])

    def take_from(hops, k):
        a2a_copy(0, hops, k, k).wait_recv()
        a2a_copy(1, hops, k, k).wait_recv()
        at = pl.ds(column_of(-hops, k) * part_y, part_y)
        a2a_recv[at] = z_part_of(a2a_recv[at])

    def a2a_take(i, carry):
        i = 2 * ring + 2 * first_hop - 1 - i
        take_from(far_first(i // 2, ring), lax.rem(i, 2))
        return carry

    def room_tables_full(b, carry):
        for i in range(4):
            r = 4 * b + i
            which = jnp.maximum(lengths[0, 0, r] - SHORTEST, 0)
            at = pl.ds(pl.multiple_of(r * width, width), width)
            raw_full[at, :] = jnp.where(lane // width == i, room_t[which], 0.0)
        return carry

    copies[13].wait()
    copies[14].wait()
    lax.fori_loop(0, batches, room_tables_full, 0)
    for b in range(batches):
        big = slice(128 * b, 128 * b + 128)
        high, low = split(raw_full[big, :])
        full_l[big, :] = jnp.concatenate([high, high, low], axis=1)

    q_cross = (lane // SZ).astype(F32) / SY
    q_cross = SCALE * (q_cross * q_cross)
    z_part = (lane % SZ).astype(F32) / SZ
    q_cross = q_cross + SCALE * (z_part * z_part)
    kx_f = kx.astype(F32)
    kx_sq = SCALE * (kx_f * kx_f)

    def room_second(b, carry):
        for i in range(4):
            r = 4 * b + i
            length = lengths[0, 0, r]
            which = jnp.maximum(length - SHORTEST, 0)
            at = pl.ds(pl.multiple_of(r * width, width), width)
            at8 = pl.ds(pl.multiple_of(r * 8, 8), 8)
            mine = lane // width == i
            raw_force[at8, :] = jnp.where(mine[:8], force_t[which], 0.0)
            extent = jnp.full((width, 128), length, jnp.int32)
            live = kx < extent
            extent = extent.astype(F32)
            c2, gain = factors(kx_sq / (extent * extent) + q_cross)
            room_c2[at, :] = c2
            room_gain[at, :] = gain
            room_b[at, :] = jnp.where(live, room_prev[at, :], 0.0)
        return carry

    copies[3].wait()
    copies[12].wait()
    lax.fori_loop(0, batches, room_second, 0)
    for b in range(batches):
        x = raw_force[32 * b : 32 * b + 32, :]
        high = x.astype(BF16).astype(F32)
        low = x - high
        force_l[128 * b : 128 * b + 128, :] = jnp.concatenate([high, high, low, low], axis=0).T.astype(BF16)
    take_col = jnp.broadcast_to(take_row, (8, wide)).T[:, 0:1]
    take_l[...] = jnp.where(iota((wide, slots), 1) == take_col, 1.0, 0.0).astype(BF16)

    if relayed:
        for h in range(parts):
            relay_copy(h).wait_recv()
            forward_copy(h, 0).start()
            forward_copy(h, 1).start()
    room_step(0)
    room_step(1)
    for t in range(STEPS - 1):
        hall_copy(t, 0).wait_send()
        hall_copy(t, 1).wait_send()
    room_step(2)
    hall_copy(3, 0).wait_send()
    hall_copy(3, 1).wait_send()
    take_from(0, 1 - core)
    lax.fori_loop(2 * first_hop, 2 * ring, a2a_take, 0)
    if relayed:
        take_from(ring // 2, 0)
        take_from(ring // 2, 1)
    copies[9].wait()
    for x in range(0, part_x, 2):
        pair = jnp.concatenate([stacked(a2a_recv[:, x, :], 0), stacked(a2a_recv[:, x + 1, :], 0)], axis=1)
        y = mm(broad(cosy_t), pair)
        hall_out[x] = y[:, :nz]
        hall_out[x + 1] = y[:, nz:]
    for i in range(8):
        store(0, i).start()

    room_step(3)
    room_sent(3)

    for h in range(parts):

        def a2a_sent(i, carry):
            a2a_copy(h, far_first(i // 2, ring), lax.rem(i, 2), core).wait_send()
            return carry

        lax.fori_loop(2 * first_hop, 2 * ring, a2a_sent, 0)
        a2a_copy(h, 0, 1 - core, core).wait_send()
        if relayed:
            relay_copy(h).wait_send()
            forward_copy(h, 0).wait_send()
            forward_copy(h, 1).wait_send()

    for i in range(8):
        store(0, i).wait()
    for i in range(batches):
        store(1, i).wait()


def hand_on(hall_in, room_in, hall_out, room_out, hall_mid, room_mid, load_sem, store_sem):
    loads, stores = [], []
    for j, (near, mid, far) in enumerate(((hall_in, hall_mid, hall_out), (room_in, room_mid, room_out))):
        size = near.shape[0] // 4
        for i in range(4):
            at = pl.ds(i * size, size)
            loads.append(pltpu.make_async_copy(near.at[at], mid.at[at], load_sem.at[j, i]))
            stores.append(pltpu.make_async_copy(mid.at[at], far.at[at], store_sem.at[j, i]))
    for load in loads:
        load.start()
    for load, store in zip(loads, stores):
        load.wait()
        store.start()
    for store in stores:
        store.wait()


def local(hall_now, hall_prev, room_now, room_prev, room_length, right_neighbor):
    groups = lax.axis_size("grp")
    slabs = lax.axis_size("slab")
    _, nx, part_y, nz = hall_now.shape
    _, _, count, width, cross = room_now.shape
    ny = part_y * slabs
    part_x = nx // slabs
    lanes = nx * part_y
    slots = 16 * groups
    rows = count * width
    inputs = [
        hall_now[0], hall_prev[0], room_now.reshape(rows, cross), room_prev.reshape(rows, cross), right_neighbor,
    ]
    inputs += [jnp.asarray(lane_tiles(t)) for t in hall_tables(nx, ny, nz)]
    inputs += [jnp.asarray(t) for t in room_tables(width)]
    inputs += [jnp.asarray(right_table(np.kron(dct(SY), dct(SZ))))]
    smem = pl.BlockSpec(memory_space=pltpu.SMEM)
    away = pl.BlockSpec(memory_space=pl.ANY)
    dma = pltpu.SemaphoreType.DMA
    results = pl.pallas_call(
        functools.partial(kernel, groups, slabs, count, len(inputs)),
        out_shape=(
            jax.ShapeDtypeStruct((part_x, ny, nz), F32),
            jax.ShapeDtypeStruct((rows, cross), F32),
        ),
        in_specs=[smem] + [away] * len(inputs),
        out_specs=(away, away),
        scratch_shapes=[pltpu.VMEM(x.shape, x.dtype) for x in inputs]
        + [
            pltpu.VMEM((nx, part_y, nz), F32),
            pltpu.VMEM((nx, part_y, nz), F32),
            pltpu.VMEM((nx, part_y, nz), F32),
            pltpu.VMEM((STEPS, 8, lanes), F32),
            pltpu.VMEM((STEPS - 1, 48, lanes), F32),
            pltpu.VMEM((STEPS, 8, lanes), F32),
            pltpu.VMEM((8, lanes), F32),
            pltpu.VMEM((STEPS, 2, 3, lanes // 128, 128), F32),
            pltpu.VMEM((STEPS, 2, 3, lanes // 128, 128), F32),
            pltpu.VMEM((part_y, nx, nz), F32),
            pltpu.VMEM((ny, part_x, nz), F32),
            pltpu.VMEM((rows, cross), F32),
            pltpu.VMEM((rows, cross), F32),
            pltpu.VMEM((rows, cross), F32),
            pltpu.VMEM((rows, cross), F32),
            pltpu.VMEM((8 * count, cross), F32),
            pltpu.VMEM((8 * count, 4 * width), F32),
            pltpu.VMEM((8 * count, 4 * width), F32),
            pltpu.VMEM((rows, 4 * width), F32),
            pltpu.VMEM((8 * count, 12 * width), BF16),
            pltpu.VMEM((rows, 128), BF16),
            pltpu.VMEM((rows, 12 * width), BF16),
            pltpu.VMEM((slots, 8 * count), BF16),
            pltpu.VMEM((8 * count, slots), BF16),
            pltpu.VMEM((STEPS, groups, 12, 128), F32),
            pltpu.VMEM((STEPS, groups - 1, 12, 128), F32),
            pltpu.VMEM((part_x, ny, nz), F32),
            pltpu.VMEM((rows, cross), F32),
            pltpu.VMEM((2, part_y // 2, 2 * part_x, nz), F32),
            dma((len(inputs),)),
            dma((2, 8)),
            dma((STEPS, 2)),
            dma((STEPS, 2)),
            dma((2, slabs)),
            dma((2, slabs)),
            dma((2, 4)),
            dma((STEPS,)),
            dma((STEPS,)),
        ],
        compiler_params=pltpu.CompilerParams(
            collective_id=0, has_side_effects=True, vmem_limit_bytes=60 * 1024 * 1024
        ),
    )(room_length, *inputs)
    hall_pressure, room_pressure = pl.pallas_call(
        hand_on,
        out_shape=tuple(jax.ShapeDtypeStruct(x.shape, x.dtype) for x in results),
        in_specs=[away] * 2,
        out_specs=(away, away),
        scratch_shapes=[pltpu.VMEM(x.shape, x.dtype) for x in results] + [dma((2, 4)), dma((2, 4))],
        compiler_params=pltpu.CompilerParams(vmem_limit_bytes=60 * 1024 * 1024),
    )(*results)
    return (hall_pressure[None], room_pressure.reshape(1, 1, count, width, cross))


def solution(mesh):
    in_specs = (
        P("grp", None, "slab", None),
        P("grp", None, "slab", None),
        P("grp", "slab", None, None, None),
        P("grp", "slab", None, None, None),
        P("grp", "slab", None),
        P("slab", None),
    )
    out_specs = (P("grp", "slab", None, None), P("grp", "slab", None, None, None))
    return jax.shard_map(local, mesh=mesh, in_specs=in_specs, out_specs=out_specs, check_vma=False)
```

```python
import functools
import math

import jax
import jax.numpy as jnp
import ml_dtypes
import numpy as np
from jax import lax
from jax.experimental import pallas as pl
from jax.experimental.pallas import tpu as pltpu
from jax.sharding import PartitionSpec as P

SY = 8
SZ = 16
STEPS = 4
SHORTEST = 16
TIME_STEP = 0.4
SCALE = (TIME_STEP * math.pi) ** 2
STENCIL = np.array([[270, -27, 2], [-27, 2, 0], [2, 0, 0]], np.float64) / 180.0
F32 = jnp.float32
BF16 = jnp.bfloat16
MESH = pl.DeviceIdType.MESH


def dct(length):
    k = np.arange(length)[:, None]
    i = np.arange(length)[None, :]
    w = np.where(k == 0, np.sqrt(1.0 / length), np.sqrt(2.0 / length))
    return w * np.cos(np.pi * k * (2 * i + 1) / (2 * length))


def halves(x):
    high = x.astype(np.float32).astype(ml_dtypes.bfloat16)
    low = (x - high.astype(np.float64)).astype(ml_dtypes.bfloat16)
    return high, low


def left_table(x):
    high, low = halves(x)
    return np.concatenate([high, high, low], axis=1)


def right_table(x):
    high, low = halves(x)
    return np.concatenate([high, high, low], axis=0)


def face_rows(table):
    length = table.shape[0]
    sign = np.where(np.arange(length) % 2 == 0, 1.0, -1.0)
    low = table[:, :3].T
    forced = STENCIL.T @ low
    zero = np.zeros((2, length))
    return (
        np.concatenate([low, low * sign, zero], axis=0),
        np.concatenate([forced, forced * sign, zero], axis=0),
    )


def hall_tables(nx, ny, nz):
    faces, forced = face_rows(dct(nz))
    high, low = halves(faces)
    spread = np.concatenate(
        [np.concatenate([high, high], axis=1), np.concatenate([low, 0 * low], axis=1)], axis=0
    )
    pairs = np.concatenate([forced[k : k + 1] * faces for k in range(6)], axis=0)
    both = np.concatenate(halves(pairs), axis=0)
    respond = np.concatenate(
        [np.concatenate([both, 0 * both], axis=1), np.concatenate([0 * both, both], axis=1)], axis=0
    )
    high, low = halves(forced)
    outer = np.concatenate([high, high, low, low], axis=0)
    blank = np.zeros((32, 384), ml_dtypes.bfloat16)
    outer = np.concatenate([np.concatenate([blank[:, : 128 * t], outer, blank[:, 128 * t :]], axis=1) for t in range(4)], axis=0)
    return spread, respond, outer, left_table(dct(nx).T), left_table(dct(ny).T), right_table(dct(nz))


def room_tables(width):
    faces, forced, full = [], [], []
    for length in range(SHORTEST, width + 1):
        table = np.zeros((width, width))
        table[:length, :length] = dct(length)
        low, high = face_rows(table[:, :])
        faces.append(np.tile(low, (1, 4)))
        forced.append(np.tile(high, (1, 4)))
        full.append(np.tile(table.T, (1, 4)))
    return [np.stack(t).astype(np.float32) for t in (faces, forced, full)]


def factors(q):
    h = jnp.full_like(q, 2.0 / math.factorial(16))
    for n in range(6, -1, -1):
        h = 2.0 / math.factorial(2 * n + 2) - h * q
    return 2.0 - q * h, (TIME_STEP * TIME_STEP) * h


def mm(a, b):
    return jnp.dot(a, b, preferred_element_type=F32)


def mm_nt(a, b):
    return lax.dot_general(a, b, (((1,), (1,)), ((), ())), preferred_element_type=F32)


def split(x):
    high = x.astype(BF16)
    return high, (x - high.astype(F32)).astype(BF16)


def stacked(x, axis):
    high, low = split(x)
    return jnp.concatenate([high, low, high], axis=axis)


def lane_tiles(table):
    if table.shape[1] == 128:
        return table
    tile = math.gcd(table.shape[1], 128)
    return table.reshape(table.shape[0], -1, tile).transpose(1, 0, 2)


def broad(ref, tiles=None, rows=None):
    tiles = ref.shape[0] if tiles is None else tiles
    return jnp.concatenate([ref[j, :rows] for j in range(tiles)], axis=1)


def iota(shape, dim):
    return lax.broadcasted_iota(jnp.int32, shape, dim).astype(F32)


def total(mask, values, axis):
    return jnp.sum(jnp.where(mask, values, 0.0), axis=axis, keepdims=True)


def kernel(
    groups, slabs, count, loads, *refs,
):
    lengths, sources, refs = refs[0], refs[1 : 1 + loads], refs[1 + loads :]
    hall_far, room_far = refs[:2]
    landed, refs = refs[2 : 2 + loads], refs[2 + loads :]
    (
        hall_now, hall_prev, room_now, room_prev, ids,
        spread_t, respond_t, outer_t, cosx_t, cosy_t, cosz_t, face_t, force_t, room_t, cross_t,
    ) = landed
    (
        hall_c2, hall_gain, hall_base, hall_faces, hall_resp, hall_diff, hall_other,
        hall_send, hall_recv, a2a_send, a2a_recv,
        room_c2, room_gain, room_a, room_b, room_faces, raw_faces, raw_force, raw_full,
        face_l, force_l, full_l, pack_l, take_l, room_send, room_recv, hall_out, room_out, relay,
        load_sem, store_sem, hall_ssem, hall_rsem, a2a_ssem, a2a_rsem, relay_sem, room_ssem, room_rsem,
    ) = refs
    me = lax.axis_index("grp")
    column = lax.axis_index("slab")
    nx, part_y, nz = hall_now.shape
    ny = part_y * slabs
    part_x = nx // slabs
    lanes = nx * part_y
    width = room_now.shape[0] // count
    batches = count // 4

    copies = [pltpu.make_async_copy(sources[i], landed[i], load_sem.at[i]) for i in range(loads)]
    order = [0, 5, 2, 4, 11, 1, 6, 3, 12, 7, 13, 8, 10, 9, 14]
    for i in order:
        copies[i].start()

    barrier = pltpu.get_barrier_semaphore()

    def greet_grp(step, carry):
        pl.semaphore_signal(
            barrier, inc=1, device_id=(lax.rem(me + step, groups), column), device_id_type=MESH
        )
        return carry

    def greet_slab(step, carry):
        pl.semaphore_signal(
            barrier, inc=1, device_id=(me, lax.rem(column + step, slabs)), device_id_type=MESH
        )
        return carry

    lax.fori_loop(1, groups, greet_grp, 0)
    lax.fori_loop(1, slabs, greet_slab, 0)
    hall_other[...] = jnp.zeros_like(hall_other)

    chunk = 256
    deep = chunk // part_y

    def chunks(body, many):
        def several(i, carry):
            for j in range(many):
                body(i * many + j)
            return carry

        lax.fori_loop(0, lanes // chunk // many, several, 0)

    def spread_of(x):
        high, low = split(x)
        both = mm_nt(broad(spread_t), jnp.concatenate([high, low], axis=1))
        return both[:8] + both[8:]

    def first_faces(i):
        x = hall_now[pl.ds(i * deep, deep)].reshape(chunk, nz)
        hall_faces[0, :, pl.ds(pl.multiple_of(i * chunk, chunk), chunk)] = spread_of(x)

    copies[0].wait()
    copies[5].wait()
    chunks(first_faces, 4)

    def hall_copy(t, side):
        peer = lax.rem(me + (1 if side == 0 else groups - 1), groups)
        return pltpu.make_async_remote_copy(
            src_ref=hall_send.at[t, side],
            dst_ref=hall_recv.at[t, side],
            send_sem=hall_ssem.at[t, side],
            recv_sem=hall_rsem.at[t, side],
            device_id=(peer, column),
            device_id_type=MESH,
        )

    def hall_put(t):
        own = hall_faces[t]
        for k in range(3):
            for j in range(lanes // 128):
                cut = slice(128 * j, 128 * j + 128)
                hall_send[t, 0, k, j : j + 1, :] = own[3 + k : 4 + k, cut]
                hall_send[t, 1, k, j : j + 1, :] = own[k : k + 1, cut]
        hall_copy(t, 0).start()
        hall_copy(t, 1).start()

    def hall_get(t):
        hall_copy(t, 0).wait_recv()
        hall_copy(t, 1).wait_recv()
        for k in range(3):
            for j in range(lanes // 128):
                cut = slice(128 * j, 128 * j + 128)
                hall_other[k : k + 1, cut] = hall_recv[t, 0, k, j : j + 1, :]
                hall_other[3 + k : 4 + k, cut] = hall_recv[t, 1, k, j : j + 1, :]
        row = lax.broadcasted_iota(jnp.int32, (8, lanes), 0)
        first = jnp.where(me > 0, 0, 3)
        last = jnp.where(me < groups - 1, 6, 3)
        diff = jnp.where((row >= first) & (row < last), hall_other[...] - hall_faces[t], 0.0)
        hall_diff[t] = diff
        return diff

    def hall_respond(t, lag, diff):
        acc = hall_faces[t + lag]
        for k in range(6):
            acc = acc + hall_resp[lag - 1, 8 * k : 8 * k + 8, :] * diff[k : k + 1, :]
        hall_faces[t + lag] = acc

    def terms(e):
        high = e.astype(BF16).astype(F32)
        low = e - high
        return jnp.concatenate([high, low, high, low], axis=0)

    def accumulate_early(i):
        at = pl.ds(i * deep, deep)
        cols = pl.ds(pl.multiple_of(i * chunk, chunk), chunk)
        e = jnp.concatenate([terms(hall_diff[t, :, cols]) for t in range(3)], axis=0).T.astype(BF16)
        forced = mm(e, broad(outer_t, 3, 96))
        c2 = hall_c2[at]
        f0, f1, f2 = [forced[:, 128 * t : 128 * t + 128].reshape(deep, part_y, nz) for t in range(3)]
        square = c2 * c2
        weighted = c2 * ((square - 2.0) * f0 + f2) + (square - 1.0) * f1
        hall_base[at] = hall_base[at] + hall_gain[at] * weighted

    def accumulate_last(i):
        at = pl.ds(i * deep, deep)
        cols = pl.ds(pl.multiple_of(i * chunk, chunk), chunk)
        e = terms(hall_diff[3, :, cols]).T.astype(BF16)
        forced = mm(e, outer_t[0, :32]).reshape(deep, part_y, nz)
        hall_base[at] = hall_base[at] + hall_gain[at] * forced

    pl.semaphore_wait(barrier, groups + slabs - 2)
    hall_put(0)


    lane = lax.broadcasted_iota(jnp.int32, (width, 128), 1)
    shift = int(math.log2(width))
    blocks = [(lane >> shift) == i for i in range(4)]
    blocks8 = [block[:8] for block in blocks]
    kx = lax.broadcasted_iota(jnp.int32, (width, 128), 0)

    def room_first(b, carry):
        for i in range(4):
            r = 4 * b + i
            length = lengths[0, 0, r]
            which = jnp.maximum(length - SHORTEST, 0)
            at = pl.ds(pl.multiple_of(r * width, width), width)
            at8 = pl.ds(pl.multiple_of(r * 8, 8), 8)
            raw_faces[at8, :] = jnp.where(blocks8[i], face_t[which], 0.0)
            room_a[at, :] = jnp.where(kx < jnp.full((width, 128), length, jnp.int32), room_now[at, :], 0.0)
        return carry

    copies[2].wait()
    copies[4].wait()
    copies[11].wait()
    lax.fori_loop(0, batches, room_first, 0)
    for b in range(batches):
        cut = slice(32 * b, 32 * b + 32)
        big = slice(128 * b, 128 * b + 128)
        high, low = split(raw_faces[cut, :])
        face_l[cut, :] = jnp.concatenate([high, high, low], axis=1)
        room_faces[cut, :] = mm(face_l[cut, :], stacked(room_a[big, :], 0))

    bits = int(math.log2(count))
    wide = 8 * count
    span = ids.shape[1]
    row_lanes = min(128, span)
    flat = jnp.concatenate(
        [ids[0:1, row_lanes * j : row_lanes * (j + 1)] for j in range(span // row_lanes)], axis=0
    )
    device = (flat >> bits).astype(F32)
    slot = (flat & (count - 1)).astype(F32)
    lane_i = lax.broadcasted_iota(jnp.int32, (count, wide), 1)
    p_col = iota((count, wide), 0)
    p_row = (lane_i >> 3).astype(F32)
    f_row = (lane_i & 7).astype(F32)
    expand = lax.broadcasted_iota(jnp.int32, (row_lanes, wide), 1) >> 3
    expand = jnp.where(expand == lax.broadcasted_iota(jnp.int32, (row_lanes, wide), 0), 1.0, 0.0)
    s_row = mm(device.astype(BF16), expand.astype(BF16))[0:1]
    s_col = device.T[:count, 0:1]
    same = s_col == s_row
    rank_row = total(same & (p_col < p_row), 1.0, 0)
    rank_col = total(same & (p_row < p_col) & (f_row == 0.0), 1.0, 1)
    home = me.astype(F32) - s_col
    home = jnp.where(home < 0.0, home + groups, home)
    per_row = row_lanes // count
    home = jnp.concatenate([home] * per_row, axis=0)
    shape = (row_lanes, span // row_lanes)
    group = per_row * lax.broadcasted_iota(jnp.int32, shape, 1)
    group = group + (lax.broadcasted_iota(jnp.int32, shape, 0) >> bits)
    landing = total(group.astype(F32) == home, slot.T, 1)
    landing = sum(landing[count * i : count * (i + 1)] for i in range(per_row))
    match = landing == p_row
    ls_row = total(match, jnp.broadcast_to(s_col, (count, wide)), 0)
    lr_row = total(match, jnp.broadcast_to(rank_col, (count, wide)), 0)

    def back(s):
        return jnp.where(s == 0.0, 0.0, groups - s)

    f = f_row[0:1]
    layer = jnp.where(f < 3.0, f, f - 3.0)
    pack_row = jnp.where(
        f < 3.0, 16.0 * back(ls_row) + 6.0 + 3.0 * lr_row + layer, 16.0 * s_row + 3.0 * rank_row + layer
    )
    take_row = jnp.where(
        f < 3.0, 16.0 * ls_row + 3.0 * lr_row + layer, 16.0 * back(s_row) + 6.0 + 3.0 * rank_row + layer
    )
    pack_row = jnp.where(f < 6.0, pack_row, -1.0)
    take_row = jnp.where(f < 6.0, take_row, -1.0)
    slots = 16 * groups
    pack_l[...] = jnp.where(iota((slots, wide), 0) == pack_row, 1.0, 0.0).astype(BF16)

    def room_copy(t, step):
        return pltpu.make_async_remote_copy(
            src_ref=room_send.at[t, step],
            dst_ref=room_recv.at[t, step - 1],
            send_sem=room_ssem.at[t],
            recv_sem=room_rsem.at[t],
            device_id=(lax.rem(me + step, groups), column),
            device_id_type=MESH,
        )

    def room_all(t):
        return pltpu.make_async_remote_copy(
            src_ref=room_send.at[t, pl.ds(1, groups - 1)],
            dst_ref=room_recv.at[t],
            send_sem=room_ssem.at[t],
            recv_sem=room_rsem.at[t],
            device_id=(lax.rem(me + 1, groups), column),
            device_id_type=MESH,
        )

    def far_first(i, count):
        half = i // 2
        return count // 2 + jnp.where(lax.rem(i, 2) == 0, half, -half)

    def two_parts(x):
        return jnp.concatenate(split(x), axis=1)

    def room_put(t):
        packed = mm(pack_l[...], two_parts(room_faces[...]))
        packed = packed[:, :128] + packed[:, 128:]
        room_send[t] = packed.reshape(groups, 16, 128)[:, :12, :]

        def body(i, carry):
            room_copy(t, far_first(i, groups)).start()
            return carry

        lax.fori_loop(1, groups, body, 0)

    def store(which, i):
        near, far = ((hall_out, hall_far), (room_out, room_far))[which]
        size = near.shape[0] // (8 if which == 0 else batches)
        at = pl.ds(i * size, size)
        return pltpu.make_async_copy(near.at[at], far.at[at], store_sem.at[which, i])

    def room_get(t):
        room_all(t).wait_recv()
        got = jnp.concatenate([room_send[t, 0:1], room_recv[t]], axis=0)
        got = jnp.concatenate([got, jnp.zeros((groups, 4, 128), F32)], axis=1).reshape(slots, 128)
        other = mm(take_l[...], two_parts(got))
        return other[:, :128] + other[:, 128:] - room_faces[...]

    def room_sent(t):
        room_all(t).wait_send()

    def room_step(t):
        diff = room_get(t)
        now, prev = (room_a, room_b) if t % 2 == 0 else (room_b, room_a)
        for b in range(batches):
            cut = slice(32 * b, 32 * b + 32)
            big = slice(128 * b, 128 * b + 128)
            high, low = split(diff[cut])
            forced = mm(force_l[big, :], jnp.concatenate([high, low, high, low], axis=0))
            fresh = room_c2[big, :] * now[big, :] - prev[big, :] + room_gain[big, :] * forced
            if t < STEPS - 1:
                prev[big, :] = fresh
                room_faces[cut, :] = mm(face_l[cut, :], stacked(fresh, 0))
            else:
                x = mm(full_l[big, :], stacked(fresh, 0))
                room_out[big, :] = mm(stacked(x, 1), cross_t[...])
                store(1, b).start()
        if t < STEPS - 1:
            room_put(t + 1)
            room_sent(t)

    room_put(0)

    yz = lax.broadcasted_iota(jnp.int32, (part_y, nz), 0) + column * part_y
    ky_f = yz.astype(F32)
    kz_f = iota((part_y, nz), 1)
    q_yz = (SCALE / ny**2) * (ky_f * ky_f) + (SCALE / nz**2) * (kz_f * kz_f)

    def prepare_first(i):
        at = pl.ds(i * deep, deep)
        cols = pl.ds(pl.multiple_of(i * chunk, chunk), chunk)
        a = (lax.broadcasted_iota(jnp.int32, (deep, part_y, nz), 0) + i * deep).astype(F32)
        c2, gain = factors((SCALE / nx**2) * (a * a) + q_yz[None])
        hall_c2[at] = c2
        hall_gain[at] = gain
        fresh = c2 * hall_now[at] - hall_prev[at]
        hall_base[at] = fresh
        hall_faces[1, :, cols] = spread_of(fresh.reshape(chunk, nz))
        both = mm_nt(respond_t[0, :96], gain.reshape(chunk, nz).astype(BF16))
        hall_resp[0, :, cols] = both[:48] + both[48:]

    def prepare_second(i):
        at = pl.ds(i * deep, deep)
        cols = pl.ds(pl.multiple_of(i * chunk, chunk), chunk)
        c2 = hall_c2[at]
        gain = hall_gain[at]
        m2 = c2 * hall_base[at] - hall_now[at]
        hall_faces[2, :, cols] = spread_of(m2.reshape(chunk, nz))
        s2 = gain * c2
        s3 = s2 * c2 - gain
        both = [s.reshape(chunk, nz).astype(BF16) for s in (s2, s3)]
        both = mm_nt(broad(respond_t), jnp.concatenate(both, axis=1))
        hall_resp[1, :, cols] = both[:48] + both[48:96]
        hall_resp[2, :, cols] = both[96:144] + both[144:]

    def prepare_third(i):
        at = pl.ds(i * deep, deep)
        cols = pl.ds(pl.multiple_of(i * chunk, chunk), chunk)
        c2 = hall_c2[at]
        m1 = hall_base[at]
        m2 = c2 * m1 - hall_now[at]
        m3 = c2 * m2 - m1
        hall_base[at] = c2 * m3 - m2
        hall_faces[3, :, cols] = spread_of(m3.reshape(chunk, nz))

    copies[1].wait()
    copies[6].wait()
    chunks(prepare_first, 2)
    diff = hall_get(0)
    hall_respond(0, 1, diff)
    hall_put(1)
    chunks(prepare_second, 2)
    hall_respond(0, 2, diff)
    diff = hall_get(1)
    hall_respond(1, 1, diff)
    hall_put(2)
    chunks(prepare_third, 2)
    hall_respond(0, 3, hall_diff[0])
    hall_respond(1, 2, diff)

    q_cross = (lane >> int(math.log2(SZ))).astype(F32) * (1.0 / SY)
    q_cross = SCALE * (q_cross * q_cross)
    z_part = (lane & (SZ - 1)).astype(F32) * (1.0 / SZ)
    q_cross = q_cross + SCALE * (z_part * z_part)
    kx_f = kx.astype(F32)
    kx_sq = SCALE * (kx_f * kx_f)

    def room_second(b, carry):
        for i in range(4):
            r = 4 * b + i
            length = lengths[0, 0, r]
            which = jnp.maximum(length - SHORTEST, 0)
            at = pl.ds(pl.multiple_of(r * width, width), width)
            at8 = pl.ds(pl.multiple_of(r * 8, 8), 8)
            raw_force[at8, :] = jnp.where(blocks8[i], force_t[which], 0.0)
            extent = jnp.full((width, 128), length, jnp.int32)
            live = kx < extent
            extent = extent[:8].astype(F32)
            inverse = 1.0 / (extent * extent)
            inverse = jnp.concatenate([inverse] * (width // 8), axis=0)
            c2, gain = factors(kx_sq * inverse + q_cross)
            room_c2[at, :] = c2
            room_gain[at, :] = gain
            room_b[at, :] = jnp.where(live, room_prev[at, :], 0.0)
        return carry

    copies[3].wait()
    copies[12].wait()
    lax.fori_loop(0, batches, room_second, 0)
    for b in range(batches):
        x = raw_force[32 * b : 32 * b + 32, :]
        high = x.astype(BF16).astype(F32)
        low = x - high
        force_l[128 * b : 128 * b + 128, :] = jnp.concatenate([high, high, low, low], axis=0).T.astype(BF16)
    take_col = jnp.broadcast_to(take_row, (8, wide)).T[:, 0:1]
    take_l[...] = jnp.where(iota((wide, slots), 1) == take_col, 1.0, 0.0).astype(BF16)

    diff = hall_get(2)
    hall_respond(2, 1, diff)
    hall_put(3)
    room_step(0)
    copies[7].wait()
    chunks(accumulate_early, 2)
    hall_get(3)
    chunks(accumulate_last, 2)

    parts = 2
    part_b = part_y // parts

    ring = slabs // 2
    chip = column // 2
    core = lax.rem(column, 2)
    relayed = ring == 8

    def column_of(hops, k):
        return 2 * lax.rem(chip + hops + ring, ring) + k

    def a2a_copy(h, hops, k, source_core):
        peer = column_of(hops, k)
        return pltpu.make_async_remote_copy(
            src_ref=a2a_send.at[pl.ds(part_b * h, part_b), pl.ds(pl.multiple_of(peer * part_x, part_x), part_x), :],
            dst_ref=a2a_recv.at[pl.ds(column * part_y + part_b * h, part_b)],
            send_sem=a2a_ssem.at[h, 2 * hops + k],
            recv_sem=a2a_rsem.at[h, 2 * hops + source_core],
            device_id=(me, peer),
            device_id_type=MESH,
        )

    def relay_copy(h):
        far = pl.multiple_of(column_of(ring // 2, 0) * part_x, 2 * part_x)
        return pltpu.make_async_remote_copy(
            src_ref=a2a_send.at[pl.ds(part_b * h, part_b), pl.ds(far, 2 * part_x), :],
            dst_ref=relay.at[h],
            send_sem=relay_sem.at[h, 0],
            recv_sem=relay_sem.at[h, 1],
            device_id=(me, column_of(1 - 2 * h, core)),
            device_id_type=MESH,
        )

    def forward_copy(h, k):
        way = 1 - 2 * h
        source = column_of(-way, core)
        return pltpu.make_async_remote_copy(
            src_ref=relay.at[h, :, pl.ds(k * part_x, part_x), :],
            dst_ref=a2a_recv.at[pl.ds(source * part_y + part_b * h, part_b)],
            send_sem=relay_sem.at[h, 2 + k],
            recv_sem=a2a_rsem.at[h, ring + core],
            device_id=(me, column_of(3 * way, k)),
            device_id_type=MESH,
        )

    first_hop = 2 if relayed else 1

    copies[8].wait()
    for h in range(parts):
        for b in range(part_b * h, part_b * h + part_b, 2):
            pair = [stacked(hall_base[:, b + i, :], 0) for i in range(2)]
            y = mm(broad(cosx_t), jnp.concatenate(pair, axis=1))
            a2a_send[b] = y[:, :nz]
            a2a_send[b + 1] = y[:, nz:]

        if relayed:
            relay_copy(h).start()

        def a2a_start(i, carry):
            a2a_copy(h, far_first(i // 2, ring), lax.rem(i, 2), core).start()
            return carry

        lax.fori_loop(2 * first_hop, 2 * ring, a2a_start, 0)
        a2a_copy(h, 0, 1 - core, core).start()

    def z_part_of(x):
        x = stacked(x.reshape(part_y * part_x, nz), 1)
        return mm(x, cosz_t[...]).reshape(part_y, part_x, nz)

    copies[10].wait()
    own = pl.ds(pl.multiple_of(column * part_x, part_x), part_x)
    a2a_recv[pl.ds(column * part_y, part_y)] = z_part_of(a2a_send[:, own, :])

    def take_from(hops, k):
        a2a_copy(0, hops, k, k).wait_recv()
        a2a_copy(1, hops, k, k).wait_recv()
        at = pl.ds(column_of(-hops, k) * part_y, part_y)
        a2a_recv[at] = z_part_of(a2a_recv[at])

    def a2a_take(i, carry):
        i = 2 * ring + 2 * first_hop - 1 - i
        take_from(far_first(i // 2, ring), lax.rem(i, 2))
        return carry

    def room_tables_full(b, carry):
        for i in range(4):
            r = 4 * b + i
            which = jnp.maximum(lengths[0, 0, r] - SHORTEST, 0)
            at = pl.ds(pl.multiple_of(r * width, width), width)
            raw_full[at, :] = jnp.where(blocks[i], room_t[which], 0.0)
        return carry

    copies[13].wait()
    copies[14].wait()
    lax.fori_loop(0, batches, room_tables_full, 0)
    for b in range(batches):
        big = slice(128 * b, 128 * b + 128)
        high, low = split(raw_full[big, :])
        full_l[big, :] = jnp.concatenate([high, high, low], axis=1)

    room_step(1)
    if relayed:
        for h in range(parts):
            relay_copy(h).wait_recv()
            forward_copy(h, 0).start()
            forward_copy(h, 1).start()
    for t in range(STEPS - 1):
        hall_copy(t, 0).wait_send()
        hall_copy(t, 1).wait_send()
    room_step(2)
    hall_copy(3, 0).wait_send()
    hall_copy(3, 1).wait_send()
    take_from(0, 1 - core)
    lax.fori_loop(2 * first_hop, 2 * ring, a2a_take, 0)
    if relayed:
        take_from(ring // 2, 0)
        take_from(ring // 2, 1)
    copies[9].wait()
    for x in range(0, part_x, 2):
        pair = jnp.concatenate([stacked(a2a_recv[:, x, :], 0), stacked(a2a_recv[:, x + 1, :], 0)], axis=1)
        y = mm(broad(cosy_t), pair)
        hall_out[x] = y[:, :nz]
        hall_out[x + 1] = y[:, nz:]
    for i in range(8):
        store(0, i).start()

    room_step(3)
    room_sent(3)

    for h in range(parts):

        def a2a_sent(i, carry):
            a2a_copy(h, far_first(i // 2, ring), lax.rem(i, 2), core).wait_send()
            return carry

        lax.fori_loop(2 * first_hop, 2 * ring, a2a_sent, 0)
        a2a_copy(h, 0, 1 - core, core).wait_send()
        if relayed:
            relay_copy(h).wait_send()
            forward_copy(h, 0).wait_send()
            forward_copy(h, 1).wait_send()

    for i in range(8):
        store(0, i).wait()
    for i in range(batches):
        store(1, i).wait()


def hand_on(hall_in, room_in, hall_out, room_out, hall_mid, room_mid, load_sem, store_sem):
    loads, stores = [], []
    for j, (near, mid, far) in enumerate(((hall_in, hall_mid, hall_out), (room_in, room_mid, room_out))):
        size = near.shape[0] // 4
        for i in range(4):
            at = pl.ds(i * size, size)
            loads.append(pltpu.make_async_copy(near.at[at], mid.at[at], load_sem.at[j, i]))
            stores.append(pltpu.make_async_copy(mid.at[at], far.at[at], store_sem.at[j, i]))
    for load in loads:
        load.start()
    for load, store in zip(loads, stores):
        load.wait()
        store.start()
    for store in stores:
        store.wait()


def local(hall_now, hall_prev, room_now, room_prev, room_length, right_neighbor):
    groups = lax.axis_size("grp")
    slabs = lax.axis_size("slab")
    _, nx, part_y, nz = hall_now.shape
    _, _, count, width, cross = room_now.shape
    ny = part_y * slabs
    part_x = nx // slabs
    lanes = nx * part_y
    slots = 16 * groups
    rows = count * width
    inputs = [
        hall_now[0], hall_prev[0], room_now.reshape(rows, cross), room_prev.reshape(rows, cross), right_neighbor,
    ]
    inputs += [jnp.asarray(lane_tiles(t)) for t in hall_tables(nx, ny, nz)]
    inputs += [jnp.asarray(t) for t in room_tables(width)]
    inputs += [jnp.asarray(right_table(np.kron(dct(SY), dct(SZ))))]
    smem = pl.BlockSpec(memory_space=pltpu.SMEM)
    away = pl.BlockSpec(memory_space=pl.ANY)
    dma = pltpu.SemaphoreType.DMA
    results = pl.pallas_call(
        functools.partial(kernel, groups, slabs, count, len(inputs)),
        out_shape=(
            jax.ShapeDtypeStruct((part_x, ny, nz), F32),
            jax.ShapeDtypeStruct((rows, cross), F32),
        ),
        in_specs=[smem] + [away] * len(inputs),
        out_specs=(away, away),
        scratch_shapes=[pltpu.VMEM(x.shape, x.dtype) for x in inputs]
        + [
            pltpu.VMEM((nx, part_y, nz), F32),
            pltpu.VMEM((nx, part_y, nz), F32),
            pltpu.VMEM((nx, part_y, nz), F32),
            pltpu.VMEM((STEPS, 8, lanes), F32),
            pltpu.VMEM((STEPS - 1, 48, lanes), F32),
            pltpu.VMEM((STEPS, 8, lanes), F32),
            pltpu.VMEM((8, lanes), F32),
            pltpu.VMEM((STEPS, 2, 3, lanes // 128, 128), F32),
            pltpu.VMEM((STEPS, 2, 3, lanes // 128, 128), F32),
            pltpu.VMEM((part_y, nx, nz), F32),
            pltpu.VMEM((ny, part_x, nz), F32),
            pltpu.VMEM((rows, cross), F32),
            pltpu.VMEM((rows, cross), F32),
            pltpu.VMEM((rows, cross), F32),
            pltpu.VMEM((rows, cross), F32),
            pltpu.VMEM((8 * count, cross), F32),
            pltpu.VMEM((8 * count, 4 * width), F32),
            pltpu.VMEM((8 * count, 4 * width), F32),
            pltpu.VMEM((rows, 4 * width), F32),
            pltpu.VMEM((8 * count, 12 * width), BF16),
            pltpu.VMEM((rows, 128), BF16),
            pltpu.VMEM((rows, 12 * width), BF16),
            pltpu.VMEM((slots, 8 * count), BF16),
            pltpu.VMEM((8 * count, slots), BF16),
            pltpu.VMEM((STEPS, groups, 12, 128), F32),
            pltpu.VMEM((STEPS, groups - 1, 12, 128), F32),
            pltpu.VMEM((part_x, ny, nz), F32),
            pltpu.VMEM((rows, cross), F32),
            pltpu.VMEM((2, part_y // 2, 2 * part_x, nz), F32),
            dma((len(inputs),)),
            dma((2, 8)),
            dma((STEPS, 2)),
            dma((STEPS, 2)),
            dma((2, slabs)),
            dma((2, slabs)),
            dma((2, 4)),
            dma((STEPS,)),
            dma((STEPS,)),
        ],
        compiler_params=pltpu.CompilerParams(
            collective_id=0, has_side_effects=True, vmem_limit_bytes=60 * 1024 * 1024
        ),
    )(room_length, *inputs)
    hall_pressure, room_pressure = pl.pallas_call(
        hand_on,
        out_shape=tuple(jax.ShapeDtypeStruct(x.shape, x.dtype) for x in results),
        in_specs=[away] * 2,
        out_specs=(away, away),
        scratch_shapes=[pltpu.VMEM(x.shape, x.dtype) for x in results] + [dma((2, 4)), dma((2, 4))],
        compiler_params=pltpu.CompilerParams(vmem_limit_bytes=60 * 1024 * 1024),
    )(*results)
    return (hall_pressure[None], room_pressure.reshape(1, 1, count, width, cross))


def solution(mesh):
    in_specs = (
        P("grp", None, "slab", None),
        P("grp", None, "slab", None),
        P("grp", "slab", None, None, None),
        P("grp", "slab", None, None, None),
        P("grp", "slab", None),
        P("slab", None),
    )
    out_specs = (P("grp", "slab", None, None), P("grp", "slab", None, None, None))
    return jax.shard_map(local, mesh=mesh, in_specs=in_specs, out_specs=out_specs, check_vma=False)
```

```python
import functools
import math

import jax
import jax.numpy as jnp
import ml_dtypes
import numpy as np
from jax import lax
from jax.experimental import pallas as pl
from jax.experimental.pallas import tpu as pltpu
from jax.sharding import PartitionSpec as P

SY = 8
SZ = 16
STEPS = 4
SHORTEST = 16
TIME_STEP = 0.4
SCALE = (TIME_STEP * math.pi) ** 2
STENCIL = np.array([[270, -27, 2], [-27, 2, 0], [2, 0, 0]], np.float64) / 180.0
F32 = jnp.float32
BF16 = jnp.bfloat16
MESH = pl.DeviceIdType.MESH


def dct(length):
    k = np.arange(length)[:, None]
    i = np.arange(length)[None, :]
    w = np.where(k == 0, np.sqrt(1.0 / length), np.sqrt(2.0 / length))
    return w * np.cos(np.pi * k * (2 * i + 1) / (2 * length))


def halves(x):
    high = x.astype(np.float32).astype(ml_dtypes.bfloat16)
    low = (x - high.astype(np.float64)).astype(ml_dtypes.bfloat16)
    return high, low


def left_table(x):
    high, low = halves(x)
    return np.concatenate([high, high, low], axis=1)


def right_table(x):
    high, low = halves(x)
    return np.concatenate([high, high, low], axis=0)


def face_rows(table):
    length = table.shape[0]
    sign = np.where(np.arange(length) % 2 == 0, 1.0, -1.0)
    low = table[:, :3].T
    forced = STENCIL.T @ low
    zero = np.zeros((2, length))
    return (
        np.concatenate([low, low * sign, zero], axis=0),
        np.concatenate([forced, forced * sign, zero], axis=0),
    )


def hall_tables(nx, ny, nz):
    faces, forced = face_rows(dct(nz))
    high, low = halves(faces)
    spread = np.concatenate(
        [np.concatenate([high, high], axis=1), np.concatenate([low, 0 * low], axis=1)], axis=0
    )
    pairs = np.concatenate([forced[k : k + 1] * faces for k in range(6)], axis=0)
    both = np.concatenate(halves(pairs), axis=0)
    respond = np.concatenate(
        [np.concatenate([both, 0 * both], axis=1), np.concatenate([0 * both, both], axis=1)], axis=0
    )
    high, low = halves(forced)
    outer = np.concatenate([high, high, low, low], axis=0)
    blank = np.zeros((32, 384), ml_dtypes.bfloat16)
    outer = np.concatenate([np.concatenate([blank[:, : 128 * t], outer, blank[:, 128 * t :]], axis=1) for t in range(4)], axis=0)
    return spread, respond, outer, left_table(dct(nx).T), left_table(dct(ny).T), right_table(dct(nz))


def room_tables(width):
    faces, forced, full = [], [], []
    for length in range(SHORTEST, width + 1):
        table = np.zeros((width, width))
        table[:length, :length] = dct(length)
        low, high = face_rows(table[:, :])
        faces.append(np.tile(low, (1, 4)))
        forced.append(np.tile(high, (1, 4)))
        full.append(np.tile(table.T, (1, 4)))
    return [np.stack(t).astype(np.float32) for t in (faces, forced, full)]


def factors(q):
    h = jnp.full_like(q, 2.0 / math.factorial(16))
    for n in range(6, -1, -1):
        h = 2.0 / math.factorial(2 * n + 2) - h * q
    return 2.0 - q * h, (TIME_STEP * TIME_STEP) * h


def mm(a, b):
    return jnp.dot(a, b, preferred_element_type=F32)


def mm_nt(a, b):
    return lax.dot_general(a, b, (((1,), (1,)), ((), ())), preferred_element_type=F32)


def split(x):
    high = x.astype(BF16)
    return high, (x - high.astype(F32)).astype(BF16)


def stacked(x, axis):
    high, low = split(x)
    return jnp.concatenate([high, low, high], axis=axis)


def lane_tiles(table):
    if table.shape[1] == 128:
        return table
    tile = math.gcd(table.shape[1], 128)
    return table.reshape(table.shape[0], -1, tile).transpose(1, 0, 2)


def broad(ref, tiles=None, rows=None):
    tiles = ref.shape[0] if tiles is None else tiles
    return jnp.concatenate([ref[j, :rows] for j in range(tiles)], axis=1)


def iota(shape, dim):
    return lax.broadcasted_iota(jnp.int32, shape, dim).astype(F32)


def total(mask, values, axis):
    return jnp.sum(jnp.where(mask, values, 0.0), axis=axis, keepdims=True)


def kernel(
    groups, slabs, count, loads, *refs,
):
    lengths, sources, refs = refs[0], refs[1 : 1 + loads], refs[1 + loads :]
    hall_far, room_far = refs[:2]
    landed, refs = refs[2 : 2 + loads], refs[2 + loads :]
    (
        hall_now, hall_prev, room_now, room_prev, ids,
        spread_t, respond_t, outer_t, cosx_t, cosy_t, cosz_t, face_t, force_t, room_t, cross_t,
    ) = landed
    (
        hall_c2, hall_gain, hall_base, hall_faces, hall_resp, hall_diff, hall_other,
        hall_send, hall_recv, a2a_send, a2a_recv,
        room_c2, room_gain, room_a, room_b, room_faces, raw_faces, raw_force, raw_full,
        face_l, force_l, full_l, pack_l, take_l, room_send, room_recv, hall_out, room_out, relay,
        load_sem, store_sem, hall_ssem, hall_rsem, a2a_ssem, a2a_rsem, relay_sem, room_ssem, room_rsem,
    ) = refs
    me = lax.axis_index("grp")
    column = lax.axis_index("slab")
    nx, part_y, nz = hall_now.shape
    ny = part_y * slabs
    part_x = nx // slabs
    lanes = nx * part_y
    width = room_now.shape[0] // count
    batches = count // 4

    copies = [pltpu.make_async_copy(sources[i], landed[i], load_sem.at[i]) for i in range(loads)]
    order = [0, 5, 2, 4, 11, 1, 6, 3, 12, 7, 13, 8, 10, 9, 14]
    for i in order:
        copies[i].start()

    barrier = pltpu.get_barrier_semaphore()

    def greet_grp(step, carry):
        pl.semaphore_signal(
            barrier, inc=1, device_id=(lax.rem(me + step, groups), column), device_id_type=MESH
        )
        return carry

    def greet_slab(step, carry):
        pl.semaphore_signal(
            barrier, inc=1, device_id=(me, lax.rem(column + step, slabs)), device_id_type=MESH
        )
        return carry

    lax.fori_loop(1, groups, greet_grp, 0)
    lax.fori_loop(1, slabs, greet_slab, 0)
    hall_other[...] = jnp.zeros_like(hall_other)

    chunk = 256
    deep = chunk // part_y

    def chunks(body, many):
        def several(i, carry):
            for j in range(many):
                body(i * many + j)
            return carry

        lax.fori_loop(0, lanes // chunk // many, several, 0)

    def spread_of(x):
        high, low = split(x)
        both = mm_nt(broad(spread_t), jnp.concatenate([high, low], axis=1))
        return both[:8] + both[8:]

    def first_faces(i):
        x = hall_now[pl.ds(i * deep, deep)].reshape(chunk, nz)
        hall_faces[0, :, pl.ds(pl.multiple_of(i * chunk, chunk), chunk)] = spread_of(x)

    copies[0].wait()
    copies[5].wait()
    chunks(first_faces, 4)

    def hall_copy(t, side):
        peer = lax.rem(me + (1 if side == 0 else groups - 1), groups)
        return pltpu.make_async_remote_copy(
            src_ref=hall_send.at[t, side],
            dst_ref=hall_recv.at[t, side],
            send_sem=hall_ssem.at[t, side],
            recv_sem=hall_rsem.at[t, side],
            device_id=(peer, column),
            device_id_type=MESH,
        )

    def hall_put(t):
        own = hall_faces[t]
        for k in range(3):
            for j in range(lanes // 128):
                cut = slice(128 * j, 128 * j + 128)
                hall_send[t, 0, k, j : j + 1, :] = own[3 + k : 4 + k, cut]
                hall_send[t, 1, k, j : j + 1, :] = own[k : k + 1, cut]
        hall_copy(t, 0).start()
        hall_copy(t, 1).start()

    def hall_get(t):
        hall_copy(t, 0).wait_recv()
        hall_copy(t, 1).wait_recv()
        for k in range(3):
            for j in range(lanes // 128):
                cut = slice(128 * j, 128 * j + 128)
                hall_other[k : k + 1, cut] = hall_recv[t, 0, k, j : j + 1, :]
                hall_other[3 + k : 4 + k, cut] = hall_recv[t, 1, k, j : j + 1, :]
        row = lax.broadcasted_iota(jnp.int32, (8, lanes), 0)
        first = jnp.where(me > 0, 0, 3)
        last = jnp.where(me < groups - 1, 6, 3)
        diff = jnp.where((row >= first) & (row < last), hall_other[...] - hall_faces[t], 0.0)
        hall_diff[t] = diff
        return diff

    def hall_respond(t, lag, diff):
        acc = hall_faces[t + lag]
        for k in range(6):
            acc = acc + hall_resp[lag - 1, 8 * k : 8 * k + 8, :] * diff[k : k + 1, :]
        hall_faces[t + lag] = acc

    def terms(e):
        high = e.astype(BF16).astype(F32)
        low = e - high
        return jnp.concatenate([high, low, high, low], axis=0)

    def accumulate_early(i):
        at = pl.ds(i * deep, deep)
        cols = pl.ds(pl.multiple_of(i * chunk, chunk), chunk)
        e = jnp.concatenate([terms(hall_diff[t, :, cols]) for t in range(3)], axis=0).T.astype(BF16)
        forced = mm(e, broad(outer_t, 3, 96))
        c2 = hall_c2[at]
        f0, f1, f2 = [forced[:, 128 * t : 128 * t + 128].reshape(deep, part_y, nz) for t in range(3)]
        square = c2 * c2
        weighted = c2 * ((square - 2.0) * f0 + f2) + (square - 1.0) * f1
        hall_base[at] = hall_base[at] + hall_gain[at] * weighted

    def accumulate_last(i):
        at = pl.ds(i * deep, deep)
        cols = pl.ds(pl.multiple_of(i * chunk, chunk), chunk)
        e = terms(hall_diff[3, :, cols]).T.astype(BF16)
        forced = mm(e, outer_t[0, :32]).reshape(deep, part_y, nz)
        hall_base[at] = hall_base[at] + hall_gain[at] * forced

    pl.semaphore_wait(barrier, groups + slabs - 2)
    hall_put(0)


    lane = lax.broadcasted_iota(jnp.int32, (width, 128), 1)
    shift = int(math.log2(width))
    blocks = [(lane >> shift) == i for i in range(4)]
    blocks8 = [block[:8] for block in blocks]
    kx = lax.broadcasted_iota(jnp.int32, (width, 128), 0)

    def room_first(b, carry):
        for i in range(4):
            r = 4 * b + i
            length = lengths[0, 0, r]
            which = jnp.maximum(length - SHORTEST, 0)
            at = pl.ds(pl.multiple_of(r * width, width), width)
            at8 = pl.ds(pl.multiple_of(r * 8, 8), 8)
            raw_faces[at8, :] = jnp.where(blocks8[i], face_t[which], 0.0)
            room_a[at, :] = jnp.where(kx < jnp.full((width, 128), length, jnp.int32), room_now[at, :], 0.0)
        return carry

    copies[2].wait()
    copies[4].wait()
    copies[11].wait()
    lax.fori_loop(0, batches, room_first, 0)
    for b in range(batches):
        cut = slice(32 * b, 32 * b + 32)
        big = slice(128 * b, 128 * b + 128)
        high, low = split(raw_faces[cut, :])
        face_l[cut, :] = jnp.concatenate([high, high, low], axis=1)
        room_faces[cut, :] = mm(face_l[cut, :], stacked(room_a[big, :], 0))

    bits = int(math.log2(count))
    wide = 8 * count
    span = ids.shape[1]
    row_lanes = min(128, span)
    flat = jnp.concatenate(
        [ids[0:1, row_lanes * j : row_lanes * (j + 1)] for j in range(span // row_lanes)], axis=0
    )
    device = (flat >> bits).astype(F32)
    slot = (flat & (count - 1)).astype(F32)
    lane_i = lax.broadcasted_iota(jnp.int32, (count, wide), 1)
    p_col = iota((count, wide), 0)
    p_row = (lane_i >> 3).astype(F32)
    f_row = (lane_i & 7).astype(F32)
    expand = lax.broadcasted_iota(jnp.int32, (row_lanes, wide), 1) >> 3
    expand = jnp.where(expand == lax.broadcasted_iota(jnp.int32, (row_lanes, wide), 0), 1.0, 0.0)
    s_row = mm(device.astype(BF16), expand.astype(BF16))[0:1]
    s_col = device.T[:count, 0:1]
    same = s_col == s_row
    rank_row = total(same & (p_col < p_row), 1.0, 0)
    rank_col = total(same & (p_row < p_col) & (f_row == 0.0), 1.0, 1)
    home = me.astype(F32) - s_col
    home = jnp.where(home < 0.0, home + groups, home)
    per_row = row_lanes // count
    home = jnp.concatenate([home] * per_row, axis=0)
    shape = (row_lanes, span // row_lanes)
    group = per_row * lax.broadcasted_iota(jnp.int32, shape, 1)
    group = group + (lax.broadcasted_iota(jnp.int32, shape, 0) >> bits)
    landing = total(group.astype(F32) == home, slot.T, 1)
    landing = sum(landing[count * i : count * (i + 1)] for i in range(per_row))
    match = landing == p_row
    ls_row = total(match, jnp.broadcast_to(s_col, (count, wide)), 0)
    lr_row = total(match, jnp.broadcast_to(rank_col, (count, wide)), 0)

    def back(s):
        return jnp.where(s == 0.0, 0.0, groups - s)

    f = f_row[0:1]
    layer = jnp.where(f < 3.0, f, f - 3.0)
    pack_row = jnp.where(
        f < 3.0, 16.0 * back(ls_row) + 6.0 + 3.0 * lr_row + layer, 16.0 * s_row + 3.0 * rank_row + layer
    )
    take_row = jnp.where(
        f < 3.0, 16.0 * ls_row + 3.0 * lr_row + layer, 16.0 * back(s_row) + 6.0 + 3.0 * rank_row + layer
    )
    pack_row = jnp.where(f < 6.0, pack_row, -1.0)
    take_row = jnp.where(f < 6.0, take_row, -1.0)
    slots = 16 * groups
    pack_l[...] = jnp.where(iota((slots, wide), 0) == pack_row, 1.0, 0.0).astype(BF16)

    def room_copy(t, step):
        return pltpu.make_async_remote_copy(
            src_ref=room_send.at[t, step],
            dst_ref=room_recv.at[t, step - 1],
            send_sem=room_ssem.at[t],
            recv_sem=room_rsem.at[t],
            device_id=(lax.rem(me + step, groups), column),
            device_id_type=MESH,
        )

    def room_all(t):
        return pltpu.make_async_remote_copy(
            src_ref=room_send.at[t, pl.ds(1, groups - 1)],
            dst_ref=room_recv.at[t],
            send_sem=room_ssem.at[t],
            recv_sem=room_rsem.at[t],
            device_id=(lax.rem(me + 1, groups), column),
            device_id_type=MESH,
        )

    def far_first(i, count):
        half = i // 2
        return count // 2 + jnp.where(lax.rem(i, 2) == 0, half, -half)

    def two_parts(x):
        return jnp.concatenate(split(x), axis=1)

    def room_put(t):
        packed = mm(pack_l[...], two_parts(room_faces[...]))
        packed = packed[:, :128] + packed[:, 128:]
        room_send[t] = packed.reshape(groups, 16, 128)[:, :12, :]

        def body(i, carry):
            room_copy(t, far_first(i, groups)).start()
            return carry

        lax.fori_loop(1, groups, body, 0)

    def store(which, i):
        near, far = ((hall_out, hall_far), (room_out, room_far))[which]
        size = near.shape[0] // (8 if which == 0 else batches)
        at = pl.ds(i * size, size)
        return pltpu.make_async_copy(near.at[at], far.at[at], store_sem.at[which, i])

    def room_get(t):
        room_all(t).wait_recv()
        got = jnp.concatenate([room_send[t, 0:1], room_recv[t]], axis=0)
        got = jnp.concatenate([got, jnp.zeros((groups, 4, 128), F32)], axis=1).reshape(slots, 128)
        other = mm(take_l[...], two_parts(got))
        return other[:, :128] + other[:, 128:] - room_faces[...]

    def room_sent(t):
        room_all(t).wait_send()

    def room_step(t):
        diff = room_get(t)
        now, prev = (room_a, room_b) if t % 2 == 0 else (room_b, room_a)
        for b in range(batches):
            cut = slice(32 * b, 32 * b + 32)
            big = slice(128 * b, 128 * b + 128)
            high, low = split(diff[cut])
            forced = mm(force_l[big, :], jnp.concatenate([high, low, high, low], axis=0))
            fresh = room_c2[big, :] * now[big, :] - prev[big, :] + room_gain[big, :] * forced
            if t < STEPS - 1:
                prev[big, :] = fresh
                room_faces[cut, :] = mm(face_l[cut, :], stacked(fresh, 0))
            else:
                x = mm(full_l[big, :], stacked(fresh, 0))
                room_out[big, :] = mm(stacked(x, 1), cross_t[...])
                store(1, b).start()
        if t < STEPS - 1:
            room_put(t + 1)
            room_sent(t)

    room_put(0)

    yz = lax.broadcasted_iota(jnp.int32, (part_y, nz), 0) + column * part_y
    ky_f = yz.astype(F32)
    kz_f = iota((part_y, nz), 1)
    q_yz = (SCALE / ny**2) * (ky_f * ky_f) + (SCALE / nz**2) * (kz_f * kz_f)

    def prepare_first(i):
        at = pl.ds(i * deep, deep)
        cols = pl.ds(pl.multiple_of(i * chunk, chunk), chunk)
        a = (lax.broadcasted_iota(jnp.int32, (deep, part_y, nz), 0) + i * deep).astype(F32)
        c2, gain = factors((SCALE / nx**2) * (a * a) + q_yz[None])
        hall_c2[at] = c2
        hall_gain[at] = gain
        fresh = c2 * hall_now[at] - hall_prev[at]
        hall_base[at] = fresh
        hall_faces[1, :, cols] = spread_of(fresh.reshape(chunk, nz))
        both = mm_nt(respond_t[0, :96], gain.reshape(chunk, nz).astype(BF16))
        hall_resp[0, :, cols] = both[:48] + both[48:]

    def prepare_second(i):
        at = pl.ds(i * deep, deep)
        cols = pl.ds(pl.multiple_of(i * chunk, chunk), chunk)
        c2 = hall_c2[at]
        gain = hall_gain[at]
        m2 = c2 * hall_base[at] - hall_now[at]
        hall_faces[2, :, cols] = spread_of(m2.reshape(chunk, nz))
        s2 = gain * c2
        s3 = s2 * c2 - gain
        both = [s.reshape(chunk, nz).astype(BF16) for s in (s2, s3)]
        both = mm_nt(broad(respond_t), jnp.concatenate(both, axis=1))
        hall_resp[1, :, cols] = both[:48] + both[48:96]
        hall_resp[2, :, cols] = both[96:144] + both[144:]

    def prepare_third(i):
        at = pl.ds(i * deep, deep)
        cols = pl.ds(pl.multiple_of(i * chunk, chunk), chunk)
        c2 = hall_c2[at]
        m1 = hall_base[at]
        m2 = c2 * m1 - hall_now[at]
        m3 = c2 * m2 - m1
        hall_base[at] = c2 * m3 - m2
        hall_faces[3, :, cols] = spread_of(m3.reshape(chunk, nz))

    copies[1].wait()
    copies[6].wait()
    chunks(prepare_first, 2)
    diff = hall_get(0)
    hall_respond(0, 1, diff)
    hall_put(1)
    chunks(prepare_second, 2)
    hall_respond(0, 2, diff)
    diff = hall_get(1)
    hall_respond(1, 1, diff)
    hall_put(2)
    chunks(prepare_third, 2)
    hall_respond(0, 3, hall_diff[0])
    hall_respond(1, 2, diff)

    q_cross = (lane >> int(math.log2(SZ))).astype(F32) * (1.0 / SY)
    q_cross = SCALE * (q_cross * q_cross)
    z_part = (lane & (SZ - 1)).astype(F32) * (1.0 / SZ)
    q_cross = q_cross + SCALE * (z_part * z_part)
    kx_f = kx.astype(F32)
    kx_sq = SCALE * (kx_f * kx_f)

    def room_second(b, carry):
        for i in range(4):
            r = 4 * b + i
            length = lengths[0, 0, r]
            which = jnp.maximum(length - SHORTEST, 0)
            at = pl.ds(pl.multiple_of(r * width, width), width)
            at8 = pl.ds(pl.multiple_of(r * 8, 8), 8)
            raw_force[at8, :] = jnp.where(blocks8[i], force_t[which], 0.0)
            extent = jnp.full((width, 128), length, jnp.int32)
            live = kx < extent
            extent = extent[:8].astype(F32)
            inverse = 1.0 / (extent * extent)
            inverse = jnp.concatenate([inverse] * (width // 8), axis=0)
            c2, gain = factors(kx_sq * inverse + q_cross)
            room_c2[at, :] = c2
            room_gain[at, :] = gain
            room_b[at, :] = jnp.where(live, room_prev[at, :], 0.0)
        return carry

    copies[3].wait()
    copies[12].wait()
    lax.fori_loop(0, batches, room_second, 0)
    for b in range(batches):
        x = raw_force[32 * b : 32 * b + 32, :]
        high = x.astype(BF16).astype(F32)
        low = x - high
        force_l[128 * b : 128 * b + 128, :] = jnp.concatenate([high, high, low, low], axis=0).T.astype(BF16)
    take_col = jnp.broadcast_to(take_row, (8, wide)).T[:, 0:1]
    take_l[...] = jnp.where(iota((wide, slots), 1) == take_col, 1.0, 0.0).astype(BF16)

    diff = hall_get(2)
    hall_respond(2, 1, diff)
    hall_put(3)
    room_step(0)
    copies[7].wait()
    chunks(accumulate_early, 4)
    hall_get(3)
    chunks(accumulate_last, 4)

    parts = 2
    part_b = part_y // parts

    ring = slabs // 2
    chip = column // 2
    core = lax.rem(column, 2)
    relayed = ring == 8

    def column_of(hops, k):
        return 2 * lax.rem(chip + hops + ring, ring) + k

    def a2a_copy(h, hops, k, source_core):
        peer = column_of(hops, k)
        return pltpu.make_async_remote_copy(
            src_ref=a2a_send.at[pl.ds(part_b * h, part_b), pl.ds(pl.multiple_of(peer * part_x, part_x), part_x), :],
            dst_ref=a2a_recv.at[pl.ds(column * part_y + part_b * h, part_b)],
            send_sem=a2a_ssem.at[h, 2 * hops + k],
            recv_sem=a2a_rsem.at[h, 2 * hops + source_core],
            device_id=(me, peer),
            device_id_type=MESH,
        )

    def relay_copy(h):
        far = pl.multiple_of(column_of(ring // 2, 0) * part_x, 2 * part_x)
        return pltpu.make_async_remote_copy(
            src_ref=a2a_send.at[pl.ds(part_b * h, part_b), pl.ds(far, 2 * part_x), :],
            dst_ref=relay.at[h],
            send_sem=relay_sem.at[h, 0],
            recv_sem=relay_sem.at[h, 1],
            device_id=(me, column_of(1 - 2 * h, core)),
            device_id_type=MESH,
        )

    def forward_copy(h, k):
        way = 1 - 2 * h
        source = column_of(-way, core)
        return pltpu.make_async_remote_copy(
            src_ref=relay.at[h, :, pl.ds(k * part_x, part_x), :],
            dst_ref=a2a_recv.at[pl.ds(source * part_y + part_b * h, part_b)],
            send_sem=relay_sem.at[h, 2 + k],
            recv_sem=a2a_rsem.at[h, ring + core],
            device_id=(me, column_of(3 * way, k)),
            device_id_type=MESH,
        )

    first_hop = 2 if relayed else 1

    copies[8].wait()
    for h in range(parts):
        for b in range(part_b * h, part_b * h + part_b, 2):
            pair = [stacked(hall_base[:, b + i, :], 0) for i in range(2)]
            y = mm(broad(cosx_t), jnp.concatenate(pair, axis=1))
            a2a_send[b] = y[:, :nz]
            a2a_send[b + 1] = y[:, nz:]

        if relayed:
            relay_copy(h).start()

        def a2a_start(i, carry):
            a2a_copy(h, far_first(i // 2, ring), lax.rem(i, 2), core).start()
            return carry

        lax.fori_loop(2 * first_hop, 2 * ring, a2a_start, 0)
        a2a_copy(h, 0, 1 - core, core).start()

    def z_part_of(x):
        rows = stacked(x.reshape(x.shape[0] * part_x, nz), 1)
        return mm(rows, cosz_t[...]).reshape(x.shape)

    copies[10].wait()
    own = pl.ds(pl.multiple_of(column * part_x, part_x), part_x)
    a2a_recv[pl.ds(column * part_y, part_y)] = z_part_of(a2a_send[:, own, :])

    def take_from(h, hops, kinds):
        spots = []
        for k in kinds:
            a2a_copy(h, hops, k, k).wait_recv()
            spots.append(pl.ds(column_of(-hops, k) * part_y + part_b * h, part_b))
        x = jnp.concatenate([a2a_recv[at] for at in spots], axis=0)
        x = z_part_of(x)
        for i, at in enumerate(spots):
            a2a_recv[at] = x[part_b * i : part_b * (i + 1)]

    def take_half(h):
        def body(i, carry):
            take_from(h, far_first(i, ring), (0, 1))
            return carry

        lax.fori_loop(first_hop, ring, body, 0)
        take_from(h, 0, (1 - core,))
        if relayed:
            take_from(h, ring // 2, (0, 1))

    def room_tables_full(b, carry):
        for i in range(4):
            r = 4 * b + i
            which = jnp.maximum(lengths[0, 0, r] - SHORTEST, 0)
            at = pl.ds(pl.multiple_of(r * width, width), width)
            raw_full[at, :] = jnp.where(blocks[i], room_t[which], 0.0)
        return carry

    copies[13].wait()
    copies[14].wait()
    lax.fori_loop(0, batches, room_tables_full, 0)
    for b in range(batches):
        big = slice(128 * b, 128 * b + 128)
        high, low = split(raw_full[big, :])
        full_l[big, :] = jnp.concatenate([high, high, low], axis=1)

    room_step(1)
    if relayed:
        for h in range(parts):
            relay_copy(h).wait_recv()
            forward_copy(h, 0).start()
            forward_copy(h, 1).start()
    for t in range(STEPS - 1):
        hall_copy(t, 0).wait_send()
        hall_copy(t, 1).wait_send()
    room_step(2)
    hall_copy(3, 0).wait_send()
    hall_copy(3, 1).wait_send()
    take_half(0)
    take_half(1)
    copies[9].wait()
    for x in range(0, part_x, 2):
        pair = jnp.concatenate([stacked(a2a_recv[:, x, :], 0), stacked(a2a_recv[:, x + 1, :], 0)], axis=1)
        y = mm(broad(cosy_t), pair)
        hall_out[x] = y[:, :nz]
        hall_out[x + 1] = y[:, nz:]
    for i in range(8):
        store(0, i).start()

    room_step(3)
    room_sent(3)

    for h in range(parts):

        def a2a_sent(i, carry):
            a2a_copy(h, far_first(i // 2, ring), lax.rem(i, 2), core).wait_send()
            return carry

        lax.fori_loop(2 * first_hop, 2 * ring, a2a_sent, 0)
        a2a_copy(h, 0, 1 - core, core).wait_send()
        if relayed:
            relay_copy(h).wait_send()
            forward_copy(h, 0).wait_send()
            forward_copy(h, 1).wait_send()

    for i in range(8):
        store(0, i).wait()
    for i in range(batches):
        store(1, i).wait()


def hand_on(hall_in, room_in, hall_out, room_out, hall_mid, room_mid, load_sem, store_sem):
    loads, stores = [], []
    for j, (near, mid, far) in enumerate(((hall_in, hall_mid, hall_out), (room_in, room_mid, room_out))):
        size = near.shape[0] // 8
        for i in range(8):
            at = pl.ds(i * size, size)
            loads.append(pltpu.make_async_copy(near.at[at], mid.at[at], load_sem.at[j, i]))
            stores.append(pltpu.make_async_copy(mid.at[at], far.at[at], store_sem.at[j, i]))
    for load in loads:
        load.start()
    for load, store in zip(loads, stores):
        load.wait()
        store.start()
    for store in stores:
        store.wait()


def local(hall_now, hall_prev, room_now, room_prev, room_length, right_neighbor):
    groups = lax.axis_size("grp")
    slabs = lax.axis_size("slab")
    _, nx, part_y, nz = hall_now.shape
    _, _, count, width, cross = room_now.shape
    ny = part_y * slabs
    part_x = nx // slabs
    lanes = nx * part_y
    slots = 16 * groups
    rows = count * width
    inputs = [
        hall_now[0], hall_prev[0], room_now.reshape(rows, cross), room_prev.reshape(rows, cross), right_neighbor,
    ]
    inputs += [jnp.asarray(lane_tiles(t)) for t in hall_tables(nx, ny, nz)]
    inputs += [jnp.asarray(t) for t in room_tables(width)]
    inputs += [jnp.asarray(right_table(np.kron(dct(SY), dct(SZ))))]
    smem = pl.BlockSpec(memory_space=pltpu.SMEM)
    away = pl.BlockSpec(memory_space=pl.ANY)
    dma = pltpu.SemaphoreType.DMA
    results = pl.pallas_call(
        functools.partial(kernel, groups, slabs, count, len(inputs)),
        out_shape=(
            jax.ShapeDtypeStruct((part_x, ny, nz), F32),
            jax.ShapeDtypeStruct((rows, cross), F32),
        ),
        in_specs=[smem] + [away] * len(inputs),
        out_specs=(away, away),
        scratch_shapes=[pltpu.VMEM(x.shape, x.dtype) for x in inputs]
        + [
            pltpu.VMEM((nx, part_y, nz), F32),
            pltpu.VMEM((nx, part_y, nz), F32),
            pltpu.VMEM((nx, part_y, nz), F32),
            pltpu.VMEM((STEPS, 8, lanes), F32),
            pltpu.VMEM((STEPS - 1, 48, lanes), F32),
            pltpu.VMEM((STEPS, 8, lanes), F32),
            pltpu.VMEM((8, lanes), F32),
            pltpu.VMEM((STEPS, 2, 3, lanes // 128, 128), F32),
            pltpu.VMEM((STEPS, 2, 3, lanes // 128, 128), F32),
            pltpu.VMEM((part_y, nx, nz), F32),
            pltpu.VMEM((ny, part_x, nz), F32),
            pltpu.VMEM((rows, cross), F32),
            pltpu.VMEM((rows, cross), F32),
            pltpu.VMEM((rows, cross), F32),
            pltpu.VMEM((rows, cross), F32),
            pltpu.VMEM((8 * count, cross), F32),
            pltpu.VMEM((8 * count, 4 * width), F32),
            pltpu.VMEM((8 * count, 4 * width), F32),
            pltpu.VMEM((rows, 4 * width), F32),
            pltpu.VMEM((8 * count, 12 * width), BF16),
            pltpu.VMEM((rows, 128), BF16),
            pltpu.VMEM((rows, 12 * width), BF16),
            pltpu.VMEM((slots, 8 * count), BF16),
            pltpu.VMEM((8 * count, slots), BF16),
            pltpu.VMEM((STEPS, groups, 12, 128), F32),
            pltpu.VMEM((STEPS, groups - 1, 12, 128), F32),
            pltpu.VMEM((part_x, ny, nz), F32),
            pltpu.VMEM((rows, cross), F32),
            pltpu.VMEM((2, part_y // 2, 2 * part_x, nz), F32),
            dma((len(inputs),)),
            dma((2, 8)),
            dma((STEPS, 2)),
            dma((STEPS, 2)),
            dma((2, slabs)),
            dma((2, slabs)),
            dma((2, 4)),
            dma((STEPS,)),
            dma((STEPS,)),
        ],
        compiler_params=pltpu.CompilerParams(
            collective_id=0, has_side_effects=True, vmem_limit_bytes=60 * 1024 * 1024
        ),
    )(room_length, *inputs)
    hall_pressure, room_pressure = pl.pallas_call(
        hand_on,
        out_shape=tuple(jax.ShapeDtypeStruct(x.shape, x.dtype) for x in results),
        in_specs=[away] * 2,
        out_specs=(away, away),
        scratch_shapes=[pltpu.VMEM(x.shape, x.dtype) for x in results] + [dma((2, 8)), dma((2, 8))],
        compiler_params=pltpu.CompilerParams(vmem_limit_bytes=60 * 1024 * 1024),
    )(*results)
    return (hall_pressure[None], room_pressure.reshape(1, 1, count, width, cross))


def solution(mesh):
    in_specs = (
        P("grp", None, "slab", None),
        P("grp", None, "slab", None),
        P("grp", "slab", None, None, None),
        P("grp", "slab", None, None, None),
        P("grp", "slab", None),
        P("slab", None),
    )
    out_specs = (P("grp", "slab", None, None), P("grp", "slab", None, None, None))
    return jax.shard_map(local, mesh=mesh, in_specs=in_specs, out_specs=out_specs, check_vma=False)
```

```python
import functools
import math

import jax
import jax.numpy as jnp
import ml_dtypes
import numpy as np
from jax import lax
from jax.experimental import pallas as pl
from jax.experimental.pallas import tpu as pltpu
from jax.sharding import PartitionSpec as P

SY = 8
SZ = 16
STEPS = 4
SHORTEST = 16
TIME_STEP = 0.4
SCALE = (TIME_STEP * math.pi) ** 2
STENCIL = np.array([[270, -27, 2], [-27, 2, 0], [2, 0, 0]], np.float64) / 180.0
F32 = jnp.float32
BF16 = jnp.bfloat16
MESH = pl.DeviceIdType.MESH


def dct(length):
    k = np.arange(length)[:, None]
    i = np.arange(length)[None, :]
    w = np.where(k == 0, np.sqrt(1.0 / length), np.sqrt(2.0 / length))
    return w * np.cos(np.pi * k * (2 * i + 1) / (2 * length))


def halves(x):
    high = x.astype(np.float32).astype(ml_dtypes.bfloat16)
    low = (x - high.astype(np.float64)).astype(ml_dtypes.bfloat16)
    return high, low


def left_table(x):
    high, low = halves(x)
    return np.concatenate([high, high, low], axis=1)


def right_table(x):
    high, low = halves(x)
    return np.concatenate([high, high, low], axis=0)


def face_rows(table):
    length = table.shape[0]
    sign = np.where(np.arange(length) % 2 == 0, 1.0, -1.0)
    low = table[:, :3].T
    forced = STENCIL.T @ low
    zero = np.zeros((2, length))
    return (
        np.concatenate([low, low * sign, zero], axis=0),
        np.concatenate([forced, forced * sign, zero], axis=0),
    )


def hall_tables(nx, ny, nz):
    faces, forced = face_rows(dct(nz))
    high, low = halves(faces)
    spread = np.concatenate(
        [np.concatenate([high, high], axis=1), np.concatenate([low, 0 * low], axis=1)], axis=0
    )
    pairs = np.concatenate([forced[k : k + 1] * faces for k in range(6)], axis=0)
    both = np.concatenate(halves(pairs), axis=0)
    respond = np.concatenate(
        [np.concatenate([both, 0 * both], axis=1), np.concatenate([0 * both, both], axis=1)], axis=0
    )
    high, low = halves(forced)
    outer = np.concatenate([high, high, low, low], axis=0)
    blank = np.zeros((32, 384), ml_dtypes.bfloat16)
    outer = np.concatenate([np.concatenate([blank[:, : 128 * t], outer, blank[:, 128 * t :]], axis=1) for t in range(4)], axis=0)
    return spread, respond, outer, left_table(dct(nx).T), left_table(dct(ny).T), right_table(dct(nz))


def room_tables(width):
    faces, forced, full = [], [], []
    for length in range(SHORTEST, width + 1):
        table = np.zeros((width, width))
        table[:length, :length] = dct(length)
        low, high = face_rows(table[:, :])
        faces.append(np.tile(low, (1, 4)))
        forced.append(np.tile(high, (1, 4)))
        full.append(np.tile(table.T, (1, 4)))
    return [np.stack(t).astype(np.float32) for t in (faces, forced, full)]


def factors(q):
    h = jnp.full_like(q, 2.0 / math.factorial(16))
    for n in range(6, -1, -1):
        h = 2.0 / math.factorial(2 * n + 2) - h * q
    return 2.0 - q * h, (TIME_STEP * TIME_STEP) * h


def mm(a, b):
    return jnp.dot(a, b, preferred_element_type=F32)


def mm_nt(a, b):
    return lax.dot_general(a, b, (((1,), (1,)), ((), ())), preferred_element_type=F32)


def split(x):
    high = x.astype(BF16)
    return high, (x - high.astype(F32)).astype(BF16)


def stacked(x, axis):
    high, low = split(x)
    return jnp.concatenate([high, low, high], axis=axis)


def lane_tiles(table):
    if table.shape[1] == 128:
        return table
    tile = math.gcd(table.shape[1], 128)
    return table.reshape(table.shape[0], -1, tile).transpose(1, 0, 2)


def broad(ref, tiles=None, rows=None):
    tiles = ref.shape[0] if tiles is None else tiles
    return jnp.concatenate([ref[j, :rows] for j in range(tiles)], axis=1)


def iota(shape, dim):
    return lax.broadcasted_iota(jnp.int32, shape, dim).astype(F32)


def total(mask, values, axis):
    return jnp.sum(jnp.where(mask, values, 0.0), axis=axis, keepdims=True)


def kernel(
    groups, slabs, count, loads, *refs,
):
    lengths, sources, refs = refs[0], refs[1 : 1 + loads], refs[1 + loads :]
    hall_far, room_far = refs[:2]
    landed, refs = refs[2 : 2 + loads], refs[2 + loads :]
    (
        hall_now, hall_prev, room_now, room_prev, ids,
        spread_t, respond_t, outer_t, cosx_t, cosy_t, cosz_t, face_t, force_t, room_t, cross_t,
    ) = landed
    (
        hall_c2, hall_gain, hall_base, hall_faces, hall_resp, hall_diff, hall_other,
        hall_send, hall_recv, a2a_send, a2a_recv,
        room_c2, room_gain, room_a, room_b, room_faces, raw_faces, raw_force, raw_full,
        face_l, force_l, full_l, pack_l, take_l, room_send, room_recv, hall_out, room_out, relay,
        load_sem, store_sem, hall_ssem, hall_rsem, a2a_ssem, a2a_rsem, relay_sem, room_ssem, room_rsem,
    ) = refs
    me = lax.axis_index("grp")
    column = lax.axis_index("slab")
    nx, part_y, nz = hall_now.shape
    ny = part_y * slabs
    part_x = nx // slabs
    lanes = nx * part_y
    width = room_now.shape[0] // count
    batches = count // 4

    copies = [pltpu.make_async_copy(sources[i], landed[i], load_sem.at[i]) for i in range(loads)]
    order = [0, 5, 2, 4, 11, 1, 6, 3, 12, 7, 13, 8, 10, 9, 14]
    for i in order:
        copies[i].start()

    barrier = pltpu.get_barrier_semaphore()

    def greet_grp(step, carry):
        pl.semaphore_signal(
            barrier, inc=1, device_id=(lax.rem(me + step, groups), column), device_id_type=MESH
        )
        return carry

    def greet_slab(step, carry):
        pl.semaphore_signal(
            barrier, inc=1, device_id=(me, lax.rem(column + step, slabs)), device_id_type=MESH
        )
        return carry

    lax.fori_loop(1, groups, greet_grp, 0)
    lax.fori_loop(1, slabs, greet_slab, 0)
    hall_other[...] = jnp.zeros_like(hall_other)

    chunk = 256
    deep = chunk // part_y

    def chunks(body, many):
        def several(i, carry):
            for j in range(many):
                body(i * many + j)
            return carry

        lax.fori_loop(0, lanes // chunk // many, several, 0)

    def spread_of(x):
        high, low = split(x)
        both = mm_nt(broad(spread_t), jnp.concatenate([high, low], axis=1))
        return both[:8] + both[8:]

    def first_faces(i):
        x = hall_now[pl.ds(i * deep, deep)].reshape(chunk, nz)
        hall_faces[0, :, pl.ds(pl.multiple_of(i * chunk, chunk), chunk)] = spread_of(x)

    copies[0].wait()
    copies[5].wait()
    chunks(first_faces, 4)

    def hall_copy(t, side):
        peer = lax.rem(me + (1 if side == 0 else groups - 1), groups)
        return pltpu.make_async_remote_copy(
            src_ref=hall_send.at[t, side],
            dst_ref=hall_recv.at[t, side],
            send_sem=hall_ssem.at[t, side],
            recv_sem=hall_rsem.at[t, side],
            device_id=(peer, column),
            device_id_type=MESH,
        )

    def hall_put(t):
        own = hall_faces[t]
        for k in range(3):
            for j in range(lanes // 128):
                cut = slice(128 * j, 128 * j + 128)
                hall_send[t, 0, k, j : j + 1, :] = own[3 + k : 4 + k, cut]
                hall_send[t, 1, k, j : j + 1, :] = own[k : k + 1, cut]
        hall_copy(t, 0).start()
        hall_copy(t, 1).start()

    def hall_get(t):
        hall_copy(t, 0).wait_recv()
        hall_copy(t, 1).wait_recv()
        for k in range(3):
            for j in range(lanes // 128):
                cut = slice(128 * j, 128 * j + 128)
                hall_other[k : k + 1, cut] = hall_recv[t, 0, k, j : j + 1, :]
                hall_other[3 + k : 4 + k, cut] = hall_recv[t, 1, k, j : j + 1, :]
        row = lax.broadcasted_iota(jnp.int32, (8, lanes), 0)
        first = jnp.where(me > 0, 0, 3)
        last = jnp.where(me < groups - 1, 6, 3)
        diff = jnp.where((row >= first) & (row < last), hall_other[...] - hall_faces[t], 0.0)
        hall_diff[t] = diff
        return diff

    def hall_respond(t, lag, diff):
        acc = hall_faces[t + lag]
        for k in range(6):
            acc = acc + hall_resp[lag - 1, 8 * k : 8 * k + 8, :] * diff[k : k + 1, :]
        hall_faces[t + lag] = acc

    def terms(e):
        high = e.astype(BF16).astype(F32)
        low = e - high
        return jnp.concatenate([high, low, high, low], axis=0)

    def accumulate(i):
        at = pl.ds(i * deep, deep)
        cols = pl.ds(pl.multiple_of(i * chunk, chunk), chunk)
        e = jnp.concatenate([terms(hall_diff[t, :, cols]) for t in range(STEPS)], axis=0).T.astype(BF16)
        forced = mm(e, broad(outer_t))
        c2 = hall_c2[at]
        f0, f1, f2, f3 = [forced[:, 128 * t : 128 * t + 128].reshape(deep, part_y, nz) for t in range(STEPS)]
        square = c2 * c2
        weighted = c2 * ((square - 2.0) * f0 + f2) + (square - 1.0) * f1 + f3
        hall_base[at] = hall_base[at] + hall_gain[at] * weighted

    pl.semaphore_wait(barrier, groups + slabs - 2)
    hall_put(0)


    lane = lax.broadcasted_iota(jnp.int32, (width, 128), 1)
    shift = int(math.log2(width))
    blocks = [(lane >> shift) == i for i in range(4)]
    blocks8 = [block[:8] for block in blocks]
    kx = lax.broadcasted_iota(jnp.int32, (width, 128), 0)

    def room_first(b, carry):
        for i in range(4):
            r = 4 * b + i
            length = lengths[0, 0, r]
            which = jnp.maximum(length - SHORTEST, 0)
            at = pl.ds(pl.multiple_of(r * width, width), width)
            at8 = pl.ds(pl.multiple_of(r * 8, 8), 8)
            raw_faces[at8, :] = jnp.where(blocks8[i], face_t[which], 0.0)
            room_a[at, :] = jnp.where(kx < jnp.full((width, 128), length, jnp.int32), room_now[at, :], 0.0)
        return carry

    copies[2].wait()
    copies[4].wait()
    copies[11].wait()
    lax.fori_loop(0, batches, room_first, 0)
    for b in range(batches):
        cut = slice(32 * b, 32 * b + 32)
        big = slice(128 * b, 128 * b + 128)
        high, low = split(raw_faces[cut, :])
        face_l[cut, :] = jnp.concatenate([high, high, low], axis=1)
        room_faces[cut, :] = mm(face_l[cut, :], stacked(room_a[big, :], 0))

    bits = int(math.log2(count))
    wide = 8 * count
    span = ids.shape[1]
    row_lanes = min(128, span)
    flat = jnp.concatenate(
        [ids[0:1, row_lanes * j : row_lanes * (j + 1)] for j in range(span // row_lanes)], axis=0
    )
    device = (flat >> bits).astype(F32)
    slot = (flat & (count - 1)).astype(F32)
    lane_i = lax.broadcasted_iota(jnp.int32, (count, wide), 1)
    p_col = iota((count, wide), 0)
    p_row = (lane_i >> 3).astype(F32)
    f_row = (lane_i & 7).astype(F32)
    expand = lax.broadcasted_iota(jnp.int32, (row_lanes, wide), 1) >> 3
    expand = jnp.where(expand == lax.broadcasted_iota(jnp.int32, (row_lanes, wide), 0), 1.0, 0.0)
    s_row = mm(device.astype(BF16), expand.astype(BF16))[0:1]
    s_col = device.T[:count, 0:1]
    same = s_col == s_row
    rank_row = total(same & (p_col < p_row), 1.0, 0)
    rank_col = total(same & (p_row < p_col) & (f_row == 0.0), 1.0, 1)
    home = me.astype(F32) - s_col
    home = jnp.where(home < 0.0, home + groups, home)
    per_row = row_lanes // count
    home = jnp.concatenate([home] * per_row, axis=0)
    shape = (row_lanes, span // row_lanes)
    group = per_row * lax.broadcasted_iota(jnp.int32, shape, 1)
    group = group + (lax.broadcasted_iota(jnp.int32, shape, 0) >> bits)
    landing = total(group.astype(F32) == home, slot.T, 1)
    landing = sum(landing[count * i : count * (i + 1)] for i in range(per_row))
    match = landing == p_row
    ls_row = total(match, jnp.broadcast_to(s_col, (count, wide)), 0)
    lr_row = total(match, jnp.broadcast_to(rank_col, (count, wide)), 0)

    def back(s):
        return jnp.where(s == 0.0, 0.0, groups - s)

    f = f_row[0:1]
    layer = jnp.where(f < 3.0, f, f - 3.0)
    pack_row = jnp.where(
        f < 3.0, 16.0 * back(ls_row) + 6.0 + 3.0 * lr_row + layer, 16.0 * s_row + 3.0 * rank_row + layer
    )
    take_row = jnp.where(
        f < 3.0, 16.0 * ls_row + 3.0 * lr_row + layer, 16.0 * back(s_row) + 6.0 + 3.0 * rank_row + layer
    )
    pack_row = jnp.where(f < 6.0, pack_row, -1.0)
    take_row = jnp.where(f < 6.0, take_row, -1.0)
    slots = 16 * groups
    pack_l[...] = jnp.where(iota((slots, wide), 0) == pack_row, 1.0, 0.0).astype(BF16)

    def room_copy(t, step):
        return pltpu.make_async_remote_copy(
            src_ref=room_send.at[t, step],
            dst_ref=room_recv.at[t, step - 1],
            send_sem=room_ssem.at[t],
            recv_sem=room_rsem.at[t],
            device_id=(lax.rem(me + step, groups), column),
            device_id_type=MESH,
        )

    def room_all(t):
        return pltpu.make_async_remote_copy(
            src_ref=room_send.at[t, pl.ds(1, groups - 1)],
            dst_ref=room_recv.at[t],
            send_sem=room_ssem.at[t],
            recv_sem=room_rsem.at[t],
            device_id=(lax.rem(me + 1, groups), column),
            device_id_type=MESH,
        )

    def far_first(i, count):
        half = i // 2
        return count // 2 + jnp.where(lax.rem(i, 2) == 0, half, -half)

    def two_parts(x):
        return jnp.concatenate(split(x), axis=1)

    def room_put(t):
        packed = mm(pack_l[...], two_parts(room_faces[...]))
        packed = packed[:, :128] + packed[:, 128:]
        room_send[t] = packed.reshape(groups, 16, 128)[:, :12, :]

        room_copy(t, groups // 2).start()

        def body(i, carry):
            room_copy(t, groups // 2 + i).start()
            room_copy(t, groups // 2 - i).start()
            return carry

        lax.fori_loop(1, groups // 2, body, 0)

    def store(which, i):
        near, far = ((hall_out, hall_far), (room_out, room_far))[which]
        size = near.shape[0] // (8 if which == 0 else batches)
        at = pl.ds(i * size, size)
        return pltpu.make_async_copy(near.at[at], far.at[at], store_sem.at[which, i])

    def room_get(t):
        room_all(t).wait_recv()
        got = jnp.concatenate([room_send[t, 0:1], room_recv[t]], axis=0)
        got = jnp.concatenate([got, jnp.zeros((groups, 4, 128), F32)], axis=1).reshape(slots, 128)
        other = mm(take_l[...], two_parts(got))
        return other[:, :128] + other[:, 128:] - room_faces[...]

    def room_sent(t):
        room_all(t).wait_send()

    def room_step(t):
        diff = room_get(t)
        now, prev = (room_a, room_b) if t % 2 == 0 else (room_b, room_a)
        for b in range(batches):
            cut = slice(32 * b, 32 * b + 32)
            big = slice(128 * b, 128 * b + 128)
            high, low = split(diff[cut])
            forced = mm(force_l[big, :], jnp.concatenate([high, low, high, low], axis=0))
            fresh = room_c2[big, :] * now[big, :] - prev[big, :] + room_gain[big, :] * forced
            if t < STEPS - 1:
                prev[big, :] = fresh
                room_faces[cut, :] = mm(face_l[cut, :], stacked(fresh, 0))
            else:
                x = mm(full_l[big, :], stacked(fresh, 0))
                room_out[big, :] = mm(stacked(x, 1), cross_t[...])
                store(1, b).start()
        if t < STEPS - 1:
            room_put(t + 1)
            room_sent(t)

    room_put(0)

    yz = lax.broadcasted_iota(jnp.int32, (part_y, nz), 0) + column * part_y
    ky_f = yz.astype(F32)
    kz_f = iota((part_y, nz), 1)
    q_yz = (SCALE / ny**2) * (ky_f * ky_f) + (SCALE / nz**2) * (kz_f * kz_f)

    def prepare_first(i):
        at = pl.ds(i * deep, deep)
        cols = pl.ds(pl.multiple_of(i * chunk, chunk), chunk)
        a = (lax.broadcasted_iota(jnp.int32, (deep, part_y, nz), 0) + i * deep).astype(F32)
        c2, gain = factors((SCALE / nx**2) * (a * a) + q_yz[None])
        hall_c2[at] = c2
        hall_gain[at] = gain
        fresh = c2 * hall_now[at] - hall_prev[at]
        hall_base[at] = fresh
        hall_faces[1, :, cols] = spread_of(fresh.reshape(chunk, nz))
        both = mm_nt(respond_t[0, :96], gain.reshape(chunk, nz).astype(BF16))
        hall_resp[0, :, cols] = both[:48] + both[48:]

    def prepare_second(i):
        at = pl.ds(i * deep, deep)
        cols = pl.ds(pl.multiple_of(i * chunk, chunk), chunk)
        c2 = hall_c2[at]
        gain = hall_gain[at]
        m2 = c2 * hall_base[at] - hall_now[at]
        hall_faces[2, :, cols] = spread_of(m2.reshape(chunk, nz))
        s2 = gain * c2
        s3 = s2 * c2 - gain
        both = [s.reshape(chunk, nz).astype(BF16) for s in (s2, s3)]
        both = mm_nt(broad(respond_t), jnp.concatenate(both, axis=1))
        hall_resp[1, :, cols] = both[:48] + both[48:96]
        hall_resp[2, :, cols] = both[96:144] + both[144:]

    def prepare_third(i):
        at = pl.ds(i * deep, deep)
        cols = pl.ds(pl.multiple_of(i * chunk, chunk), chunk)
        c2 = hall_c2[at]
        m1 = hall_base[at]
        m2 = c2 * m1 - hall_now[at]
        m3 = c2 * m2 - m1
        hall_base[at] = c2 * m3 - m2
        hall_faces[3, :, cols] = spread_of(m3.reshape(chunk, nz))

    copies[1].wait()
    copies[6].wait()
    chunks(prepare_first, 2)
    diff = hall_get(0)
    hall_respond(0, 1, diff)
    hall_put(1)
    chunks(prepare_second, 2)
    hall_respond(0, 2, diff)
    diff = hall_get(1)
    hall_respond(1, 1, diff)
    hall_put(2)
    chunks(prepare_third, 2)
    hall_respond(0, 3, hall_diff[0])
    hall_respond(1, 2, diff)

    q_cross = (lane >> int(math.log2(SZ))).astype(F32) * (1.0 / SY)
    q_cross = SCALE * (q_cross * q_cross)
    z_part = (lane & (SZ - 1)).astype(F32) * (1.0 / SZ)
    q_cross = q_cross + SCALE * (z_part * z_part)
    kx_f = kx.astype(F32)
    kx_sq = SCALE * (kx_f * kx_f)

    def room_second(b, carry):
        for i in range(4):
            r = 4 * b + i
            length = lengths[0, 0, r]
            which = jnp.maximum(length - SHORTEST, 0)
            at = pl.ds(pl.multiple_of(r * width, width), width)
            at8 = pl.ds(pl.multiple_of(r * 8, 8), 8)
            raw_force[at8, :] = jnp.where(blocks8[i], force_t[which], 0.0)
            extent = jnp.full((width, 128), length, jnp.int32)
            live = kx < extent
            extent = extent[:8].astype(F32)
            inverse = 1.0 / (extent * extent)
            inverse = jnp.concatenate([inverse] * (width // 8), axis=0)
            c2, gain = factors(kx_sq * inverse + q_cross)
            room_c2[at, :] = c2
            room_gain[at, :] = gain
            room_b[at, :] = jnp.where(live, room_prev[at, :], 0.0)
        return carry

    copies[3].wait()
    copies[12].wait()
    lax.fori_loop(0, batches, room_second, 0)
    for b in range(batches):
        x = raw_force[32 * b : 32 * b + 32, :]
        high = x.astype(BF16).astype(F32)
        low = x - high
        force_l[128 * b : 128 * b + 128, :] = jnp.concatenate([high, high, low, low], axis=0).T.astype(BF16)
    take_col = jnp.broadcast_to(take_row, (8, wide)).T[:, 0:1]
    take_l[...] = jnp.where(iota((wide, slots), 1) == take_col, 1.0, 0.0).astype(BF16)

    diff = hall_get(2)
    hall_respond(2, 1, diff)
    hall_put(3)
    room_step(0)
    copies[7].wait()
    hall_get(3)
    chunks(accumulate, 4)

    parts = 2
    part_b = part_y // parts

    ring = slabs // 2
    chip = column // 2
    core = lax.rem(column, 2)
    relayed = ring == 8

    def column_of(hops, k):
        return 2 * lax.rem(chip + hops + ring, ring) + k

    def a2a_copy(h, hops, k, source_core):
        peer = column_of(hops, k)
        return pltpu.make_async_remote_copy(
            src_ref=a2a_send.at[pl.ds(part_b * h, part_b), pl.ds(pl.multiple_of(peer * part_x, part_x), part_x), :],
            dst_ref=a2a_recv.at[pl.ds(column * part_y + part_b * h, part_b)],
            send_sem=a2a_ssem.at[h, 2 * hops + k],
            recv_sem=a2a_rsem.at[h, 2 * hops + source_core],
            device_id=(me, peer),
            device_id_type=MESH,
        )

    def relay_copy(h):
        far = pl.multiple_of(column_of(ring // 2, 0) * part_x, 2 * part_x)
        return pltpu.make_async_remote_copy(
            src_ref=a2a_send.at[pl.ds(part_b * h, part_b), pl.ds(far, 2 * part_x), :],
            dst_ref=relay.at[h],
            send_sem=relay_sem.at[h, 0],
            recv_sem=relay_sem.at[h, 1],
            device_id=(me, column_of(1 - 2 * h, core)),
            device_id_type=MESH,
        )

    def forward_copy(h, k):
        way = 1 - 2 * h
        source = column_of(-way, core)
        return pltpu.make_async_remote_copy(
            src_ref=relay.at[h, :, pl.ds(k * part_x, part_x), :],
            dst_ref=a2a_recv.at[pl.ds(source * part_y + part_b * h, part_b)],
            send_sem=relay_sem.at[h, 2 + k],
            recv_sem=a2a_rsem.at[h, ring + core],
            device_id=(me, column_of(3 * way, k)),
            device_id_type=MESH,
        )

    first_hop = 2 if relayed else 1

    copies[8].wait()
    for h in range(parts):
        for b in range(part_b * h, part_b * h + part_b, 2):
            pair = [stacked(hall_base[:, b + i, :], 0) for i in range(2)]
            y = mm(broad(cosx_t), jnp.concatenate(pair, axis=1))
            a2a_send[b] = y[:, :nz]
            a2a_send[b + 1] = y[:, nz:]

        if relayed:
            relay_copy(h).start()

        def a2a_start(i, carry):
            a2a_copy(h, far_first(i, ring), 0, core).start()
            a2a_copy(h, far_first(i, ring), 1, core).start()
            return carry

        lax.fori_loop(first_hop, ring, a2a_start, 0)
        a2a_copy(h, 0, 1 - core, core).start()

    def z_part_of(x):
        rows = stacked(x.reshape(x.shape[0] * part_x, nz), 1)
        return mm(rows, cosz_t[...]).reshape(x.shape)

    copies[10].wait()
    own = pl.ds(pl.multiple_of(column * part_x, part_x), part_x)
    a2a_recv[pl.ds(column * part_y, part_y)] = z_part_of(a2a_send[:, own, :])

    def take_from(h, hops, kinds):
        spots = []
        for k in kinds:
            a2a_copy(h, hops, k, k).wait_recv()
            spots.append(pl.ds(column_of(-hops, k) * part_y + part_b * h, part_b))
        x = jnp.concatenate([a2a_recv[at] for at in spots], axis=0)
        x = z_part_of(x)
        for i, at in enumerate(spots):
            a2a_recv[at] = x[part_b * i : part_b * (i + 1)]

    def take_half(h):
        def body(i, carry):
            take_from(h, far_first(i, ring), (0, 1))
            return carry

        lax.fori_loop(first_hop, ring, body, 0)
        take_from(h, 0, (1 - core,))
        if relayed:
            take_from(h, ring // 2, (0, 1))

    def room_tables_full(b, carry):
        for i in range(4):
            r = 4 * b + i
            which = jnp.maximum(lengths[0, 0, r] - SHORTEST, 0)
            at = pl.ds(pl.multiple_of(r * width, width), width)
            raw_full[at, :] = jnp.where(blocks[i], room_t[which], 0.0)
        return carry

    copies[13].wait()
    copies[14].wait()
    lax.fori_loop(0, batches, room_tables_full, 0)
    for b in range(batches):
        big = slice(128 * b, 128 * b + 128)
        high, low = split(raw_full[big, :])
        full_l[big, :] = jnp.concatenate([high, high, low], axis=1)

    room_step(1)
    if relayed:
        for h in range(parts):
            relay_copy(h).wait_recv()
            forward_copy(h, 0).start()
            forward_copy(h, 1).start()
    for t in range(STEPS - 1):
        hall_copy(t, 0).wait_send()
        hall_copy(t, 1).wait_send()
    room_step(2)
    hall_copy(3, 0).wait_send()
    hall_copy(3, 1).wait_send()
    take_half(0)
    take_half(1)
    copies[9].wait()
    for x in range(0, part_x, 2):
        pair = jnp.concatenate([stacked(a2a_recv[:, x, :], 0), stacked(a2a_recv[:, x + 1, :], 0)], axis=1)
        y = mm(broad(cosy_t), pair)
        hall_out[x] = y[:, :nz]
        hall_out[x + 1] = y[:, nz:]
    for i in range(8):
        store(0, i).start()

    room_step(3)
    room_sent(3)

    for h in range(parts):

        def a2a_sent(i, carry):
            a2a_copy(h, far_first(i // 2, ring), lax.rem(i, 2), core).wait_send()
            return carry

        lax.fori_loop(2 * first_hop, 2 * ring, a2a_sent, 0)
        a2a_copy(h, 0, 1 - core, core).wait_send()
        if relayed:
            relay_copy(h).wait_send()
            forward_copy(h, 0).wait_send()
            forward_copy(h, 1).wait_send()

    for i in range(8):
        store(0, i).wait()
    for i in range(batches):
        store(1, i).wait()


def hand_on(hall_in, room_in, hall_out, room_out, hall_mid, room_mid, load_sem, store_sem):
    loads, stores = [], []
    for j, (near, mid, far) in enumerate(((hall_in, hall_mid, hall_out), (room_in, room_mid, room_out))):
        size = near.shape[0] // 4
        for i in range(4):
            at = pl.ds(i * size, size)
            loads.append(pltpu.make_async_copy(near.at[at], mid.at[at], load_sem.at[j, i]))
            stores.append(pltpu.make_async_copy(mid.at[at], far.at[at], store_sem.at[j, i]))
    for load in loads:
        load.start()
    for load, store in zip(loads, stores):
        load.wait()
        store.start()
    for store in stores:
        store.wait()


def local(hall_now, hall_prev, room_now, room_prev, room_length, right_neighbor):
    groups = lax.axis_size("grp")
    slabs = lax.axis_size("slab")
    _, nx, part_y, nz = hall_now.shape
    _, _, count, width, cross = room_now.shape
    ny = part_y * slabs
    part_x = nx // slabs
    lanes = nx * part_y
    slots = 16 * groups
    rows = count * width
    inputs = [
        hall_now[0], hall_prev[0], room_now.reshape(rows, cross), room_prev.reshape(rows, cross), right_neighbor,
    ]
    inputs += [jnp.asarray(lane_tiles(t)) for t in hall_tables(nx, ny, nz)]
    inputs += [jnp.asarray(t) for t in room_tables(width)]
    inputs += [jnp.asarray(right_table(np.kron(dct(SY), dct(SZ))))]
    smem = pl.BlockSpec(memory_space=pltpu.SMEM)
    away = pl.BlockSpec(memory_space=pl.ANY)
    dma = pltpu.SemaphoreType.DMA
    results = pl.pallas_call(
        functools.partial(kernel, groups, slabs, count, len(inputs)),
        out_shape=(
            jax.ShapeDtypeStruct((part_x, ny, nz), F32),
            jax.ShapeDtypeStruct((rows, cross), F32),
        ),
        in_specs=[smem] + [away] * len(inputs),
        out_specs=(away, away),
        scratch_shapes=[pltpu.VMEM(x.shape, x.dtype) for x in inputs]
        + [
            pltpu.VMEM((nx, part_y, nz), F32),
            pltpu.VMEM((nx, part_y, nz), F32),
            pltpu.VMEM((nx, part_y, nz), F32),
            pltpu.VMEM((STEPS, 8, lanes), F32),
            pltpu.VMEM((STEPS - 1, 48, lanes), F32),
            pltpu.VMEM((STEPS, 8, lanes), F32),
            pltpu.VMEM((8, lanes), F32),
            pltpu.VMEM((STEPS, 2, 3, lanes // 128, 128), F32),
            pltpu.VMEM((STEPS, 2, 3, lanes // 128, 128), F32),
            pltpu.VMEM((part_y, nx, nz), F32),
            pltpu.VMEM((ny, part_x, nz), F32),
            pltpu.VMEM((rows, cross), F32),
            pltpu.VMEM((rows, cross), F32),
            pltpu.VMEM((rows, cross), F32),
            pltpu.VMEM((rows, cross), F32),
            pltpu.VMEM((8 * count, cross), F32),
            pltpu.VMEM((8 * count, 4 * width), F32),
            pltpu.VMEM((8 * count, 4 * width), F32),
            pltpu.VMEM((rows, 4 * width), F32),
            pltpu.VMEM((8 * count, 12 * width), BF16),
            pltpu.VMEM((rows, 128), BF16),
            pltpu.VMEM((rows, 12 * width), BF16),
            pltpu.VMEM((slots, 8 * count), BF16),
            pltpu.VMEM((8 * count, slots), BF16),
            pltpu.VMEM((STEPS, groups, 12, 128), F32),
            pltpu.VMEM((STEPS, groups - 1, 12, 128), F32),
            pltpu.VMEM((part_x, ny, nz), F32),
            pltpu.VMEM((rows, cross), F32),
            pltpu.VMEM((2, part_y // 2, 2 * part_x, nz), F32),
            dma((len(inputs),)),
            dma((2, 8)),
            dma((STEPS, 2)),
            dma((STEPS, 2)),
            dma((2, slabs)),
            dma((2, slabs)),
            dma((2, 4)),
            dma((STEPS,)),
            dma((STEPS,)),
        ],
        compiler_params=pltpu.CompilerParams(
            collective_id=0, has_side_effects=True, vmem_limit_bytes=60 * 1024 * 1024
        ),
    )(room_length, *inputs)
    hall_pressure, room_pressure = pl.pallas_call(
        hand_on,
        out_shape=tuple(jax.ShapeDtypeStruct(x.shape, x.dtype) for x in results),
        in_specs=[away] * 2,
        out_specs=(away, away),
        scratch_shapes=[pltpu.VMEM(x.shape, x.dtype) for x in results] + [dma((2, 4)), dma((2, 4))],
        compiler_params=pltpu.CompilerParams(vmem_limit_bytes=60 * 1024 * 1024),
    )(*results)
    return (hall_pressure[None], room_pressure.reshape(1, 1, count, width, cross))


def solution(mesh):
    in_specs = (
        P("grp", None, "slab", None),
        P("grp", None, "slab", None),
        P("grp", "slab", None, None, None),
        P("grp", "slab", None, None, None),
        P("grp", "slab", None),
        P("slab", None),
    )
    out_specs = (P("grp", "slab", None, None), P("grp", "slab", None, None, None))
    return jax.shard_map(local, mesh=mesh, in_specs=in_specs, out_specs=out_specs, check_vma=False)
```
